128 devices in a mesh: inst: 16 (over z, y_hi, core), tp: 8 (over x, y_lo).
Axes of the slice: x: 4, y: 4 (y_hi: 2, y_lo: 2; y = y_hi * 2 + y_lo), z: 4, core: 2. Of those that a mesh axis runs over, the one named last changes fastest.
Arguments:
- queries: bfloat16 [352, 2, 8192], P('inst', None, 'tp'), may hold values from -10 to 10
- hidden_in: bfloat16 [352, 2, 8192], P('inst', None, 'tp'), may hold values from -6 to 6
- kv_weight: bfloat16 [8192, 2, 1024], P(None, None, 'tp'), may hold values from -0.0625 to 0.0625
- kv_pool: bfloat16 [3328, 2, 128, 1024], P('inst', None, None, 'tp'), may hold values from -6 to 6
- page_table: int32 [16, 208], P('inst'), may hold values from 0 to 207, each once within a row
- long_lengths: int32 [16, 2], P('inst'), may hold values from 1 to 8192
- short_lengths: int32 [16, 20], P('inst'), may hold values from 1 to 510
- mig_order: int32 [16, 20], P('inst'), may hold values from 0 to 19, each once within a row
- destination: int32 [256, 1], P('inst'), may hold values from 0 to 15; in each aligned block of 16 rows (0 to 15, 16 to 31, ...) at most 2 rows name the same one
Outputs:
- stay_out: bfloat16 [352, 2, 8192], P('inst', None, 'tp')
- moved_out: bfloat16 [512, 2, 8192], P('inst', None, 'tp')
- moved_cache: bfloat16 [512, 2, 512, 1024], P('inst', None, None, 'tp')
- load_share: float32 [16], P('inst')
The draws below stay inside these ranges and needn't reach their ends.
Inputs may be any that keep to these rules, and one draw needn't show every extreme that they name: `page_table`: each row holds every page number of its instance once. `mig_order`: each row holds every short request id once. Among the 16 rows of one instance no destination appears more than 2 times.
All inputs are finite; a program needn't handle non-finite values.
Results may differ from the reference program's by a relative error of at most 0.0051.
Values may be sent and summed in bfloat16 or wider, within the bound.
No kernel may reach another device: no remote copies, remote signals or barrier semaphores. Data moves between devices by JAX's collectives and lax.ppermute only.
A program may use at most 128 MiB of HBM per device.

```python
import math
import jax
import jax.numpy as jnp
import numpy as np
from jax import lax

D = 8192
HEADS = 64
KV_HEADS = 8
HD = 128
PAGE = 128
MAXPG = 64
MIGPG = 4
LONG = 2
MIG = 16
CAP = 2
STEPS = 2
SHORT = 20
REQS = 22
INSTANCES = 16
MAXLEN = 8192
MIGLEN = 512
PAGES = 208
RECV = 32
QW = 8192
KV_WIDTH = 1024


def draw_kv_pool(key, part):
    key = jax.random.fold_in(key, 1)
    shape = (INSTANCES * PAGES, 2, PAGE, KV_WIDTH)
    result = jnp.clip(jax.random.normal(key, shape, jnp.float32), -6.0, 6.0)
    return result.astype(jnp.bfloat16)


def draw_queries(key, part):
    key = jax.random.fold_in(key, 2)
    shape = (INSTANCES * REQS, STEPS, QW)
    result = jnp.clip(jax.random.normal(key, shape, jnp.float32), -4.0, 4.0)
    return result.astype(jnp.bfloat16)


def ragged_lengths(key, count, largest):
    first_key, second_key = jax.random.split(key)
    base = jax.random.randint(first_key, (count,), 1, largest + 1)
    spot = jax.random.randint(second_key, (), 0, count)
    places = jnp.arange(count)
    base = jnp.where(places == spot, largest, base)
    base = jnp.where(places == (spot + 1) % count, 1, base)
    return base.astype(jnp.int32)


def draw_long_lengths(key, part):
    key = jax.random.fold_in(key, 3)
    return ragged_lengths(key, INSTANCES * LONG, MAXLEN).reshape(INSTANCES, LONG)


def draw_short_lengths(key, part):
    key = jax.random.fold_in(key, 4)
    return ragged_lengths(key, INSTANCES * SHORT, MIGLEN - 2).reshape(INSTANCES, SHORT)


def block_scale(own_key, extent, pieces, low, top_value):
    def one(axis_at, parts):
        steps = jax.random.uniform(jax.random.fold_in(jax.random.fold_in(own_key, 6), axis_at), (parts,), jnp.float32, low / len(pieces), top_value / len(pieces))
        return jnp.repeat(jnp.exp(steps), extent[axis_at] // parts).reshape((-1,) + (1,) * (len(extent) - axis_at - 1))

    loudness = one(*pieces[0])
    for cut in pieces[1:]:
        loudness = loudness * one(*cut)
    return loudness


def shared_out(key, own, number, rows, count, top, reach, lean):
    ranking = jax.random.permutation(key, count)
    packed, ordinary = load_shares(count, rows * top, reach, lean, True), load_shares(count, rows * top, reach, lean, False)
    places = jnp.arange(count)

    def named(tallies, offset_by):
        used = int((tallies > 0).sum())
        fixed = max(1, used // 4)
        passed = fixed + (places - fixed + offset_by * (used - fixed)) % max(1, count - fixed)
        return jnp.zeros((count,), jnp.int32).at[ranking[jnp.where(places < fixed, places, passed)]].set(jnp.asarray(tallies, jnp.int32))

    tallies = jnp.where(number % 4 == 0, named(packed, number // 4), named(ordinary, number - number // 4 - 1))
    mixed = jax.random.permutation(jax.random.fold_in(own, 3), count)
    donor, receiver = mixed[0:count // 2 * 2:2], mixed[1:count // 2 * 2:2]
    slack = jnp.minimum(tallies[donor] - 1, reach - tallies[receiver]) // 2
    slack = jnp.where((donor == ranking[0]) | (receiver == ranking[0]) | (tallies[receiver] == 0), 0, jnp.maximum(slack, 0))
    passed = jax.random.randint(jax.random.fold_in(own, 4), (count // 2,), 0, 1 << 20) % (slack + 1)
    tallies = tallies.at[donor].add(-passed).at[receiver].add(passed)
    items = jnp.searchsorted(jnp.cumsum(tallies), jnp.arange(rows * top), side="right").astype(jnp.int32)
    listing = items.reshape(top, rows).T
    listing = listing[jax.random.permutation(jax.random.fold_in(own, 1), rows)]
    offset_by = jax.random.randint(jax.random.fold_in(own, 2), (rows, 1), 0, top)
    return jnp.take_along_axis(listing, (jnp.arange(top)[None, :] + offset_by) % top, axis=1)


def load_shares(amount, total, bound, skew, full):
    weights = [(1 << 20) // math.isqrt(standing ** skew) + 1 for standing in range(1, amount + 1)]
    largest = bound if full else min(bound, max(-(-total // amount), total * weights[0] // sum(weights)))
    least = 1 if total - largest >= amount - 1 else 0
    counts, surplus = [largest] + [least] * (amount - 1), total - largest - least * (amount - 1)
    while surplus > 0:
        free = [i for i in range(1, amount) if counts[i] < largest] or [i for i in range(1, amount) if counts[i] < bound]
        mass, remaining = sum([weights[i] for i in free]), surplus
        for i in free:
            more = min(bound - counts[i], max(1, remaining * weights[i] // mass), surplus)
            counts[i] = counts[i] + more
            surplus = surplus - more
    return np.array(counts)


def gaussian(own_key, extent, deviation, most, cuts=(), kind=jnp.bfloat16):
    entries = deviation * jax.random.normal(own_key, extent, jnp.float32)
    if cuts:
        entries = entries * block_scale(own_key, extent, cuts, -0.22, 0.18)
    return jnp.clip(entries, -most, most).astype(kind)


def setup_inputs(seed: int = 0) -> dict:
    splits = jax.random.split(jax.random.key(seed), 10)
    queries = draw_queries(jax.random.fold_in(splits[9], 71), 0)
    hidden_in = gaussian(splits[1], (INSTANCES * REQS, STEPS, D), 1.0, 6.0, ((0, 16), (2, 8)))
    kv_weight = gaussian(splits[2], (D, 2, KV_WIDTH), D ** -0.5, 0.0625, ((2, 8),))
    kv_pool = draw_kv_pool(jax.random.fold_in(splits[9], 71), 0)
    page_table = jax.vmap(lambda own: jax.random.permutation(own, PAGES))(jax.random.split(splits[4], INSTANCES)).reshape((INSTANCES, PAGES)).astype(jnp.int32)
    long_lengths = draw_long_lengths(jax.random.fold_in(splits[9], 71), 0)
    short_lengths = draw_short_lengths(jax.random.fold_in(splits[9], 71), 0)
    mig_order = jax.vmap(lambda own: jax.random.permutation(own, SHORT))(jax.random.split(splits[7], INSTANCES)).reshape((INSTANCES, SHORT)).astype(jnp.int32)
    destination_keys = jax.random.split(jax.random.fold_in(splits[8], 1), (INSTANCES * MIG) // MIG)
    destination_turns = jax.random.permutation(jax.random.fold_in(splits[8], 3), (INSTANCES * MIG) // MIG)
    destination = jax.vmap(lambda own, number: shared_out(jax.random.fold_in(splits[8], 2), own, number, MIG, INSTANCES, 1, CAP, 1))(destination_keys, destination_turns).reshape((INSTANCES * MIG, 1))
    return dict(queries=queries, hidden_in=hidden_in, kv_weight=kv_weight, kv_pool=kv_pool, page_table=page_table, long_lengths=long_lengths, short_lengths=short_lengths, mig_order=mig_order, destination=destination)


def attend(query, cache_keys, cache_values, length, fresh_kv):
    step_count = query.shape[0]
    key_total = cache_keys.shape[0]
    head_count = cache_keys.shape[-1] // HD
    group_size = HEADS // KV_HEADS
    query_heads = query.astype(jnp.float32).reshape(step_count, head_count, group_size, HD)
    joined_keys = jnp.concatenate([cache_keys, fresh_kv[:, 0]], axis=0).astype(jnp.float32)
    joined_keys = joined_keys.reshape(key_total + step_count, head_count, HD)
    joined_values = jnp.concatenate([cache_values, fresh_kv[:, 1]], axis=0).astype(jnp.float32)
    joined_values = joined_values.reshape(key_total + step_count, head_count, HD)
    scores = jnp.einsum('tkgd,skd->tkgs', query_heads, joined_keys) / math.sqrt(HD)
    position = jnp.arange(key_total + step_count)
    step_index = jnp.arange(step_count)
    valid = jnp.where(position[None, :] < key_total, position[None, :] < length, position[None, :] - key_total <= step_index[:, None])
    scores = jnp.where(valid[:, None, None, :], scores, -1e+30)
    peak = lax.optimization_barrier(jnp.max(scores, axis=-1, keepdims=True))
    expd = jnp.exp(scores - peak)
    weights = (expd / lax.optimization_barrier(jnp.sum(expd, axis=-1, keepdims=True))).astype(jnp.bfloat16)
    blended = jnp.einsum('tkgs,skd->tkgd', weights.astype(jnp.float32), joined_values)
    return blended.reshape(step_count, head_count * group_size * HD).astype(jnp.bfloat16)

def finish(cache, length, fresh_kv):
    position = jnp.arange(cache.shape[1])
    retained = jnp.where((position < length)[None, :, None], cache, jnp.zeros_like(cache))
    for step_index in range(fresh_kv.shape[0]):
        retained = jnp.where((position == length + step_index)[None, :, None], fresh_kv[step_index][:, None, :], retained)
    return retained

def reference(queries, hidden_in, kv_weight, kv_pool, page_table, long_lengths, short_lengths, mig_order, destination):
    fresh_all = jnp.einsum('rtd,dck->rtck', hidden_in.astype(jnp.float32), kv_weight.astype(jnp.float32)).astype(jnp.bfloat16)
    fresh_all = fresh_all.reshape(INSTANCES, REQS, STEPS, 2, KV_WIDTH)
    query_all = queries.reshape(INSTANCES, REQS, STEPS, QW)
    pool_all = kv_pool.reshape(INSTANCES, PAGES, 2, PAGE, KV_WIDTH)

    def one_instance(inst_index):
        page_pool = pool_all[inst_index]
        page_list = page_table[inst_index]
        fresh_here = fresh_all[inst_index]
        query_here = query_all[inst_index]
        long_pages = page_pool[page_list[:LONG * MAXPG]].reshape(LONG, MAXPG, 2, PAGE, KV_WIDTH)
        long_keys = long_pages[:, :, 0].reshape(LONG, MAXLEN, KV_WIDTH)
        long_values = long_pages[:, :, 1].reshape(LONG, MAXLEN, KV_WIDTH)
        long_out = jax.vmap(attend)(query_here[:LONG], long_keys, long_values, long_lengths[inst_index], fresh_here[:LONG])
        short_pages = page_pool[page_list[LONG * MAXPG:]].reshape(SHORT, MIGPG, 2, PAGE, KV_WIDTH)
        short_keys = short_pages[:, :, 0].reshape(SHORT, MIGLEN, KV_WIDTH)
        short_values = short_pages[:, :, 1].reshape(SHORT, MIGLEN, KV_WIDTH)
        lengths = short_lengths[inst_index]
        short_all = jax.vmap(attend)(query_here[LONG:], short_keys, short_values, lengths, fresh_here[LONG:])
        leaving = mig_order[inst_index, :MIG]
        staying = jnp.ones((SHORT,), dtype=bool).at[leaving].set(False)
        short_kept = jnp.where(staying[:, None, None], short_all, jnp.zeros_like(short_all))
        leaving_cache = jnp.stack([short_keys[leaving], short_values[leaving]], axis=1)
        leaving_done = jax.vmap(finish)(leaving_cache, lengths[leaving], fresh_here[LONG:][leaving])
        resident = (jnp.sum(long_lengths[inst_index]) + jnp.sum(jnp.where(staying, lengths, 0)) + STEPS * (LONG + SHORT - MIG)).astype(jnp.int32)
        leaving_load = (lengths[leaving] + STEPS).astype(jnp.int32)
        return (jnp.concatenate([long_out, short_kept], axis=0), short_all[leaving], leaving_done, resident, leaving_load)
    stay_all, leaving_out, leaving_done, resident_all, leaving_load = lax.map(one_instance, jnp.arange(INSTANCES))
    targets = destination.reshape(INSTANCES, MIG)
    earlier = jnp.arange(MIG)[None, :] < jnp.arange(MIG)[:, None]
    slot_rank = lax.optimization_barrier(jnp.sum((targets[:, :, None] == targets[:, None, :]) & earlier[None], axis=2)).astype(jnp.int32)
    source = jnp.broadcast_to(jnp.arange(INSTANCES)[:, None], (INSTANCES, MIG)).astype(jnp.int32)
    moved_out = jnp.zeros((INSTANCES, INSTANCES, CAP, STEPS, QW), jnp.bfloat16).at[targets, source, slot_rank].set(leaving_out)
    moved_cache = jnp.zeros((INSTANCES, INSTANCES, CAP, 2, MIGLEN, KV_WIDTH), jnp.bfloat16).at[targets, source, slot_rank].set(leaving_done)
    loads = resident_all + jnp.zeros((INSTANCES,), jnp.int32).at[targets.reshape(-1)].add(leaving_load.reshape(-1))
    load_share = loads.astype(jnp.float32) * INSTANCES / jnp.sum(loads).astype(jnp.float32)
    return (stay_all.reshape(INSTANCES * REQS, STEPS, QW), moved_out.reshape(INSTANCES * RECV, STEPS, QW), moved_cache.reshape(INSTANCES * RECV, 2, MIGLEN, KV_WIDTH), load_share)
```

```python
import math

import jax
import jax.numpy as jnp
from jax import lax
from jax.experimental import pallas as pl
from jax.experimental.pallas import tpu as pltpu
from jax.sharding import PartitionSpec as P

HEADS = 64
KV_HEADS = 8
HD = 128
PAGE = 128
MAXPG = 64
MIGPG = 4
LONG = 2
MIG = 16
CAP = 2
STEPS = 2
SHORT = 20
REQS = 22
MIGLEN = 512
INST = 16
PAGES = 208
ROWS = 16
DUPS = 4
PIECE = MIGLEN // INST

A_DUP = MIGLEN
A_META = A_DUP + 2 * PIECE
A_ROWS = A_META + 16
B_SIDE = MIGLEN
B_ROWS = B_SIDE + 64

SMEM = pltpu.SMEM
VMEM = pltpu.VMEM


def spec(space):
    return pl.BlockSpec(memory_space=space)


def page_copy(pool, page, part, dst, sem):
    return pltpu.make_async_copy(pool.at[page, part], dst, sem)


def build_kernel(table, longs, shorts, order, dest, pool, out, count, meta, sems, dup_sems, meta_sems):
    for i in range(INST):
        count[i] = 0
    lane = lax.broadcasted_iota(jnp.int32, (16, 128), 1)

    def first_copy(k, p):
        page = table[0, LONG * MAXPG + order[0, k] * MIGPG + p]
        return page_copy(
            pool, page, 0, out.at[dest[0, k], pl.ds(p * PAGE, PAGE)], sems.at[k * MIGPG + p]
        )

    def dup_copy(k, m, c):
        page = table[0, LONG * MAXPG + order[0, k] * MIGPG + m // MIGPG]
        return pltpu.make_async_copy(
            pool.at[page, c, pl.ds(m % MIGPG * PIECE, PIECE)],
            out.at[m, pl.ds(A_DUP + c * PIECE, PIECE)],
            dup_sems.at[m * 2 + c],
        )

    def each(k, carry):
        row, dup_at, total = carry
        to = dest[0, k]
        slot = count[to]
        count[to] = slot + 1
        length = shorts[0, order[0, k]]

        @pl.when(slot == 0)
        def _():
            for p in range(MIGPG):
                first_copy(k, p).start()

        at = to * CAP + slot
        row = jnp.where(lane == at, length & 255, row)
        row = jnp.where(lane == at + 32, length >> 8, row)
        dup_at = jnp.where((slot == 1) & (dup_at < 0), k, dup_at)
        return row, dup_at, total

    row, dup_at, _ = lax.fori_loop(
        0, MIG, each, (jnp.zeros((16, 128), jnp.int32), jnp.int32(-1), jnp.int32(0))
    )

    @pl.when(dup_at >= 0)
    def _():
        for m in range(INST):
            for c in range(2):
                dup_copy(dup_at, m, c).start()

    total = jnp.int32(STEPS * REQS)
    for i in range(LONG):
        total = total + longs[0, i]
    for i in range(SHORT):
        total = total + shorts[0, i]
    row = jnp.where(lane == 64, total & 127, row)
    row = jnp.where(lane == 65, (total >> 7) & 127, row)
    row = jnp.where(lane == 66, total >> 14, row)
    meta[...] = row.astype(jnp.float32).astype(jnp.bfloat16)

    def meta_copy(m):
        return pltpu.make_async_copy(meta, out.at[m, pl.ds(A_META, 16)], meta_sems.at[m])

    for m in range(INST):
        meta_copy(m).start()
    for i in range(INST):
        count[i] = 0

    def finish(k, carry):
        to = dest[0, k]
        slot = count[to]
        count[to] = slot + 1

        @pl.when(slot == 0)
        def _():
            for p in range(MIGPG):
                first_copy(k, p).wait()

        return carry

    lax.fori_loop(0, MIG, finish, 0)

    @pl.when(dup_at >= 0)
    def _():
        for m in range(INST):
            for c in range(2):
                dup_copy(dup_at, m, c).wait()

    for m in range(INST):
        meta_copy(m).wait()


def build(tables, pool):
    return pl.pallas_call(
        build_kernel,
        out_shape=jax.ShapeDtypeStruct((INST, A_ROWS, 128), jnp.bfloat16),
        in_specs=[spec(SMEM)] * 5 + [spec(pl.ANY)],
        out_specs=spec(pl.ANY),
        scratch_shapes=[
            pltpu.SMEM((INST,), jnp.int32),
            pltpu.VMEM((16, 128), jnp.bfloat16),
            pltpu.SemaphoreType.DMA((MIG * MIGPG,)),
            pltpu.SemaphoreType.DMA((2 * INST,)),
            pltpu.SemaphoreType.DMA((INST,)),
        ],
        cost_estimate=pl.CostEstimate(flops=0, bytes_accessed=5 << 20, transcendentals=0),
        name="build_first",
    )(*tables, pool)


def second_kernel(table, order, dest, pool, out, count, sems):
    def copy(k, p, c):
        page = table[0, LONG * MAXPG + order[0, k] * MIGPG + p]
        return page_copy(
            pool,
            page,
            c,
            out.at[dest[0, k], pl.ds(c * MIGLEN + p * PAGE, PAGE)],
            sems.at[(k * MIGPG + p) * 2 + c],
        )

    for begin in (True, False):
        for i in range(INST):
            count[i] = 0

        def each(k, carry):
            to = dest[0, k]
            slot = count[to]
            count[to] = slot + 1

            @pl.when(slot == 1)
            def _():
                for p in range(MIGPG):
                    for c in range(2):
                        if begin:
                            copy(k, p, c).start()
                        else:
                            copy(k, p, c).wait()

            return carry

        lax.fori_loop(0, MIG, each, 0)


def build_second(table, order, dest, pool):
    return pl.pallas_call(
        second_kernel,
        out_shape=jax.ShapeDtypeStruct((INST, 2 * MIGLEN, 128), jnp.bfloat16),
        in_specs=[spec(SMEM)] * 3 + [spec(pl.ANY)],
        out_specs=spec(pl.ANY),
        scratch_shapes=[
            pltpu.SMEM((INST,), jnp.int32),
            pltpu.SemaphoreType.DMA((MIG * MIGPG * 2,)),
        ],
        name="build_second",
    )(table, order, dest, pool)


def dot_nt(a, b):
    return lax.dot_general(a, b, (((1,), (1,)), ((), ())), preferred_element_type=jnp.float32)


def dot_nn(a, b):
    return lax.dot_general(a, b, (((1,), (0,)), ((), ())), preferred_element_type=jnp.float32)


GROUP = 4
CHUNK = 1024
SCALE = 1.0 / math.sqrt(HD)


def attend_kernel(
    table, longs, shorts, order, dest, query, keys_values, values, pool, stay, out,
    count, place, cache, score, side, page_sems, move_sems, side_sem,
):
    def load(pg, sem):
        return pltpu.make_async_copy(pool.at[table[0, pg]], cache.at[:, pg], sem)

    def wait_pages(first, size, sem):
        pltpu.make_async_copy(
            cache.at[:, pl.ds(first, size)], cache.at[:, pl.ds(first, size)], sem
        ).wait()

    for r in range(SHORT // GROUP):
        def start_short(i, carry, r=r):
            load(LONG * MAXPG + r * GROUP * MIGPG + i, page_sems.at[r]).start()
            return carry

        lax.fori_loop(0, GROUP * MIGPG, start_short, 0)
    for j in range(LONG):
        def start_long(i, carry, j=j):
            load(j * MAXPG + i, page_sems.at[SHORT // GROUP + j]).start()
            return carry

        lax.fori_loop(0, MAXPG, start_long, 0)

    for i in range(INST):
        count[i] = 0
    for i in range(SHORT):
        place[i] = -1

    def move(k, p):
        page = table[0, LONG * MAXPG + order[0, k] * MIGPG + p]
        return page_copy(
            pool, page, 1, out.at[dest[0, k], pl.ds(p * PAGE, PAGE)], move_sems.at[k * MIGPG + p]
        )

    def settle(k, carry):
        to = dest[0, k]
        slot = count[to]
        count[to] = slot + 1
        place[order[0, k]] = to * CAP + slot

        @pl.when(slot == 0)
        def _():
            for p in range(MIGPG):
                move(k, p).start()

        return carry

    lax.fori_loop(0, MIG, settle, 0)

    def fresh_scores(q, r):
        s = dot_nt(q, keys_values[r]) * SCALE
        step = lax.broadcasted_iota(jnp.int32, s.shape, 0) // 8
        col = lax.broadcasted_iota(jnp.int32, s.shape, 1)
        return jnp.where((col <= step) & (col < STEPS), s, -1e30)

    def short_group(g, carry):
        first = pl.multiple_of(LONG * MAXPG + g * GROUP * MIGPG, GROUP * MIGPG)
        wait_pages(first, GROUP * MIGPG, page_sems.at[g])
        pos = lax.broadcasted_iota(jnp.int32, (ROWS, MIGLEN), 1)
        old, new = [], []
        for i in range(GROUP):
            r = g * GROUP + i
            q = query[LONG + r]
            k = cache[0, pl.ds(first + i * MIGPG, MIGPG)].reshape(MIGLEN, HD)
            s = dot_nt(q, k) * SCALE
            old.append(jnp.where(pos < shorts[0, r], s, -1e30))
            new.append(fresh_scores(q, LONG + r))
        old = jnp.concatenate(old, axis=0)
        new = jnp.concatenate(new, axis=0)
        peak = jnp.maximum(jnp.max(old, 1, keepdims=True), jnp.max(new, 1, keepdims=True))
        old = jnp.exp(old - peak)
        new = jnp.exp(new - peak)
        denominator = jnp.sum(old, 1, keepdims=True) + jnp.sum(new, 1, keepdims=True)
        old = (old / denominator).astype(jnp.bfloat16)
        new = (new / denominator).astype(jnp.bfloat16)
        for i in range(GROUP):
            r = g * GROUP + i
            v = cache[1, pl.ds(first + i * MIGPG, MIGPG)].reshape(MIGLEN, HD)
            o = dot_nn(old[i * ROWS:(i + 1) * ROWS], v)
            o = o + dot_nn(new[i * ROWS:(i + 1) * ROWS], values[LONG + r])
            o = o.astype(jnp.bfloat16)
            at = place[r]

            @pl.when(at < 0)
            def _():
                stay[LONG + r] = o

            @pl.when(at >= 0)
            def _():
                stay[LONG + r] = jnp.zeros_like(o)
                side[at, pl.ds(0, ROWS)] = o
                side[at, pl.ds(ROWS, 16)] = keys_values[LONG + r]

        return carry

    lax.fori_loop(0, SHORT // GROUP, short_group, 0)
    side_copies = [
        pltpu.make_async_copy(
            side.at[i], out.at[i // CAP, pl.ds(B_SIDE + i % CAP * 32, 32)], side_sem.at[i]
        )
        for i in range(INST * CAP)
    ]
    for c in side_copies:
        c.start()

    for j in range(LONG):
        wait_pages(j * MAXPG, MAXPG, page_sems.at[SHORT // GROUP + j])
        q = query[j]
        new = fresh_scores(q, j)
        top = jnp.max(new, 1, keepdims=True)
        length = longs[0, j]
        steps = MAXPG * PAGE // CHUNK
        per = CHUNK // PAGE
        for i in range(steps):
            k = cache[0, pl.ds(j * MAXPG + i * per, per)].reshape(CHUNK, HD)
            s = dot_nt(q, k) * SCALE
            pos = lax.broadcasted_iota(jnp.int32, s.shape, 1) + i * CHUNK
            s = jnp.where(pos < length, s, -1e30)
            score[j, i] = s
            top = jnp.maximum(top, jnp.max(s, 1, keepdims=True))
        new = jnp.exp(new - top)
        denominator = jnp.sum(new, 1, keepdims=True)
        for i in range(steps):
            e = jnp.exp(score[j, i] - top)
            score[j, i] = e
            denominator = denominator + jnp.sum(e, 1, keepdims=True)
        inverse = 1.0 / denominator
        o = dot_nn((new * inverse).astype(jnp.bfloat16), values[j])
        for i in range(steps):
            v = cache[1, pl.ds(j * MAXPG + i * per, per)].reshape(CHUNK, HD)
            o = o + dot_nn((score[j, i] * inverse).astype(jnp.bfloat16), v)
        stay[j] = o.astype(jnp.bfloat16)

    for i in range(INST):
        count[i] = 0

    def finish(k, carry):
        to = dest[0, k]
        slot = count[to]
        count[to] = slot + 1

        @pl.when(slot == 0)
        def _():
            for p in range(MIGPG):
                move(k, p).wait()

        return carry

    lax.fori_loop(0, MIG, finish, 0)
    for c in side_copies:
        c.wait()


def attend(tables, query, keys_values, values, pool):
    return pl.pallas_call(
        attend_kernel,
        out_shape=(
            jax.ShapeDtypeStruct((REQS, ROWS, HD), jnp.bfloat16),
            jax.ShapeDtypeStruct((INST, B_ROWS, HD), jnp.bfloat16),
        ),
        in_specs=[spec(SMEM)] * 5 + [spec(VMEM)] * 3 + [spec(pl.ANY)],
        out_specs=(spec(VMEM), spec(pl.ANY)),
        scratch_shapes=[
            pltpu.SMEM((INST,), jnp.int32),
            pltpu.SMEM((SHORT,), jnp.int32),
            pltpu.VMEM((2, PAGES, PAGE, HD), jnp.bfloat16),
            pltpu.VMEM((LONG, MAXPG * PAGE // CHUNK, ROWS, CHUNK), jnp.float32),
            pltpu.VMEM((INST * CAP, 32, HD), jnp.bfloat16),
            pltpu.SemaphoreType.DMA((SHORT // GROUP + LONG,)),
            pltpu.SemaphoreType.DMA((MIG * MIGPG,)),
            pltpu.SemaphoreType.DMA((INST * CAP,)),
        ],
        compiler_params=pltpu.CompilerParams(vmem_limit_bytes=24 << 20),
        cost_estimate=pl.CostEstimate(
            flops=4 * 26624 * 16 * 128, bytes_accessed=17 << 20, transcendentals=26624 * 16
        ),
        name="attend_all",
    )(*tables, query, keys_values, values, pool)


def join_kernel(here, *refs):
    pieces, out = refs[:-1], refs[-1]
    me = here[0]
    width = pieces[0].shape[1]
    for k, piece in enumerate(pieces):
        at = pl.multiple_of(((me + 8 - k) % 8) * width, width)
        out[:, pl.ds(at, width)] = piece[...]


def join(here, pieces):
    rows, width = pieces[0].shape
    return pl.pallas_call(
        join_kernel,
        out_shape=jax.ShapeDtypeStruct((rows, width * len(pieces)), jnp.bfloat16),
        in_specs=[spec(SMEM)] + [spec(VMEM)] * len(pieces),
        out_specs=spec(VMEM),
        name="join_hidden",
    )(here, *pieces)


def pick_kernel(source, block, out):
    out[...] = block[...]


def pick(source, received):
    return pl.pallas_call(
        pick_kernel,
        out_shape=jax.ShapeDtypeStruct((DUPS, 2 * PIECE, HD), jnp.bfloat16),
        grid_spec=pltpu.PrefetchScalarGridSpec(
            num_scalar_prefetch=1,
            grid=(DUPS,),
            in_specs=[
                pl.BlockSpec(
                    (1, 2 * PIECE, HD), lambda j, source: (source[j], A_DUP // (2 * PIECE), 0)
                )
            ],
            out_specs=pl.BlockSpec((1, 2 * PIECE, HD), lambda j, source: (j, 0, 0)),
        ),
        name="pick_pieces",
    )(source, received)


def place_kernel(full, lens, rank, here, first, second, dup, cache, out):
    s = pl.program_id(0)
    pos = lax.broadcasted_iota(jnp.int32, (PAGE, HD), 0)
    for slot in range(CAP):
        length = lens[s * CAP + slot]
        filled = length > 0
        if slot == 0:
            sources = [
                lambda p: first[0, pl.ds(p * PAGE, PAGE)],
                lambda p: second[0, pl.ds(p * PAGE, PAGE)],
            ]
        elif full:
            sources = [
                lambda p: dup[0, pl.ds(p * PAGE, PAGE)],
                lambda p: dup[0, pl.ds(MIGLEN + p * PAGE, PAGE)],
            ]
        else:
            me = here[0]
            j = rank[s]

            def piece(p, c):
                parts = []
                for q in range(MIGPG):
                    x = me ^ (p * MIGPG + q)
                    e = ((x >> 2) & 3) | (((x >> 1) & 1) << 2) | ((x & 1) << 3)
                    parts.append(dup[e, j, pl.ds(c * PIECE, PIECE)])
                return jnp.concatenate(parts, axis=0)

            sources = [lambda p: piece(p, 0), lambda p: piece(p, 1)]
        for p in range(MIGPG):
            whole = filled & (length >= (p + 1) * PAGE)
            empty = jnp.logical_not(filled) | (length + STEPS <= p * PAGE)

            @pl.when(whole)
            def _():
                for c in range(2):
                    cache[slot, c, pl.ds(p * PAGE, PAGE)] = sources[c](p)

            @pl.when(empty)
            def _():
                for c in range(2):
                    cache[slot, c, pl.ds(p * PAGE, PAGE)] = jnp.zeros((PAGE, HD), jnp.bfloat16)

            @pl.when(jnp.logical_not(whole | empty))
            def _():
                fresh = second[0, pl.ds(B_SIDE + slot * 32 + ROWS, 16)].astype(jnp.float32)
                at = pos + p * PAGE
                for c in range(2):
                    x = sources[c](p).astype(jnp.float32)
                    x = jnp.where(at < length, x, 0.0)
                    for t in range(STEPS):
                        x = jnp.where(at == length + t, fresh[c * 2 + t:c * 2 + t + 1], x)
                    cache[slot, c, pl.ds(p * PAGE, PAGE)] = x.astype(jnp.bfloat16)

        @pl.when(filled)
        def _():
            out[slot] = second[0, pl.ds(B_SIDE + slot * 32, ROWS)]

        @pl.when(jnp.logical_not(filled))
        def _():
            out[slot] = jnp.zeros((ROWS, HD), jnp.bfloat16)


def place_all(full, lens, rank, here, first, second, dup):
    def kernel(*refs):
        place_kernel(full, *refs)

    if full:
        dup_spec = pl.BlockSpec((1, 2 * MIGLEN, HD), lambda s, *_: (s, 0, 0))
    else:
        dup_spec = pl.BlockSpec(dup.shape, lambda s, *_: (0, 0, 0, 0))
    return pl.pallas_call(
        kernel,
        out_shape=(
            jax.ShapeDtypeStruct((INST * CAP, 2, MIGLEN, HD), jnp.bfloat16),
            jax.ShapeDtypeStruct((INST * CAP, ROWS, HD), jnp.bfloat16),
        ),
        grid_spec=pltpu.PrefetchScalarGridSpec(
            num_scalar_prefetch=3,
            grid=(INST,),
            in_specs=[
                pl.BlockSpec((1, MIGLEN, HD), lambda s, *_: (s, 0, 0)),
                pl.BlockSpec((1, B_ROWS, HD), lambda s, *_: (s, 0, 0)),
                dup_spec,
            ],
            out_specs=[
                pl.BlockSpec((CAP, 2, MIGLEN, HD), lambda s, *_: (s, 0, 0, 0)),
                pl.BlockSpec((CAP, ROWS, HD), lambda s, *_: (s, 0, 0)),
            ],
        ),
        compiler_params=pltpu.CompilerParams(vmem_limit_bytes=16 << 20),
        name="place_full" if full else "place_short",
    )(lens, rank, here, first, second, dup)


def swap(value, axis, bit):
    count = lax.axis_size(axis)
    return lax.ppermute(value, axis, [(i, i ^ bit) for i in range(count)])


def on_device(
    queries,
    hidden_in,
    kv_weight,
    kv_pool,
    page_table,
    long_lengths,
    short_lengths,
    mig_order,
    destination,
):
    inst_index = lax.axis_index("inst")
    tp_index = lax.axis_index("tp")
    targets = destination.reshape(1, MIG)
    tables = (page_table, long_lengths, short_lengths, mig_order, targets)

    first = build(tables, kv_pool)
    got_first = lax.all_to_all(first, "inst", split_axis=0, concat_axis=0, tiled=True)

    hidden = hidden_in.reshape(REQS * STEPS, -1)
    pieces = [hidden]
    for k in range(1, 8):
        pieces.append(lax.ppermute(hidden, "tp", [(i, (i + k) % 8) for i in range(8)]))
    hidden_all = join(tp_index.reshape(1), pieces)
    fresh = jnp.einsum(
        "rd,dcn->rcn", hidden_all, kv_weight, preferred_element_type=jnp.float32
    ).astype(jnp.bfloat16)
    fresh = fresh.reshape(REQS, STEPS, 2, HD)
    values = jnp.pad(fresh[:, :, 1], ((0, 0), (0, 16 - STEPS), (0, 0)))
    keys_values = jnp.pad(
        fresh.transpose(0, 2, 1, 3).reshape(REQS, 2 * STEPS, HD),
        ((0, 0), (0, 16 - 2 * STEPS), (0, 0)),
    )
    stay, second = attend(
        tables, queries.reshape(REQS, ROWS, HD), keys_values, values, kv_pool
    )
    stay_out = stay.reshape(REQS, STEPS, KV_HEADS * HD)
    got_second = lax.all_to_all(second, "inst", split_axis=0, concat_axis=0, tiled=True)

    meta = got_first[:, A_META].astype(jnp.float32).astype(jnp.int32)
    lengths = (meta[:, :32] + 256 * meta[:, 32:64]).reshape(INST, INST, CAP)
    all_load = jnp.sum(meta[:, 64] + 128 * meta[:, 65] + 16384 * meta[:, 66])
    doubled = jnp.sum((lengths[:, :, 1] > 0).astype(jnp.int32), axis=1)
    index = jnp.arange(INST)
    rank = jnp.sum(jnp.where(index[None, :] < index[:, None], doubled[None, :], 0), axis=1)
    overflow = (jnp.sum(doubled) > DUPS) | (jnp.max(doubled) > 1)
    rank = jnp.minimum(rank, DUPS - 1)
    source = jnp.sum(
        jnp.where(
            (rank[None, :] == jnp.arange(DUPS)[:, None]) & (doubled[None, :] > 0), index[None, :], 0
        ),
        axis=1,
    )
    source = jnp.minimum(source, INST - 1)
    arriving = jnp.sum(
        jnp.where(index[None, :, None] == inst_index, lengths, 0), axis=1
    ).reshape(INST * CAP)
    staying = jnp.any(
        mig_order[0, MIG:][:, None] == jnp.arange(SHORT)[None, :], axis=0
    )
    resident = (
        jnp.sum(long_lengths)
        + jnp.sum(jnp.where(staying, short_lengths[0], 0))
        + STEPS * (LONG + SHORT - MIG)
    )
    own_load = resident + jnp.sum(jnp.where(arriving > 0, arriving + STEPS, 0))
    load_share = (own_load.astype(jnp.float32) * INST / all_load.astype(jnp.float32)).reshape(1)

    dup = pick(source, got_first)[None]
    for bit in (4, 8, 2, 1):
        dup = jnp.concatenate([dup, swap(dup, "inst", bit)], axis=0)

    here = inst_index.reshape(1)

    def short_path(args):
        lens, rank, first, second, dup = args
        return tuple(place_all(False, lens, rank, here, first, second, dup))

    def long_path(args):
        lens, rank, first, second, _ = args
        send = build_second(page_table, mig_order, targets, kv_pool)
        got = lax.all_to_all(send, "inst", split_axis=0, concat_axis=0, tiled=True)
        return tuple(place_all(True, lens, rank, here, first, second, got))

    moved_cache, moved = lax.cond(
        overflow, long_path, short_path, (arriving, rank, got_first, got_second, dup)
    )
    moved_out = moved.reshape(INST * CAP, STEPS, KV_HEADS * HD)
    return (stay_out, moved_out, moved_cache, load_share)


def solution(mesh):
    placed = (
        P("inst", None, "tp"),
        P("inst", None, "tp"),
        P(None, None, "tp"),
        P("inst", None, None, "tp"),
        P("inst", None),
        P("inst", None),
        P("inst", None),
        P("inst", None),
        P("inst", None),
    )
    return jax.shard_map(
        on_device,
        mesh=mesh,
        in_specs=placed,
        out_specs=(
            P("inst", None, "tp"),
            P("inst", None, "tp"),
            P("inst", None, None, "tp"),
            P("inst"),
        ),
        check_vma=False,
    )
```

```python
import math

import jax
import jax.numpy as jnp
from jax import lax
from jax.experimental import pallas as pl
from jax.experimental.pallas import tpu as pltpu
from jax.sharding import PartitionSpec as P

HEADS = 64
KV_HEADS = 8
HD = 128
PAGE = 128
MAXPG = 64
MIGPG = 4
LONG = 2
MIG = 16
CAP = 2
STEPS = 2
SHORT = 20
REQS = 22
MIGLEN = 512
INST = 16
PAGES = 208
ROWS = 16
DUPS = 4
PIECE = MIGLEN // INST

A_DUP = 2 * MIGLEN
A_META = A_DUP + 2 * PIECE
A_ROWS = A_META + 16
B_DUP = 64
B_ROWS = B_DUP + DUPS * 2 * PIECE

SMEM = pltpu.SMEM
VMEM = pltpu.VMEM


def spec(space):
    return pl.BlockSpec(memory_space=space)


def clear(count):
    for i in range(INST):
        count[i] = 0


def take_slot(count, to):
    slot = count[to]
    count[to] = slot + 1
    return slot


def build_kernel(
    table, longs, shorts, order, dest, pool, out, count, held, extra, stage, sems, extra_sems, out_sems, stage_sem
):
    def load(k, p):
        page = table[0, LONG * MAXPG + order[0, k] * MIGPG + p]
        return pltpu.make_async_copy(
            pool.at[page], held.at[dest[0, k], pl.ds(p * 2 * PAGE, 2 * PAGE)], sems.at[k * MIGPG + p]
        )

    def load_extra(k, p):
        page = table[0, LONG * MAXPG + order[0, k] * MIGPG + p]
        return pltpu.make_async_copy(pool.at[page], extra.at[p], extra_sems.at[p])

    def send(k):
        to = dest[0, k]
        return pltpu.make_async_copy(
            held.at[to], out.at[to, pl.ds(0, 2 * MIGLEN)], out_sems.at[k]
        )

    clear(count)

    def begin(k, dup_at):
        slot = take_slot(count, dest[0, k])

        @pl.when(slot == 0)
        def _():
            for p in range(MIGPG):
                load(k, p).start()

        first = (slot == 1) & (dup_at < 0)

        @pl.when(first)
        def _():
            for p in range(MIGPG):
                load_extra(k, p).start()

        return jnp.where(first, k, dup_at)

    dup_at = lax.fori_loop(0, MIG, begin, jnp.int32(-1))
    clear(count)
    lane = lax.broadcasted_iota(jnp.int32, (16, 128), 1)

    def each(k, row):
        to = dest[0, k]
        slot = take_slot(count, to)
        length = shorts[0, order[0, k]]

        @pl.when(slot == 0)
        def _():
            for p in range(MIGPG):
                load(k, p).wait()
            send(k).start()

        at = to * CAP + slot
        row = jnp.where(lane == at, length & 255, row)
        return jnp.where(lane == at + 32, length >> 8, row)

    row = lax.fori_loop(0, MIG, each, jnp.zeros((16, 128), jnp.int32))
    total = jnp.int32(STEPS * REQS)
    for i in range(LONG):
        total = total + longs[0, i]
    for i in range(SHORT):
        total = total + shorts[0, i]
    row = jnp.where(lane == 64, total & 127, row)
    row = jnp.where(lane == 65, (total >> 7) & 127, row)
    row = jnp.where(lane == 66, total >> 14, row)
    dup_to = jnp.where(dup_at >= 0, dest[0, jnp.maximum(dup_at, 0)] + 1, 0)
    row = jnp.where(lane == 67, dup_to, row)
    tables = row.astype(jnp.float32).astype(jnp.bfloat16)

    @pl.when(dup_at >= 0)
    def _():
        for p in range(MIGPG):
            load_extra(dup_at, p).wait()
        for m in range(INST):
            for c in range(2):
                stage[m, pl.ds(c * PIECE, PIECE)] = extra[
                    m // MIGPG, pl.ds(c * PAGE + m % MIGPG * PIECE, PIECE)
                ]

    for m in range(INST):
        stage[m, pl.ds(2 * PIECE, 16)] = tables
    last = pltpu.make_async_copy(stage, out.at[:, pl.ds(A_DUP, A_ROWS - A_DUP)], stage_sem)
    last.start()
    clear(count)

    def finish(k, carry):
        slot = take_slot(count, dest[0, k])

        @pl.when(slot == 0)
        def _():
            send(k).wait()

        return carry

    lax.fori_loop(0, MIG, finish, 0)
    last.wait()


def build(tables, pool):
    return pl.pallas_call(
        build_kernel,
        out_shape=jax.ShapeDtypeStruct((INST, A_ROWS, HD), jnp.bfloat16),
        in_specs=[spec(SMEM)] * 5 + [spec(pl.ANY)],
        out_specs=spec(pltpu.HBM),
        scratch_shapes=[
            pltpu.SMEM((INST,), jnp.int32),
            pltpu.VMEM((INST, 2 * MIGLEN, HD), jnp.bfloat16),
            pltpu.VMEM((MIGPG, 2 * PAGE, HD), jnp.bfloat16),
            pltpu.VMEM((INST, A_ROWS - A_DUP, HD), jnp.bfloat16),
            pltpu.SemaphoreType.DMA((MIG * MIGPG,)),
            pltpu.SemaphoreType.DMA((MIGPG,)),
            pltpu.SemaphoreType.DMA((MIG,)),
            pltpu.SemaphoreType.DMA(()),
        ],
        compiler_params=pltpu.CompilerParams(vmem_limit_bytes=60 << 20),
        cost_estimate=pl.CostEstimate(flops=0, bytes_accessed=9 << 20, transcendentals=0),
        name="build_first",
    )(*tables, pool)


def second_kernel(table, order, dest, pool, out, count, held, sems, out_sems):
    def load(k, p):
        page = table[0, LONG * MAXPG + order[0, k] * MIGPG + p]
        return pltpu.make_async_copy(
            pool.at[page], held.at[dest[0, k], pl.ds(p * 2 * PAGE, 2 * PAGE)], sems.at[k * MIGPG + p]
        )

    def send(k):
        to = dest[0, k]
        return pltpu.make_async_copy(held.at[to], out.at[to], out_sems.at[k])

    for stage in range(3):
        clear(count)

        def each(k, carry):
            slot = take_slot(count, dest[0, k])

            @pl.when(slot == 1)
            def _():
                if stage == 0:
                    for p in range(MIGPG):
                        load(k, p).start()
                elif stage == 1:
                    for p in range(MIGPG):
                        load(k, p).wait()
                    send(k).start()
                else:
                    send(k).wait()

            return carry

        lax.fori_loop(0, MIG, each, 0)


def build_second(table, order, dest, pool):
    return pl.pallas_call(
        second_kernel,
        out_shape=jax.ShapeDtypeStruct((INST, 2 * MIGLEN, HD), jnp.bfloat16),
        in_specs=[spec(SMEM)] * 3 + [spec(pl.ANY)],
        out_specs=spec(pl.ANY),
        scratch_shapes=[
            pltpu.SMEM((INST,), jnp.int32),
            pltpu.VMEM((INST, 2 * MIGLEN, HD), jnp.bfloat16),
            pltpu.SemaphoreType.DMA((MIG * MIGPG,)),
            pltpu.SemaphoreType.DMA((MIG,)),
        ],
        compiler_params=pltpu.CompilerParams(vmem_limit_bytes=12 << 20),
        name="build_second",
    )(table, order, dest, pool)


def dot_nt(a, b):
    return lax.dot_general(a, b, (((1,), (1,)), ((), ())), preferred_element_type=jnp.float32)


def dot_nn(a, b):
    return lax.dot_general(a, b, (((1,), (0,)), ((), ())), preferred_element_type=jnp.float32)


GROUP = 4
CHUNK = 1024
SCALE = 1.0 / math.sqrt(HD)


def attend_kernel(
    table, longs, shorts, order, dest, query, keys_values, values, pool, stay, side,
    count, place, cache, score, page_sems,
):
    def load(pg, sem):
        return pltpu.make_async_copy(pool.at[table[0, pg]], cache.at[:, pg], sem)

    def wait_pages(first, size, sem):
        pltpu.make_async_copy(
            cache.at[:, pl.ds(first, size)], cache.at[:, pl.ds(first, size)], sem
        ).wait()

    for r in range(SHORT // GROUP):
        def start_short(i, carry, r=r):
            load(LONG * MAXPG + r * GROUP * MIGPG + i, page_sems.at[r]).start()
            return carry

        lax.fori_loop(0, GROUP * MIGPG, start_short, 0)
    for j in range(LONG):
        def start_long(i, carry, j=j):
            load(j * MAXPG + i, page_sems.at[SHORT // GROUP + j]).start()
            return carry

        lax.fori_loop(0, MAXPG, start_long, 0)

    clear(count)
    for i in range(SHORT):
        place[i] = -1

    def settle(k, carry):
        to = dest[0, k]
        place[order[0, k]] = to * CAP + take_slot(count, to)
        return carry

    lax.fori_loop(0, MIG, settle, 0)

    def fresh_scores(q, r):
        s = dot_nt(q, keys_values[r]) * SCALE
        step = lax.broadcasted_iota(jnp.int32, s.shape, 0) // 8
        col = lax.broadcasted_iota(jnp.int32, s.shape, 1)
        return jnp.where((col <= step) & (col < STEPS), s, -1e30)

    def short_group(g, carry):
        first = pl.multiple_of(LONG * MAXPG + g * GROUP * MIGPG, GROUP * MIGPG)
        wait_pages(first, GROUP * MIGPG, page_sems.at[g])
        pos = lax.broadcasted_iota(jnp.int32, (ROWS, MIGLEN), 1)
        old, new = [], []
        for i in range(GROUP):
            r = g * GROUP + i
            q = query[LONG + r]
            k = cache[0, pl.ds(first + i * MIGPG, MIGPG)].reshape(MIGLEN, HD)
            s = dot_nt(q, k) * SCALE
            old.append(jnp.where(pos < shorts[0, r], s, -1e30))
            new.append(fresh_scores(q, LONG + r))
        old = jnp.concatenate(old, axis=0)
        new = jnp.concatenate(new, axis=0)
        peak = jnp.maximum(jnp.max(old, 1, keepdims=True), jnp.max(new, 1, keepdims=True))
        old = jnp.exp(old - peak)
        new = jnp.exp(new - peak)
        denominator = jnp.sum(old, 1, keepdims=True) + jnp.sum(new, 1, keepdims=True)
        old = (old / denominator).astype(jnp.bfloat16)
        new = (new / denominator).astype(jnp.bfloat16)
        for i in range(GROUP):
            r = g * GROUP + i
            v = cache[1, pl.ds(first + i * MIGPG, MIGPG)].reshape(MIGLEN, HD)
            o = dot_nn(old[i * ROWS:(i + 1) * ROWS], v)
            o = o + dot_nn(new[i * ROWS:(i + 1) * ROWS], values[LONG + r])
            o = o.astype(jnp.bfloat16)
            at = place[r]

            @pl.when(at < 0)
            def _():
                stay[LONG + r] = o

            @pl.when(at >= 0)
            def _():
                stay[LONG + r] = jnp.zeros_like(o)
                side[at, pl.ds(0, ROWS)] = o
                side[at, pl.ds(ROWS, 16)] = keys_values[LONG + r]

        return carry

    lax.fori_loop(0, SHORT // GROUP, short_group, 0)

    for j in range(LONG):
        wait_pages(j * MAXPG, MAXPG, page_sems.at[SHORT // GROUP + j])
        q = query[j]
        new = fresh_scores(q, j)
        top = jnp.max(new, 1, keepdims=True)
        length = longs[0, j]
        steps = MAXPG * PAGE // CHUNK
        per = CHUNK // PAGE
        for i in range(steps):
            k = cache[0, pl.ds(j * MAXPG + i * per, per)].reshape(CHUNK, HD)
            s = dot_nt(q, k) * SCALE
            pos = lax.broadcasted_iota(jnp.int32, s.shape, 1) + i * CHUNK
            s = jnp.where(pos < length, s, -1e30)
            score[j, i] = s
            top = jnp.maximum(top, jnp.max(s, 1, keepdims=True))
        new = jnp.exp(new - top)
        denominator = jnp.sum(new, 1, keepdims=True)
        for i in range(steps):
            e = jnp.exp(score[j, i] - top)
            score[j, i] = e
            denominator = denominator + jnp.sum(e, 1, keepdims=True)
        inverse = 1.0 / denominator
        o = dot_nn((new * inverse).astype(jnp.bfloat16), values[j])
        for i in range(steps):
            v = cache[1, pl.ds(j * MAXPG + i * per, per)].reshape(CHUNK, HD)
            o = o + dot_nn((score[j, i] * inverse).astype(jnp.bfloat16), v)
        stay[j] = o.astype(jnp.bfloat16)


def attend(tables, query, keys_values, values, pool):
    return pl.pallas_call(
        attend_kernel,
        out_shape=(
            jax.ShapeDtypeStruct((REQS, ROWS, HD), jnp.bfloat16),
            jax.ShapeDtypeStruct((INST * CAP, 32, HD), jnp.bfloat16),
        ),
        in_specs=[spec(SMEM)] * 5 + [spec(VMEM)] * 3 + [spec(pl.ANY)],
        out_specs=(spec(VMEM), spec(VMEM)),
        scratch_shapes=[
            pltpu.SMEM((INST,), jnp.int32),
            pltpu.SMEM((SHORT,), jnp.int32),
            pltpu.VMEM((2, PAGES, PAGE, HD), jnp.bfloat16),
            pltpu.VMEM((LONG, MAXPG * PAGE // CHUNK, ROWS, CHUNK), jnp.float32),
            pltpu.SemaphoreType.DMA((SHORT // GROUP + LONG,)),
        ],
        compiler_params=pltpu.CompilerParams(vmem_limit_bytes=24 << 20),
        cost_estimate=pl.CostEstimate(
            flops=4 * 26624 * 16 * 128, bytes_accessed=14 << 20, transcendentals=26624 * 16
        ),
        name="attend_all",
    )(*tables, query, keys_values, values, pool)


def join_kernel(here, own, mate, out):
    me = here[0]
    width = own.shape[2]
    for k in range(4):
        for other in range(2):
            x = (me // 2 + 4 - k) % 4
            y = (me + other) % 2
            at = pl.multiple_of((x * 2 + y) * width, width)
            out[:, pl.ds(at, width)] = (mate if other else own)[k]


def join(here, own, mate):
    _, rows, width = own.shape
    return pl.pallas_call(
        join_kernel,
        out_shape=jax.ShapeDtypeStruct((rows, width * 8), jnp.bfloat16),
        in_specs=[spec(SMEM), spec(VMEM), spec(VMEM)],
        out_specs=spec(VMEM),
        name="join_hidden",
    )(here, own, mate)


def route_kernel(received, side, out, small, count, sem):
    copy = pltpu.make_async_copy(received.at[:, pl.ds(A_DUP, A_ROWS - A_DUP)], small, sem)
    copy.start()
    clear(count)
    for d in range(INST):
        for c in range(CAP):
            out[d, pl.ds(c * 32, 32)] = side[d * CAP + c]
    copy.wait()
    lane = lax.broadcasted_iota(jnp.int32, (16, 128), 1)
    targets = []
    for s in range(INST):
        tables = small[s, pl.ds(2 * PIECE, 16)].astype(jnp.float32)
        targets.append(jnp.max(jnp.where(lane == 67, tables, 0.0)).astype(jnp.int32) - 1)
    for s in range(INST):
        to = targets[s]
        at = jnp.maximum(to, 0)

        @pl.when((to >= 0) & (count[at] < DUPS))
        def _():
            slot = take_slot(count, at)
            row = pl.multiple_of(B_DUP + slot * 2 * PIECE, 2 * PIECE)
            out[at, pl.ds(row, 2 * PIECE)] = small[s, pl.ds(0, 2 * PIECE)]


def route(received, side):
    return pl.pallas_call(
        route_kernel,
        out_shape=jax.ShapeDtypeStruct((INST, B_ROWS, HD), jnp.bfloat16),
        in_specs=[spec(pl.ANY), spec(VMEM)],
        out_specs=spec(VMEM),
        scratch_shapes=[
            pltpu.VMEM((INST, A_ROWS - A_DUP, HD), jnp.bfloat16),
            pltpu.SMEM((INST,), jnp.int32),
            pltpu.SemaphoreType.DMA(()),
        ],
        cost_estimate=pl.CostEstimate(flops=0, bytes_accessed=2 << 20, transcendentals=0),
        name="route_pieces",
    )(received, side)


def window_base(length):
    return pl.multiple_of(jnp.minimum(length // 16 * 16, MIGLEN - 32), 16)


def masked_page(read, write, length, fresh, p):
    grown = length + STEPS if fresh is not None else length
    whole = length >= (p + 1) * PAGE
    empty = grown <= p * PAGE

    @pl.when(whole)
    def _():
        for c in range(2):
            write(p, c, read(p, c))

    @pl.when(empty)
    def _():
        for c in range(2):
            write(p, c, jnp.zeros((PAGE, HD), jnp.bfloat16))

    @pl.when(jnp.logical_not(whole | empty))
    def _():
        at = lax.broadcasted_iota(jnp.int32, (PAGE, HD), 0) + p * PAGE
        for c in range(2):
            x = jnp.where(at < length, read(p, c).astype(jnp.float32), 0.0)
            if fresh is not None:
                rows = fresh().astype(jnp.float32)
                for t in range(STEPS):
                    x = jnp.where(at == length + t, rows[c * 2 + t:c * 2 + t + 1], x)
            write(p, c, x.astype(jnp.bfloat16))


def place_kernel(lens, block, cache, window):
    s = pl.program_id(0)
    length = lens[s * CAP]

    def read(p, c):
        return block[0, pl.ds((p * 2 + c) * PAGE, PAGE)]

    def write(p, c, x):
        cache[0, c, pl.ds(p * PAGE, PAGE)] = x

    for p in range(MIGPG):
        masked_page(read, write, length, None, p)
    cache[1] = jnp.zeros((2, MIGLEN, HD), jnp.bfloat16)
    base = window_base(length)
    for c in range(2):
        window[0, c] = cache[0, c, pl.ds(base, 32)]


def place_first(lens, received):
    return pl.pallas_call(
        place_kernel,
        out_shape=(
            jax.ShapeDtypeStruct((INST * CAP, 2, MIGLEN, HD), jnp.bfloat16),
            jax.ShapeDtypeStruct((INST, 2, 32, HD), jnp.bfloat16),
        ),
        grid_spec=pltpu.PrefetchScalarGridSpec(
            num_scalar_prefetch=1,
            grid=(INST,),
            in_specs=[pl.BlockSpec((1, 2 * MIGLEN, HD), lambda s, _: (s, 0, 0))],
            out_specs=[
                pl.BlockSpec((CAP, 2, MIGLEN, HD), lambda s, _: (s, 0, 0, 0)),
                pl.BlockSpec((1, 2, 32, HD), lambda s, _: (s, 0, 0, 0)),
            ],
        ),
        compiler_params=pltpu.CompilerParams(vmem_limit_bytes=8 << 20),
        cost_estimate=pl.CostEstimate(flops=0, bytes_accessed=13 << 20, transcendentals=0),
        name="place_first",
    )(lens, received)


def settle_kernel(full, lens, window, second, extra, _, cache, out, patched, dups, sems, dup_sems):
    at = lax.broadcasted_iota(jnp.int32, (32, HD), 0)

    def patch_copy(s, c):
        return pltpu.make_async_copy(
            patched.at[s, c],
            cache.at[s * CAP, c, pl.ds(window_base(lens[s * CAP]), 32)],
            sems.at[s * 2 + c],
        )

    def dup_copy(s):
        return pltpu.make_async_copy(dups.at[s], cache.at[s * CAP + 1], dup_sems.at[s])

    for s in range(INST):
        length = lens[s * CAP]

        @pl.when(length > 0)
        def _():
            fresh = second[s, pl.ds(ROWS, 16)].astype(jnp.float32)
            where = at + window_base(length)
            for c in range(2):
                x = window[s, c].astype(jnp.float32)
                for t in range(STEPS):
                    x = jnp.where(where == length + t, fresh[c * 2 + t:c * 2 + t + 1], x)
                patched[s, c] = x.astype(jnp.bfloat16)
                patch_copy(s, c).start()

    order = jnp.int32(0)
    for s in range(INST):
        length = lens[s * CAP + 1]
        rank = jnp.minimum(order, DUPS - 1)
        order = order + (length > 0).astype(jnp.int32)

        @pl.when(length > 0)
        def _():
            def read(p, c):
                if full:
                    return extra[s, pl.ds((p * 2 + c) * PAGE, PAGE)]
                row = pl.multiple_of(B_DUP + rank * 2 * PIECE + c * PIECE, PIECE)
                return jnp.concatenate(
                    [second[p * MIGPG + i, pl.ds(row, PIECE)] for i in range(MIGPG)], axis=0
                )

            def write(p, c, x):
                dups[s, c, pl.ds(p * PAGE, PAGE)] = x

            for p in range(MIGPG):
                masked_page(read, write, length, lambda: second[s, pl.ds(32 + ROWS, 16)], p)
            dup_copy(s).start()

    for s in range(INST):
        for slot in range(CAP):
            filled = lens[s * CAP + slot] > 0
            rows = second[s, pl.ds(slot * 32, ROWS)]
            out[s * CAP + slot] = jnp.where(filled, rows, jnp.zeros_like(rows))
    for s in range(INST):
        @pl.when(lens[s * CAP] > 0)
        def _():
            for c in range(2):
                patch_copy(s, c).wait()

        @pl.when(lens[s * CAP + 1] > 0)
        def _():
            dup_copy(s).wait()


def settle_all(full, lens, window, second, extra, cache):
    def kernel(*refs):
        settle_kernel(full, *refs)

    return pl.pallas_call(
        kernel,
        out_shape=(
            jax.ShapeDtypeStruct(cache.shape, jnp.bfloat16),
            jax.ShapeDtypeStruct((INST * CAP, ROWS, HD), jnp.bfloat16),
        ),
        in_specs=[spec(SMEM)] + [spec(VMEM)] * 3 + [spec(pl.ANY)],
        out_specs=(spec(pl.ANY), spec(VMEM)),
        scratch_shapes=[
            pltpu.VMEM((INST, 2, 32, HD), jnp.bfloat16),
            pltpu.VMEM((INST, 2, MIGLEN, HD), jnp.bfloat16),
            pltpu.SemaphoreType.DMA((INST * 2,)),
            pltpu.SemaphoreType.DMA((INST,)),
        ],
        input_output_aliases={4: 0},
        compiler_params=pltpu.CompilerParams(vmem_limit_bytes=20 << 20),
        name="settle_full" if full else "settle_short",
    )(lens, window, second, extra, cache)


def on_device(
    queries,
    hidden_in,
    kv_weight,
    kv_pool,
    page_table,
    long_lengths,
    short_lengths,
    mig_order,
    destination,
):
    inst_index = lax.axis_index("inst")
    tp_index = lax.axis_index("tp")
    targets = destination.reshape(1, MIG)
    tables = (page_table, long_lengths, short_lengths, mig_order, targets)
    pages = kv_pool.reshape(PAGES, 2 * PAGE, HD)

    hidden = hidden_in.reshape(REQS * STEPS, -1)
    pieces = [hidden]
    for k in range(1, 4):
        pieces.append(
            lax.ppermute(hidden, "tp", [(i, (i // 2 + k) % 4 * 2 + i % 2) for i in range(8)])
        )
    own = jnp.stack(pieces)
    own, late_targets = lax.optimization_barrier((own, targets))
    mate = lax.ppermute(own, "tp", [(i, i ^ 1) for i in range(8)])
    first = build((*tables[:4], late_targets), pages)
    first, mate = lax.optimization_barrier((first, mate))
    got_first = lax.all_to_all(first, "inst", split_axis=0, concat_axis=0, tiled=True)

    hidden_all = join(tp_index.reshape(1), own, mate)
    fresh = jnp.einsum(
        "rd,dcn->rcn", hidden_all, kv_weight, preferred_element_type=jnp.float32
    ).astype(jnp.bfloat16)
    fresh = fresh.reshape(REQS, STEPS, 2, HD)
    values = jnp.pad(fresh[:, :, 1], ((0, 0), (0, 16 - STEPS), (0, 0)))
    keys_values = jnp.pad(
        fresh.transpose(0, 2, 1, 3).reshape(REQS, 2 * STEPS, HD),
        ((0, 0), (0, 16 - 2 * STEPS), (0, 0)),
    )
    stay, side = attend(
        tables, queries.reshape(REQS, ROWS, HD), keys_values, values, kv_pool
    )
    stay_out = stay.reshape(REQS, STEPS, KV_HEADS * HD)
    second = route(got_first, side)
    got_second = lax.all_to_all(second, "inst", split_axis=0, concat_axis=0, tiled=True)

    meta = got_first[:, A_META].astype(jnp.float32).astype(jnp.int32)
    lengths = (meta[:, :32] + 256 * meta[:, 32:64]).reshape(INST, INST, CAP)
    all_load = jnp.sum(meta[:, 64] + 128 * meta[:, 65] + 16384 * meta[:, 66])
    doubled = (lengths[:, :, 1] > 0).astype(jnp.int32)
    overflow = (jnp.max(jnp.sum(doubled, axis=0)) > DUPS) | (jnp.max(jnp.sum(doubled, axis=1)) > 1)
    index = jnp.arange(INST)
    arriving = jnp.sum(
        jnp.where(index[None, :, None] == inst_index, lengths, 0), axis=1
    ).reshape(INST * CAP)
    staying = jnp.any(
        mig_order[0, MIG:][:, None] == jnp.arange(SHORT)[None, :], axis=0
    )
    resident = (
        jnp.sum(long_lengths)
        + jnp.sum(jnp.where(staying, short_lengths[0], 0))
        + STEPS * (LONG + SHORT - MIG)
    )
    own_load = resident + jnp.sum(jnp.where(arriving > 0, arriving + STEPS, 0))
    load_share = (own_load.astype(jnp.float32) * INST / all_load.astype(jnp.float32)).reshape(1)

    cache, window = place_first(arriving, got_first)

    def short_path(args):
        lens, window, second, cache = args
        return tuple(settle_all(False, lens, window, second, window, cache))

    def long_path(args):
        lens, window, second, cache = args
        send = build_second(page_table, mig_order, targets, pages)
        got = lax.all_to_all(send, "inst", split_axis=0, concat_axis=0, tiled=True)
        return tuple(settle_all(True, lens, window, second, got, cache))

    moved_cache, moved = lax.cond(
        overflow, long_path, short_path, (arriving, window, got_second, cache)
    )
    moved_out = moved.reshape(INST * CAP, STEPS, KV_HEADS * HD)
    return (stay_out, moved_out, moved_cache, load_share)


def solution(mesh):
    placed = (
        P("inst", None, "tp"),
        P("inst", None, "tp"),
        P(None, None, "tp"),
        P("inst", None, None, "tp"),
        P("inst", None),
        P("inst", None),
        P("inst", None),
        P("inst", None),
        P("inst", None),
    )
    return jax.shard_map(
        on_device,
        mesh=mesh,
        in_specs=placed,
        out_specs=(
            P("inst", None, "tp"),
            P("inst", None, "tp"),
            P("inst", None, None, "tp"),
            P("inst"),
        ),
        check_vma=False,
    )
```

```python
import math

import jax
import jax.numpy as jnp
from jax import lax
from jax.experimental import pallas as pl
from jax.experimental.pallas import tpu as pltpu
from jax.sharding import PartitionSpec as P

HEADS = 64
KV_HEADS = 8
HD = 128
PAGE = 128
MAXPG = 64
MIGPG = 4
LONG = 2
MIG = 16
CAP = 2
STEPS = 2
SHORT = 20
REQS = 22
MIGLEN = 512
INST = 16
PAGES = 208
ROWS = 16
DUPS = 4
PIECE = MIGLEN // INST

A_DUP = 2 * MIGLEN
A_META = A_DUP + 2 * PIECE
A_ROWS = A_META + 16
B_DUP = 64
B_ROWS = B_DUP + DUPS * 2 * PIECE

SMEM = pltpu.SMEM
VMEM = pltpu.VMEM


def spec(space):
    return pl.BlockSpec(memory_space=space)


def clear(count):
    for i in range(INST):
        count[i] = 0


def take_slot(count, to):
    slot = count[to]
    count[to] = slot + 1
    return slot


def build_kernel(part, table, longs, shorts, order, dest, pool, *refs):
    out, count, held, extra, stage, sems, extra_sems, out_sems, stage_sem = refs[part:]
    half = MIG // 2
    begin_at, end_at = (half, MIG) if part else (0, half)

    def load(k, p):
        page = table[0, LONG * MAXPG + order[0, k] * MIGPG + p]
        return pltpu.make_async_copy(
            pool.at[page], held.at[k - begin_at, pl.ds(p * 2 * PAGE, 2 * PAGE)], sems.at[k * MIGPG + p]
        )

    def load_extra(k, p):
        page = table[0, LONG * MAXPG + order[0, k] * MIGPG + p]
        return pltpu.make_async_copy(pool.at[page], extra.at[p], extra_sems.at[p])

    def send(k):
        return pltpu.make_async_copy(
            held.at[k - begin_at], out.at[dest[0, k], pl.ds(0, 2 * MIGLEN)], out_sems.at[k]
        )

    clear(count)

    def begin(k, dup_at):
        slot = take_slot(count, dest[0, k])

        @pl.when((slot == 0) & (k >= begin_at))
        def _():
            for p in range(MIGPG):
                load(k, p).start()

        first = (slot == 1) & (dup_at < 0)
        if part:
            @pl.when(first)
            def _():
                for p in range(MIGPG):
                    load_extra(k, p).start()

        return jnp.where(first, k, dup_at)

    dup_at = lax.fori_loop(0, end_at, begin, jnp.int32(-1))
    clear(count)
    lane = lax.broadcasted_iota(jnp.int32, (16, 128), 1)

    def each(k, row):
        to = dest[0, k]
        slot = take_slot(count, to)
        length = shorts[0, order[0, k]]

        @pl.when((slot == 0) & (k >= begin_at))
        def _():
            for p in range(MIGPG):
                load(k, p).wait()
            send(k).start()

        at = to * CAP + slot
        row = jnp.where(lane == at, length & 255, row)
        return jnp.where(lane == at + 32, length >> 8, row)

    row = lax.fori_loop(0, end_at, each, jnp.zeros((16, 128), jnp.int32))
    if part:
        last = pltpu.make_async_copy(stage, out.at[:, pl.ds(A_DUP, A_ROWS - A_DUP)], stage_sem)
        total = jnp.int32(STEPS * REQS)
        for i in range(LONG):
            total = total + longs[0, i]
        for i in range(SHORT):
            total = total + shorts[0, i]
        row = jnp.where(lane == 64, total & 127, row)
        row = jnp.where(lane == 65, (total >> 7) & 127, row)
        row = jnp.where(lane == 66, total >> 14, row)
        dup_to = jnp.where(dup_at >= 0, dest[0, jnp.maximum(dup_at, 0)] + 1, 0)
        row = jnp.where(lane == 67, dup_to, row)
        tables = row.astype(jnp.float32).astype(jnp.bfloat16)

        @pl.when(dup_at >= 0)
        def _():
            for p in range(MIGPG):
                load_extra(dup_at, p).wait()
            for m in range(INST):
                for c in range(2):
                    stage[m, pl.ds(c * PIECE, PIECE)] = extra[
                        m // MIGPG, pl.ds(c * PAGE + m % MIGPG * PIECE, PIECE)
                    ]

        for m in range(INST):
            stage[m, pl.ds(2 * PIECE, 16)] = tables
        last.start()
    clear(count)

    def finish(k, carry):
        slot = take_slot(count, dest[0, k])

        @pl.when((slot == 0) & (k >= begin_at))
        def _():
            send(k).wait()

        return carry

    lax.fori_loop(0, end_at, finish, 0)
    if part:
        last.wait()


def build(part, tables, pool, *earlier):
    def kernel(*refs):
        build_kernel(part, *refs)

    return pl.pallas_call(
        kernel,
        out_shape=jax.ShapeDtypeStruct((INST, A_ROWS, HD), jnp.bfloat16),
        in_specs=[spec(SMEM)] * 5 + [spec(pl.ANY)] + [spec(pltpu.HBM)] * len(earlier),
        out_specs=spec(pltpu.HBM),
        scratch_shapes=[
            pltpu.SMEM((INST,), jnp.int32),
            pltpu.VMEM((MIG // 2, 2 * MIGLEN, HD), jnp.bfloat16),
            pltpu.VMEM((MIGPG, 2 * PAGE, HD), jnp.bfloat16),
            pltpu.VMEM((INST, A_ROWS - A_DUP, HD), jnp.bfloat16),
            pltpu.SemaphoreType.DMA((MIG * MIGPG,)),
            pltpu.SemaphoreType.DMA((MIGPG,)),
            pltpu.SemaphoreType.DMA((MIG,)),
            pltpu.SemaphoreType.DMA(()),
        ],
        input_output_aliases={6: 0} if part else {},
        compiler_params=pltpu.CompilerParams(vmem_limit_bytes=60 << 20),
        cost_estimate=pl.CostEstimate(flops=0, bytes_accessed=9 << 20, transcendentals=0),
        name="build_rest" if part else "build_half",
    )(*tables, pool, *earlier)


def second_kernel(table, order, dest, pool, out, count, held, sems, out_sems):
    def load(k, p):
        page = table[0, LONG * MAXPG + order[0, k] * MIGPG + p]
        return pltpu.make_async_copy(
            pool.at[page], held.at[dest[0, k], pl.ds(p * 2 * PAGE, 2 * PAGE)], sems.at[k * MIGPG + p]
        )

    def send(k):
        to = dest[0, k]
        return pltpu.make_async_copy(held.at[to], out.at[to], out_sems.at[k])

    for stage in range(3):
        clear(count)

        def each(k, carry):
            slot = take_slot(count, dest[0, k])

            @pl.when(slot == 1)
            def _():
                if stage == 0:
                    for p in range(MIGPG):
                        load(k, p).start()
                elif stage == 1:
                    for p in range(MIGPG):
                        load(k, p).wait()
                    send(k).start()
                else:
                    send(k).wait()

            return carry

        lax.fori_loop(0, MIG, each, 0)


def build_second(table, order, dest, pool):
    return pl.pallas_call(
        second_kernel,
        out_shape=jax.ShapeDtypeStruct((INST, 2 * MIGLEN, HD), jnp.bfloat16),
        in_specs=[spec(SMEM)] * 3 + [spec(pl.ANY)],
        out_specs=spec(pl.ANY),
        scratch_shapes=[
            pltpu.SMEM((INST,), jnp.int32),
            pltpu.VMEM((INST, 2 * MIGLEN, HD), jnp.bfloat16),
            pltpu.SemaphoreType.DMA((MIG * MIGPG,)),
            pltpu.SemaphoreType.DMA((MIG,)),
        ],
        compiler_params=pltpu.CompilerParams(vmem_limit_bytes=12 << 20),
        name="build_second",
    )(table, order, dest, pool)


def dot_nt(a, b):
    return lax.dot_general(a, b, (((1,), (1,)), ((), ())), preferred_element_type=jnp.float32)


def dot_nn(a, b):
    return lax.dot_general(a, b, (((1,), (0,)), ((), ())), preferred_element_type=jnp.float32)


GROUP = 4
CHUNK = 1024
SCALE = 1.0 / math.sqrt(HD)


def attend_kernel(
    table, longs, shorts, order, dest, query, keys_values, values, pool, stay, side,
    count, place, cache, score, page_sems,
):
    def load(pg, sem):
        return pltpu.make_async_copy(pool.at[table[0, pg]], cache.at[:, pg], sem)

    def wait_pages(first, size, sem):
        pltpu.make_async_copy(
            cache.at[:, pl.ds(first, size)], cache.at[:, pl.ds(first, size)], sem
        ).wait()

    for r in range(SHORT // GROUP):
        def start_short(i, carry, r=r):
            load(LONG * MAXPG + r * GROUP * MIGPG + i, page_sems.at[r]).start()
            return carry

        lax.fori_loop(0, GROUP * MIGPG, start_short, 0)
    for j in range(LONG):
        def start_long(i, carry, j=j):
            load(j * MAXPG + i, page_sems.at[SHORT // GROUP + j]).start()
            return carry

        lax.fori_loop(0, MAXPG, start_long, 0)

    clear(count)
    for i in range(SHORT):
        place[i] = -1

    def settle(k, carry):
        to = dest[0, k]
        place[order[0, k]] = to * CAP + take_slot(count, to)
        return carry

    lax.fori_loop(0, MIG, settle, 0)

    def fresh_scores(q, r):
        s = dot_nt(q, keys_values[r]) * SCALE
        step = lax.broadcasted_iota(jnp.int32, s.shape, 0) // 8
        col = lax.broadcasted_iota(jnp.int32, s.shape, 1)
        return jnp.where((col <= step) & (col < STEPS), s, -1e30)

    def short_group(g, carry):
        first = pl.multiple_of(LONG * MAXPG + g * GROUP * MIGPG, GROUP * MIGPG)
        wait_pages(first, GROUP * MIGPG, page_sems.at[g])
        pos = lax.broadcasted_iota(jnp.int32, (ROWS, MIGLEN), 1)
        old, new = [], []
        for i in range(GROUP):
            r = g * GROUP + i
            q = query[LONG + r]
            k = cache[0, pl.ds(first + i * MIGPG, MIGPG)].reshape(MIGLEN, HD)
            s = dot_nt(q, k) * SCALE
            old.append(jnp.where(pos < shorts[0, r], s, -1e30))
            new.append(fresh_scores(q, LONG + r))
        old = jnp.concatenate(old, axis=0)
        new = jnp.concatenate(new, axis=0)
        peak = jnp.maximum(jnp.max(old, 1, keepdims=True), jnp.max(new, 1, keepdims=True))
        old = jnp.exp(old - peak)
        new = jnp.exp(new - peak)
        denominator = jnp.sum(old, 1, keepdims=True) + jnp.sum(new, 1, keepdims=True)
        old = (old / denominator).astype(jnp.bfloat16)
        new = (new / denominator).astype(jnp.bfloat16)
        for i in range(GROUP):
            r = g * GROUP + i
            v = cache[1, pl.ds(first + i * MIGPG, MIGPG)].reshape(MIGLEN, HD)
            o = dot_nn(old[i * ROWS:(i + 1) * ROWS], v)
            o = o + dot_nn(new[i * ROWS:(i + 1) * ROWS], values[LONG + r])
            o = o.astype(jnp.bfloat16)
            at = place[r]

            @pl.when(at < 0)
            def _():
                stay[LONG + r] = o

            @pl.when(at >= 0)
            def _():
                stay[LONG + r] = jnp.zeros_like(o)
                side[at, pl.ds(0, ROWS)] = o
                side[at, pl.ds(ROWS, 16)] = keys_values[LONG + r]

        return carry

    lax.fori_loop(0, SHORT // GROUP, short_group, 0)

    for j in range(LONG):
        wait_pages(j * MAXPG, MAXPG, page_sems.at[SHORT // GROUP + j])
        q = query[j]
        new = fresh_scores(q, j)
        top = jnp.max(new, 1, keepdims=True)
        length = longs[0, j]
        steps = MAXPG * PAGE // CHUNK
        per = CHUNK // PAGE
        for i in range(steps):
            k = cache[0, pl.ds(j * MAXPG + i * per, per)].reshape(CHUNK, HD)
            s = dot_nt(q, k) * SCALE
            pos = lax.broadcasted_iota(jnp.int32, s.shape, 1) + i * CHUNK
            s = jnp.where(pos < length, s, -1e30)
            score[j, i] = s
            top = jnp.maximum(top, jnp.max(s, 1, keepdims=True))
        new = jnp.exp(new - top)
        denominator = jnp.sum(new, 1, keepdims=True)
        for i in range(steps):
            e = jnp.exp(score[j, i] - top)
            score[j, i] = e
            denominator = denominator + jnp.sum(e, 1, keepdims=True)
        inverse = 1.0 / denominator
        o = dot_nn((new * inverse).astype(jnp.bfloat16), values[j])
        for i in range(steps):
            v = cache[1, pl.ds(j * MAXPG + i * per, per)].reshape(CHUNK, HD)
            o = o + dot_nn((score[j, i] * inverse).astype(jnp.bfloat16), v)
        stay[j] = o.astype(jnp.bfloat16)


def attend(tables, query, keys_values, values, pool):
    return pl.pallas_call(
        attend_kernel,
        out_shape=(
            jax.ShapeDtypeStruct((REQS, ROWS, HD), jnp.bfloat16),
            jax.ShapeDtypeStruct((INST * CAP, 32, HD), jnp.bfloat16),
        ),
        in_specs=[spec(SMEM)] * 5 + [spec(VMEM)] * 3 + [spec(pl.ANY)],
        out_specs=(spec(VMEM), spec(VMEM)),
        scratch_shapes=[
            pltpu.SMEM((INST,), jnp.int32),
            pltpu.SMEM((SHORT,), jnp.int32),
            pltpu.VMEM((2, PAGES, PAGE, HD), jnp.bfloat16),
            pltpu.VMEM((LONG, MAXPG * PAGE // CHUNK, ROWS, CHUNK), jnp.float32),
            pltpu.SemaphoreType.DMA((SHORT // GROUP + LONG,)),
        ],
        compiler_params=pltpu.CompilerParams(vmem_limit_bytes=24 << 20),
        cost_estimate=pl.CostEstimate(
            flops=4 * 26624 * 16 * 128, bytes_accessed=14 << 20, transcendentals=26624 * 16
        ),
        name="attend_all",
    )(*tables, query, keys_values, values, pool)


def join_kernel(here, blocks, out):
    me = here[0]
    width = blocks.shape[2]
    for k in range(8):
        x = (me // 2 + 4 - k % 4) % 4
        y = (me + k // 4) % 2
        at = pl.multiple_of((x * 2 + y) * width, width)
        out[:, pl.ds(at, width)] = blocks[k]


def join(here, blocks):
    _, rows, width = blocks.shape
    return pl.pallas_call(
        join_kernel,
        out_shape=jax.ShapeDtypeStruct((rows, width * 8), jnp.bfloat16),
        in_specs=[spec(SMEM), spec(VMEM)],
        out_specs=spec(VMEM),
        name="join_hidden",
    )(here, blocks)


def route_kernel(received, side, out, small, count, sem):
    copy = pltpu.make_async_copy(received.at[:, pl.ds(A_DUP, A_ROWS - A_DUP)], small, sem)
    copy.start()
    clear(count)
    for d in range(INST):
        for c in range(CAP):
            out[d, pl.ds(c * 32, 32)] = side[d * CAP + c]
    copy.wait()
    lane = lax.broadcasted_iota(jnp.int32, (16, 128), 1)
    targets = []
    for s in range(INST):
        tables = small[s, pl.ds(2 * PIECE, 16)].astype(jnp.float32)
        targets.append(jnp.max(jnp.where(lane == 67, tables, 0.0)).astype(jnp.int32) - 1)
    for s in range(INST):
        to = targets[s]
        at = jnp.maximum(to, 0)

        @pl.when((to >= 0) & (count[at] < DUPS))
        def _():
            slot = take_slot(count, at)
            row = pl.multiple_of(B_DUP + slot * 2 * PIECE, 2 * PIECE)
            out[at, pl.ds(row, 2 * PIECE)] = small[s, pl.ds(0, 2 * PIECE)]


def route(received, side):
    return pl.pallas_call(
        route_kernel,
        out_shape=jax.ShapeDtypeStruct((INST, B_ROWS, HD), jnp.bfloat16),
        in_specs=[spec(pl.ANY), spec(VMEM)],
        out_specs=spec(VMEM),
        scratch_shapes=[
            pltpu.VMEM((INST, A_ROWS - A_DUP, HD), jnp.bfloat16),
            pltpu.SMEM((INST,), jnp.int32),
            pltpu.SemaphoreType.DMA(()),
        ],
        cost_estimate=pl.CostEstimate(flops=0, bytes_accessed=2 << 20, transcendentals=0),
        name="route_pieces",
    )(received, side)


def decode_kernel(here, longs, shorts, order, received, lens, load, small, sem):
    copy = pltpu.make_async_copy(received.at[:, pl.ds(A_META, 16)], small, sem)
    copy.start()
    resident = jnp.int32(STEPS * (LONG + SHORT - MIG))
    for i in range(LONG):
        resident = resident + longs[0, i]
    for i in range(MIG, SHORT):
        resident = resident + shorts[0, order[0, i]]
    copy.wait()

    def total(x, axis=None):
        return jnp.sum(x, axis=axis, keepdims=True)

    x = jnp.max(small[...].astype(jnp.float32), axis=1)
    lane = lax.broadcasted_iota(jnp.int32, x.shape, 1)
    table = jnp.where(lane < INST * CAP, x + 256.0 * pltpu.roll(x, 96, 1), 0.0)
    own = resident.astype(jnp.float32)
    result = jnp.zeros_like(x)
    for slot in range(CAP):
        length = total(jnp.where(lane == here[0] * CAP + slot, table, 0.0), 1)
        result = jnp.where(lane == slot, length, result)
        own = own + total(jnp.where(length > 0.0, length + STEPS, 0.0))
    lens[...] = result.astype(jnp.int32)
    digits = jnp.where(lane == 64, 1.0, jnp.where(lane == 65, 128.0, jnp.where(lane == 66, 16384.0, 0.0)))
    share = own * INST / total(x * digits)
    double = jnp.where((table > 0.0) & (lane % 2 == 1), 1.0, 0.0)
    sends = jnp.max(total(double, 1), keepdims=True)
    takes = jnp.max(total(double, 0), keepdims=True)
    over = jnp.where((sends > 1.0) | (takes > DUPS), 1.0, 0.0)
    row = lax.broadcasted_iota(jnp.int32, (8, 128), 0)
    load[...] = jnp.where(row == 0, share, over)


def decode(here, longs, shorts, order, received):
    return pl.pallas_call(
        decode_kernel,
        out_shape=(
            jax.ShapeDtypeStruct((INST, 128), jnp.int32),
            jax.ShapeDtypeStruct((8, 128), jnp.float32),
        ),
        in_specs=[spec(SMEM)] * 4 + [spec(pl.ANY)],
        out_specs=(spec(VMEM), spec(VMEM)),
        scratch_shapes=[
            pltpu.VMEM((INST, 16, HD), jnp.bfloat16),
            pltpu.SemaphoreType.DMA(()),
        ],
        name="decode_tables",
    )(here, longs, shorts, order, received)


def window_base(length):
    return pl.multiple_of(jnp.minimum(length // 16 * 16, MIGLEN - 32), 16)


def masked_page(read, write, length, fresh, p):
    grown = length + STEPS if fresh is not None else length
    whole = length >= (p + 1) * PAGE
    empty = grown <= p * PAGE

    @pl.when(whole)
    def _():
        for c in range(2):
            write(p, c, read(p, c))

    @pl.when(empty)
    def _():
        for c in range(2):
            write(p, c, jnp.zeros((PAGE, HD), jnp.bfloat16))

    @pl.when(jnp.logical_not(whole | empty))
    def _():
        at = lax.broadcasted_iota(jnp.int32, (PAGE, HD), 0) + p * PAGE
        for c in range(2):
            x = jnp.where(at < length, read(p, c).astype(jnp.float32), 0.0)
            if fresh is not None:
                rows = fresh().astype(jnp.float32)
                for t in range(STEPS):
                    x = jnp.where(at == length + t, rows[c * 2 + t:c * 2 + t + 1], x)
            write(p, c, x.astype(jnp.bfloat16))


def place_kernel(lens, block, cache, window):
    s = pl.program_id(0)
    length = lens[s, 0]

    def read(p, c):
        return block[0, pl.ds((p * 2 + c) * PAGE, PAGE)]

    def write(p, c, x):
        cache[0, c, pl.ds(p * PAGE, PAGE)] = x

    for p in range(MIGPG):
        masked_page(read, write, length, None, p)
    cache[1] = jnp.zeros((2, MIGLEN, HD), jnp.bfloat16)
    base = window_base(length)
    for c in range(2):
        window[0, c] = cache[0, c, pl.ds(base, 32)]


def place_first(lens, received):
    return pl.pallas_call(
        place_kernel,
        out_shape=(
            jax.ShapeDtypeStruct((INST * CAP, 2, MIGLEN, HD), jnp.bfloat16),
            jax.ShapeDtypeStruct((INST, 2, 32, HD), jnp.bfloat16),
        ),
        grid_spec=pltpu.PrefetchScalarGridSpec(
            num_scalar_prefetch=1,
            grid=(INST,),
            in_specs=[pl.BlockSpec((1, 2 * MIGLEN, HD), lambda s, _: (s, 0, 0))],
            out_specs=[
                pl.BlockSpec((CAP, 2, MIGLEN, HD), lambda s, _: (s, 0, 0, 0)),
                pl.BlockSpec((1, 2, 32, HD), lambda s, _: (s, 0, 0, 0)),
            ],
        ),
        compiler_params=pltpu.CompilerParams(vmem_limit_bytes=8 << 20),
        cost_estimate=pl.CostEstimate(flops=0, bytes_accessed=13 << 20, transcendentals=0),
        name="place_first",
    )(lens, received)


def settle_kernel(full, lens, window, second, extra, _, cache, out, patched, dups, sems, dup_sems):
    at = lax.broadcasted_iota(jnp.int32, (32, HD), 0)

    def patch_copy(s, c):
        return pltpu.make_async_copy(
            patched.at[s, c],
            cache.at[s * CAP, c, pl.ds(window_base(lens[s, 0]), 32)],
            sems.at[s * 2 + c],
        )

    def dup_copy(s):
        return pltpu.make_async_copy(dups.at[s], cache.at[s * CAP + 1], dup_sems.at[s])

    for s in range(INST):
        length = lens[s, 0]

        @pl.when(length > 0)
        def _():
            fresh = second[s, pl.ds(ROWS, 16)].astype(jnp.float32)
            where = at + window_base(length)
            for c in range(2):
                x = window[s, c].astype(jnp.float32)
                for t in range(STEPS):
                    x = jnp.where(where == length + t, fresh[c * 2 + t:c * 2 + t + 1], x)
                patched[s, c] = x.astype(jnp.bfloat16)
                patch_copy(s, c).start()

    order = jnp.int32(0)
    for s in range(INST):
        length = lens[s, 1]
        rank = jnp.minimum(order, DUPS - 1)
        order = order + (length > 0).astype(jnp.int32)

        @pl.when(length > 0)
        def _():
            def read(p, c):
                if full:
                    return extra[s, pl.ds((p * 2 + c) * PAGE, PAGE)]
                row = pl.multiple_of(B_DUP + rank * 2 * PIECE + c * PIECE, PIECE)
                return jnp.concatenate(
                    [second[p * MIGPG + i, pl.ds(row, PIECE)] for i in range(MIGPG)], axis=0
                )

            def write(p, c, x):
                dups[s, c, pl.ds(p * PAGE, PAGE)] = x

            for p in range(MIGPG):
                masked_page(read, write, length, lambda: second[s, pl.ds(32 + ROWS, 16)], p)
            dup_copy(s).start()

    for s in range(INST):
        for slot in range(CAP):
            filled = lens[s, slot] > 0
            rows = second[s, pl.ds(slot * 32, ROWS)]
            out[s * CAP + slot] = jnp.where(filled, rows, jnp.zeros_like(rows))
    for s in range(INST):
        @pl.when(lens[s, 0] > 0)
        def _():
            for c in range(2):
                patch_copy(s, c).wait()

        @pl.when(lens[s, 1] > 0)
        def _():
            dup_copy(s).wait()


def settle_all(full, lens, window, second, extra, cache):
    def kernel(*refs):
        settle_kernel(full, *refs)

    return pl.pallas_call(
        kernel,
        out_shape=(
            jax.ShapeDtypeStruct(cache.shape, jnp.bfloat16),
            jax.ShapeDtypeStruct((INST * CAP, ROWS, HD), jnp.bfloat16),
        ),
        in_specs=[spec(SMEM)] + [spec(VMEM)] * 3 + [spec(pl.ANY)],
        out_specs=(spec(pl.ANY), spec(VMEM)),
        scratch_shapes=[
            pltpu.VMEM((INST, 2, 32, HD), jnp.bfloat16),
            pltpu.VMEM((INST, 2, MIGLEN, HD), jnp.bfloat16),
            pltpu.SemaphoreType.DMA((INST * 2,)),
            pltpu.SemaphoreType.DMA((INST,)),
        ],
        input_output_aliases={4: 0},
        compiler_params=pltpu.CompilerParams(vmem_limit_bytes=20 << 20),
        name="settle_full" if full else "settle_short",
    )(lens, window, second, extra, cache)


def on_device(
    queries,
    hidden_in,
    kv_weight,
    kv_pool,
    page_table,
    long_lengths,
    short_lengths,
    mig_order,
    destination,
):
    inst_index = lax.axis_index("inst")
    tp_index = lax.axis_index("tp")
    targets = destination.reshape(1, MIG)
    tables = (page_table, long_lengths, short_lengths, mig_order, targets)
    pages = kv_pool.reshape(PAGES, 2 * PAGE, HD)

    def from_x(value, k):
        return lax.ppermute(value, "tp", [(i, (i // 2 + k) % 4 * 2 + i % 2) for i in range(8)])

    def from_y(value):
        return lax.ppermute(value, "tp", [(i, i ^ 1) for i in range(8)])

    near = [hidden_in, from_x(hidden_in, 1), from_x(hidden_in, 2), from_x(hidden_in, 3)]
    far = [from_y(hidden_in)]
    half = build(0, tables, pages)
    near[2], far[0], late_targets, half = lax.optimization_barrier(
        (near[2], far[0], targets, half)
    )
    far += [from_x(far[0], 1), from_y(near[2]), from_x(far[0], 3)]
    first = build(1, (*tables[:4], late_targets), pages, half)
    first, *blocks = lax.optimization_barrier((first, *near[1:], *far))
    blocks = jnp.stack([hidden_in, *blocks]).reshape(8, REQS * STEPS, -1)
    got_first = lax.all_to_all(first, "inst", split_axis=0, concat_axis=0, tiled=True)

    hidden_all = join(tp_index.reshape(1), blocks)
    fresh = jnp.einsum(
        "rd,dcn->rcn", hidden_all, kv_weight, preferred_element_type=jnp.float32
    ).astype(jnp.bfloat16)
    fresh = fresh.reshape(REQS, STEPS, 2, HD)
    values = jnp.pad(fresh[:, :, 1], ((0, 0), (0, 16 - STEPS), (0, 0)))
    keys_values = jnp.pad(
        fresh.transpose(0, 2, 1, 3).reshape(REQS, 2 * STEPS, HD),
        ((0, 0), (0, 16 - 2 * STEPS), (0, 0)),
    )
    stay, side = attend(
        tables, queries.reshape(REQS, ROWS, HD), keys_values, values, kv_pool
    )
    stay_out = stay.reshape(REQS, STEPS, KV_HEADS * HD)
    second = route(got_first, side)
    got_second = lax.all_to_all(second, "inst", split_axis=0, concat_axis=0, tiled=True)

    arriving, load = decode(
        inst_index.reshape(1), long_lengths, short_lengths, mig_order, got_first
    )
    load_share = load[0, :1]
    overflow = load[1, 0] > 0.5

    cache, window = place_first(arriving, got_first)

    def short_path(args):
        lens, window, second, cache = args
        return tuple(settle_all(False, lens, window, second, window, cache))

    def long_path(args):
        lens, window, second, cache = args
        send = build_second(page_table, mig_order, targets, pages)
        got = lax.all_to_all(send, "inst", split_axis=0, concat_axis=0, tiled=True)
        return tuple(settle_all(True, lens, window, second, got, cache))

    moved_cache, moved = lax.cond(
        overflow, long_path, short_path, (arriving, window, got_second, cache)
    )
    moved_out = moved.reshape(INST * CAP, STEPS, KV_HEADS * HD)
    return (stay_out, moved_out, moved_cache, load_share)


def solution(mesh):
    placed = (
        P("inst", None, "tp"),
        P("inst", None, "tp"),
        P(None, None, "tp"),
        P("inst", None, None, "tp"),
        P("inst", None),
        P("inst", None),
        P("inst", None),
        P("inst", None),
        P("inst", None),
    )
    return jax.shard_map(
        on_device,
        mesh=mesh,
        in_specs=placed,
        out_specs=(
            P("inst", None, "tp"),
            P("inst", None, "tp"),
            P("inst", None, None, "tp"),
            P("inst"),
        ),
        check_vma=False,
    )
```

```python
import math

import jax
import jax.numpy as jnp
from jax import lax
from jax.experimental import pallas as pl
from jax.experimental.pallas import tpu as pltpu
from jax.sharding import PartitionSpec as P

HEADS = 64
KV_HEADS = 8
HD = 128
PAGE = 128
MAXPG = 64
MIGPG = 4
LONG = 2
MIG = 16
CAP = 2
STEPS = 2
SHORT = 20
REQS = 22
MIGLEN = 512
INST = 16
PAGES = 208
ROWS = 16
DUPS = 4
PIECE = MIGLEN // INST

A_DUP = 2 * MIGLEN
A_META = A_DUP + 2 * PIECE
A_ROWS = A_META + 16
B_DUP = 64
B_ROWS = B_DUP + DUPS * 2 * PIECE

SMEM = pltpu.SMEM
VMEM = pltpu.VMEM


def spec(space):
    return pl.BlockSpec(memory_space=space)


def clear(count):
    for i in range(INST):
        count[i] = 0


def take_slot(count, to):
    slot = count[to]
    count[to] = slot + 1
    return slot


def build_kernel(
    table, longs, shorts, order, dest, pool, out, count, slots, held, extra, stage, sems, extra_sem, out_sems, stage_sem
):
    def load(page, k, p):
        return pltpu.make_async_copy(
            pool.at[page], held.at[k, pl.ds(p * 2 * PAGE, 2 * PAGE)], sems.at[k]
        )

    def send(k):
        return pltpu.make_async_copy(
            held.at[k], out.at[dest[0, k], pl.ds(0, 2 * MIGLEN)], out_sems.at[k]
        )

    clear(count)

    def begin(k, dup_at):
        slot = take_slot(count, dest[0, k])
        slots[k] = slot
        first = LONG * MAXPG + order[0, k] * MIGPG

        @pl.when(slot == 0)
        def _():
            for p in range(MIGPG):
                load(table[0, first + p], k, p).start()

        second = (slot == 1) & (dup_at < 0)

        @pl.when(second)
        def _():
            for p in range(MIGPG):
                pltpu.make_async_copy(pool.at[table[0, first + p]], extra.at[p], extra_sem).start()

        return jnp.where(second, k, dup_at)

    dup_at = lax.fori_loop(0, MIG, begin, jnp.int32(-1))
    lane = lax.broadcasted_iota(jnp.int32, (16, 128), 1)
    total = jnp.int32(STEPS * REQS)
    for i in range(LONG):
        total = total + longs[0, i]
    for i in range(SHORT):
        total = total + shorts[0, i]
    dup_to = jnp.where(dup_at >= 0, dest[0, jnp.maximum(dup_at, 0)] + 1, 0)
    row = jnp.zeros((16, 128), jnp.int32)
    for at, value in ((64, total & 127), (65, (total >> 7) & 127), (66, total >> 14), (67, dup_to)):
        row = jnp.where(lane == at, value, row)
    for k in range(MIG):
        at = dest[0, k] * CAP + slots[k]
        length = shorts[0, order[0, k]]
        row = jnp.where(lane == at, length & 255, row)
        row = jnp.where(lane == at + 32, length >> 8, row)
    tables = row.astype(jnp.float32).astype(jnp.bfloat16)
    for m in range(INST):
        stage[m, pl.ds(2 * PIECE, 16)] = tables

    def each(k, carry):
        @pl.when(slots[k] == 0)
        def _():
            pltpu.make_async_copy(held.at[k], held.at[k], sems.at[k]).wait()
            send(k).start()

        return carry

    lax.fori_loop(0, MIG, each, 0)

    @pl.when(dup_at >= 0)
    def _():
        pltpu.make_async_copy(extra, extra, extra_sem).wait()
        for m in range(INST):
            for c in range(2):
                stage[m, pl.ds(c * PIECE, PIECE)] = extra[
                    m // MIGPG, pl.ds(c * PAGE + m % MIGPG * PIECE, PIECE)
                ]

    last = pltpu.make_async_copy(stage, out.at[:, pl.ds(A_DUP, A_ROWS - A_DUP)], stage_sem)
    last.start()

    def finish(k, carry):
        @pl.when(slots[k] == 0)
        def _():
            send(k).wait()

        return carry

    lax.fori_loop(0, MIG, finish, 0)
    last.wait()


def build(tables, pool):
    return pl.pallas_call(
        build_kernel,
        out_shape=jax.ShapeDtypeStruct((INST, A_ROWS, HD), jnp.bfloat16),
        in_specs=[spec(SMEM)] * 5 + [spec(pl.ANY)],
        out_specs=spec(pltpu.HBM),
        scratch_shapes=[
            pltpu.SMEM((INST,), jnp.int32),
            pltpu.SMEM((MIG,), jnp.int32),
            pltpu.VMEM((MIG, 2 * MIGLEN, HD), jnp.bfloat16),
            pltpu.VMEM((MIGPG, 2 * PAGE, HD), jnp.bfloat16),
            pltpu.VMEM((INST, A_ROWS - A_DUP, HD), jnp.bfloat16),
            pltpu.SemaphoreType.DMA((MIG,)),
            pltpu.SemaphoreType.DMA(()),
            pltpu.SemaphoreType.DMA((MIG,)),
            pltpu.SemaphoreType.DMA(()),
        ],
        compiler_params=pltpu.CompilerParams(vmem_limit_bytes=60 << 20),
        cost_estimate=pl.CostEstimate(flops=0, bytes_accessed=9 << 20, transcendentals=0),
        name="build_first",
    )(*tables, pool)


def second_kernel(table, order, dest, pool, out, count, held, sems, out_sems):
    def load(k, p):
        page = table[0, LONG * MAXPG + order[0, k] * MIGPG + p]
        return pltpu.make_async_copy(
            pool.at[page], held.at[dest[0, k], pl.ds(p * 2 * PAGE, 2 * PAGE)], sems.at[k * MIGPG + p]
        )

    def send(k):
        to = dest[0, k]
        return pltpu.make_async_copy(held.at[to], out.at[to], out_sems.at[k])

    for stage in range(3):
        clear(count)

        def each(k, carry):
            slot = take_slot(count, dest[0, k])

            @pl.when(slot == 1)
            def _():
                if stage == 0:
                    for p in range(MIGPG):
                        load(k, p).start()
                elif stage == 1:
                    for p in range(MIGPG):
                        load(k, p).wait()
                    send(k).start()
                else:
                    send(k).wait()

            return carry

        lax.fori_loop(0, MIG, each, 0)


def build_second(table, order, dest, pool):
    return pl.pallas_call(
        second_kernel,
        out_shape=jax.ShapeDtypeStruct((INST, 2 * MIGLEN, HD), jnp.bfloat16),
        in_specs=[spec(SMEM)] * 3 + [spec(pl.ANY)],
        out_specs=spec(pl.ANY),
        scratch_shapes=[
            pltpu.SMEM((INST,), jnp.int32),
            pltpu.VMEM((INST, 2 * MIGLEN, HD), jnp.bfloat16),
            pltpu.SemaphoreType.DMA((MIG * MIGPG,)),
            pltpu.SemaphoreType.DMA((MIG,)),
        ],
        compiler_params=pltpu.CompilerParams(vmem_limit_bytes=12 << 20),
        name="build_second",
    )(table, order, dest, pool)


def dot_nt(a, b):
    return lax.dot_general(a, b, (((1,), (1,)), ((), ())), preferred_element_type=jnp.float32)


def dot_nn(a, b):
    return lax.dot_general(a, b, (((1,), (0,)), ((), ())), preferred_element_type=jnp.float32)


GROUP = 4
CHUNK = 1024
SCALE = 1.0 / math.sqrt(HD)


def attend_kernel(
    table, longs, shorts, order, dest, query, keys_values, values, pool, stay, out,
    count, place, cache, score, side, page_sems, long_sems, side_sem,
):
    def load(pg, sem):
        return pltpu.make_async_copy(pool.at[table[0, pg]], cache.at[:, pg], sem)

    def wait_pages(first, size, sem):
        pltpu.make_async_copy(
            cache.at[:, pl.ds(first, size)], cache.at[:, pl.ds(first, size)], sem
        ).wait()

    for r in range(SHORT // GROUP):
        def start_short(i, carry, r=r):
            load(LONG * MAXPG + r * GROUP * MIGPG + i, page_sems.at[r]).start()
            return carry

        lax.fori_loop(0, GROUP * MIGPG, start_short, 0)
    per = CHUNK // PAGE
    chunks = [(longs[0, j] + CHUNK - 1) // CHUNK for j in range(LONG)]
    for j in range(LONG):
        def start_long(i, carry, j=j):
            for p in range(per):
                load(j * MAXPG + i * per + p, long_sems.at[j, i]).start()
            return carry

        lax.fori_loop(0, chunks[j], start_long, 0)

    clear(count)
    for i in range(SHORT):
        place[i] = -1

    def settle(k, carry):
        to = dest[0, k]
        place[order[0, k]] = to * CAP + take_slot(count, to)
        return carry

    lax.fori_loop(0, MIG, settle, 0)

    def fresh_scores(q, r):
        s = dot_nt(q, keys_values[r]) * SCALE
        step = lax.broadcasted_iota(jnp.int32, s.shape, 0) // 8
        col = lax.broadcasted_iota(jnp.int32, s.shape, 1)
        return jnp.where((col <= step) & (col < STEPS), s, -1e30)

    def short_group(g, carry):
        first = pl.multiple_of(LONG * MAXPG + g * GROUP * MIGPG, GROUP * MIGPG)
        wait_pages(first, GROUP * MIGPG, page_sems.at[g])
        pos = lax.broadcasted_iota(jnp.int32, (ROWS, MIGLEN), 1)
        old, new = [], []
        for i in range(GROUP):
            r = g * GROUP + i
            q = query[LONG + r]
            k = cache[0, pl.ds(first + i * MIGPG, MIGPG)].reshape(MIGLEN, HD)
            s = dot_nt(q, k) * SCALE
            old.append(jnp.where(pos < shorts[0, r], s, -1e30))
            new.append(fresh_scores(q, LONG + r))
        old = jnp.concatenate(old, axis=0)
        new = jnp.concatenate(new, axis=0)
        peak = jnp.maximum(jnp.max(old, 1, keepdims=True), jnp.max(new, 1, keepdims=True))
        old = jnp.exp(old - peak)
        new = jnp.exp(new - peak)
        denominator = jnp.sum(old, 1, keepdims=True) + jnp.sum(new, 1, keepdims=True)
        old = (old / denominator).astype(jnp.bfloat16)
        new = (new / denominator).astype(jnp.bfloat16)
        for i in range(GROUP):
            r = g * GROUP + i
            v = cache[1, pl.ds(first + i * MIGPG, MIGPG)].reshape(MIGLEN, HD)
            o = dot_nn(old[i * ROWS:(i + 1) * ROWS], v)
            o = o + dot_nn(new[i * ROWS:(i + 1) * ROWS], values[LONG + r])
            o = o.astype(jnp.bfloat16)
            at = place[r]

            @pl.when(at < 0)
            def _():
                stay[LONG + r] = o

            @pl.when(at >= 0)
            def _():
                stay[LONG + r] = jnp.zeros_like(o)
                row = pl.multiple_of(at % CAP * 32, 32)
                side[at // CAP, pl.ds(row, ROWS)] = o
                side[at // CAP, pl.ds(pl.multiple_of(row + ROWS, 16), 16)] = keys_values[LONG + r]

        return carry

    lax.fori_loop(0, SHORT // GROUP, short_group, 0)

    side_copy = pltpu.make_async_copy(side, out.at[:, pl.ds(0, B_DUP)], side_sem)
    side_copy.start()

    for j in range(LONG):
        q = query[j]
        new = fresh_scores(q, j)
        length = longs[0, j]

        def scores(i, top, j=j, q=q, length=length):
            first = pl.multiple_of(j * MAXPG + i * per, per)
            wait_pages(first, per, long_sems.at[j, i])
            s = dot_nt(q, cache[0, pl.ds(first, per)].reshape(CHUNK, HD)) * SCALE
            pos = lax.broadcasted_iota(jnp.int32, s.shape, 1) + i * CHUNK
            s = jnp.where(pos < length, s, -1e30)
            score[j, i] = s
            return jnp.maximum(top, jnp.max(s, 1, keepdims=True))

        top = lax.fori_loop(0, chunks[j], scores, jnp.max(new, 1, keepdims=True))
        new = jnp.exp(new - top)

        def exponents(i, denominator, j=j, top=top):
            e = jnp.exp(score[j, i] - top)
            score[j, i] = e
            return denominator + jnp.sum(e, 1, keepdims=True)

        denominator = lax.fori_loop(0, chunks[j], exponents, jnp.sum(new, 1, keepdims=True))
        inverse = 1.0 / denominator

        def blend(i, o, j=j, inverse=inverse):
            first = pl.multiple_of(j * MAXPG + i * per, per)
            v = cache[1, pl.ds(first, per)].reshape(CHUNK, HD)
            return o + dot_nn((score[j, i] * inverse).astype(jnp.bfloat16), v)

        o = dot_nn((new * inverse).astype(jnp.bfloat16), values[j])
        stay[j] = lax.fori_loop(0, chunks[j], blend, o).astype(jnp.bfloat16)
    side_copy.wait()


def attend(tables, query, keys_values, values, pool):
    return pl.pallas_call(
        attend_kernel,
        out_shape=(
            jax.ShapeDtypeStruct((REQS, ROWS, HD), jnp.bfloat16),
            jax.ShapeDtypeStruct((INST, B_ROWS, HD), jnp.bfloat16),
        ),
        in_specs=[spec(SMEM)] * 5 + [spec(VMEM)] * 3 + [spec(pl.ANY)],
        out_specs=(spec(VMEM), spec(pltpu.HBM)),
        scratch_shapes=[
            pltpu.SMEM((INST,), jnp.int32),
            pltpu.SMEM((SHORT,), jnp.int32),
            pltpu.VMEM((2, PAGES, PAGE, HD), jnp.bfloat16),
            pltpu.VMEM((LONG, MAXPG * PAGE // CHUNK, ROWS, CHUNK), jnp.float32),
            pltpu.VMEM((INST, B_DUP, HD), jnp.bfloat16),
            pltpu.SemaphoreType.DMA((SHORT // GROUP,)),
            pltpu.SemaphoreType.DMA((LONG, MAXPG * PAGE // CHUNK)),
            pltpu.SemaphoreType.DMA(()),
        ],
        compiler_params=pltpu.CompilerParams(vmem_limit_bytes=24 << 20),
        cost_estimate=pl.CostEstimate(
            flops=4 * 26624 * 16 * 128, bytes_accessed=14 << 20, transcendentals=26624 * 16
        ),
        name="attend_all",
    )(*tables, query, keys_values, values, pool)


def join_kernel(here, blocks, out):
    me = here[0]
    width = blocks.shape[2]
    for k in range(8):
        x = (me // 2 + 4 - k % 4) % 4
        y = (me + k // 4) % 2
        at = pl.multiple_of((x * 2 + y) * width, width)
        out[:, pl.ds(at, width)] = blocks[k]


def join(here, blocks):
    _, rows, width = blocks.shape
    return pl.pallas_call(
        join_kernel,
        out_shape=jax.ShapeDtypeStruct((rows, width * 8), jnp.bfloat16),
        in_specs=[spec(SMEM), spec(VMEM)],
        out_specs=spec(VMEM),
        name="join_hidden",
    )(here, blocks)


def route_kernel(received, _, out, small, count, slots, sem, out_sems):
    copy = pltpu.make_async_copy(received.at[:, pl.ds(A_DUP, A_ROWS - A_DUP)], small, sem)
    copy.start()
    clear(count)
    copy.wait()
    lane = lax.broadcasted_iota(jnp.int32, (16, 128), 1)
    targets = []
    for s in range(INST):
        tables = small[s, pl.ds(2 * PIECE, 16)].astype(jnp.float32)
        targets.append(jnp.max(jnp.where(lane == 67, tables, 0.0)).astype(jnp.int32) - 1)

    def forward(s, to, slot):
        row = pl.multiple_of(B_DUP + slot * 2 * PIECE, 2 * PIECE)
        return pltpu.make_async_copy(
            small.at[s, pl.ds(0, 2 * PIECE)], out.at[to, pl.ds(row, 2 * PIECE)], out_sems.at[s]
        )

    for s, to in enumerate(targets):
        slots[s] = DUPS

        @pl.when(to >= 0)
        def _():
            slots[s] = take_slot(count, to)

        @pl.when((to >= 0) & (slots[s] < DUPS))
        def _():
            forward(s, to, slots[s]).start()

    for s, to in enumerate(targets):
        @pl.when((to >= 0) & (slots[s] < DUPS))
        def _():
            forward(s, to, slots[s]).wait()


def route(received, second):
    return pl.pallas_call(
        route_kernel,
        out_shape=jax.ShapeDtypeStruct((INST, B_ROWS, HD), jnp.bfloat16),
        in_specs=[spec(pl.ANY), spec(pltpu.HBM)],
        out_specs=spec(pltpu.HBM),
        scratch_shapes=[
            pltpu.VMEM((INST, A_ROWS - A_DUP, HD), jnp.bfloat16),
            pltpu.SMEM((INST,), jnp.int32),
            pltpu.SMEM((INST,), jnp.int32),
            pltpu.SemaphoreType.DMA(()),
            pltpu.SemaphoreType.DMA((INST,)),
        ],
        input_output_aliases={1: 0},
        cost_estimate=pl.CostEstimate(flops=0, bytes_accessed=1 << 20, transcendentals=0),
        name="route_pieces",
    )(received, second)


def decode_kernel(here, longs, shorts, order, received, lens, load, small, sem):
    copy = pltpu.make_async_copy(received.at[:, pl.ds(A_META, 16)], small, sem)
    copy.start()
    resident = jnp.int32(STEPS * (LONG + SHORT - MIG))
    for i in range(LONG):
        resident = resident + longs[0, i]
    for i in range(MIG, SHORT):
        resident = resident + shorts[0, order[0, i]]
    copy.wait()

    def total(x, axis=None):
        return jnp.sum(x, axis=axis, keepdims=True)

    x = jnp.max(small[...].astype(jnp.float32), axis=1)
    lane = lax.broadcasted_iota(jnp.int32, x.shape, 1)
    table = jnp.where(lane < INST * CAP, x + 256.0 * pltpu.roll(x, 96, 1), 0.0)
    own = resident.astype(jnp.float32)
    result = jnp.zeros_like(x)
    for slot in range(CAP):
        length = total(jnp.where(lane == here[0] * CAP + slot, table, 0.0), 1)
        result = jnp.where(lane == slot, length, result)
        own = own + total(jnp.where(length > 0.0, length + STEPS, 0.0))
    lens[...] = result.astype(jnp.int32)
    digits = jnp.where(lane == 64, 1.0, jnp.where(lane == 65, 128.0, jnp.where(lane == 66, 16384.0, 0.0)))
    share = own * INST / total(x * digits)
    double = jnp.where((table > 0.0) & (lane % 2 == 1), 1.0, 0.0)
    sends = jnp.max(total(double, 1), keepdims=True)
    takes = jnp.max(total(double, 0), keepdims=True)
    over = jnp.where((sends > 1.0) | (takes > DUPS), 1.0, 0.0)
    row = lax.broadcasted_iota(jnp.int32, (8, 128), 0)
    load[...] = jnp.where(row == 0, share, over)


def decode(here, longs, shorts, order, received):
    return pl.pallas_call(
        decode_kernel,
        out_shape=(
            jax.ShapeDtypeStruct((INST, 128), jnp.int32),
            jax.ShapeDtypeStruct((8, 128), jnp.float32),
        ),
        in_specs=[spec(SMEM)] * 4 + [spec(pl.ANY)],
        out_specs=(spec(VMEM), spec(VMEM)),
        scratch_shapes=[
            pltpu.VMEM((INST, 16, HD), jnp.bfloat16),
            pltpu.SemaphoreType.DMA(()),
        ],
        name="decode_tables",
    )(here, longs, shorts, order, received)


def window_base(length):
    return pl.multiple_of(jnp.minimum(length // 16 * 16, MIGLEN - 32), 16)


def masked_page(read, write, length, fresh, p):
    grown = length + STEPS if fresh is not None else length
    whole = length >= (p + 1) * PAGE
    empty = grown <= p * PAGE

    @pl.when(whole)
    def _():
        for c in range(2):
            write(p, c, read(p, c))

    @pl.when(empty)
    def _():
        for c in range(2):
            write(p, c, jnp.zeros((PAGE, HD), jnp.bfloat16))

    @pl.when(jnp.logical_not(whole | empty))
    def _():
        at = lax.broadcasted_iota(jnp.int32, (PAGE, HD), 0) + p * PAGE
        for c in range(2):
            x = jnp.where(at < length, read(p, c).astype(jnp.float32), 0.0)
            if fresh is not None:
                rows = fresh().astype(jnp.float32)
                for t in range(STEPS):
                    x = jnp.where(at == length + t, rows[c * 2 + t:c * 2 + t + 1], x)
            write(p, c, x.astype(jnp.bfloat16))


def place_kernel(lens, block, cache, window):
    s = pl.program_id(0)
    length = lens[s, 0]

    def read(p, c):
        return block[0, pl.ds((p * 2 + c) * PAGE, PAGE)]

    def write(p, c, x):
        cache[0, c, pl.ds(p * PAGE, PAGE)] = x

    for p in range(MIGPG):
        masked_page(read, write, length, None, p)
    cache[1] = jnp.zeros((2, MIGLEN, HD), jnp.bfloat16)
    base = window_base(length)
    for c in range(2):
        window[0, c] = cache[0, c, pl.ds(base, 32)]


def place_first(lens, received):
    return pl.pallas_call(
        place_kernel,
        out_shape=(
            jax.ShapeDtypeStruct((INST * CAP, 2, MIGLEN, HD), jnp.bfloat16),
            jax.ShapeDtypeStruct((INST, 2, 32, HD), jnp.bfloat16),
        ),
        grid_spec=pltpu.PrefetchScalarGridSpec(
            num_scalar_prefetch=1,
            grid=(INST,),
            in_specs=[pl.BlockSpec((1, 2 * MIGLEN, HD), lambda s, _: (s, 0, 0))],
            out_specs=[
                pl.BlockSpec((CAP, 2, MIGLEN, HD), lambda s, _: (s, 0, 0, 0)),
                pl.BlockSpec((1, 2, 32, HD), lambda s, _: (s, 0, 0, 0)),
            ],
        ),
        compiler_params=pltpu.CompilerParams(vmem_limit_bytes=8 << 20),
        cost_estimate=pl.CostEstimate(flops=0, bytes_accessed=13 << 20, transcendentals=0),
        name="place_first",
    )(lens, received)


def settle_kernel(full, lens, window, second, extra, _, cache, out, patched, dups, sems, dup_sems):
    at = lax.broadcasted_iota(jnp.int32, (32, HD), 0)

    def patch_copy(s, c):
        return pltpu.make_async_copy(
            patched.at[s, c],
            cache.at[s * CAP, c, pl.ds(window_base(lens[s, 0]), 32)],
            sems.at[s * 2 + c],
        )

    def dup_copy(s):
        return pltpu.make_async_copy(dups.at[s], cache.at[s * CAP + 1], dup_sems.at[s])

    for s in range(INST):
        length = lens[s, 0]

        @pl.when(length > 0)
        def _():
            fresh = second[s, pl.ds(ROWS, 16)].astype(jnp.float32)
            where = at + window_base(length)
            for c in range(2):
                x = window[s, c].astype(jnp.float32)
                for t in range(STEPS):
                    x = jnp.where(where == length + t, fresh[c * 2 + t:c * 2 + t + 1], x)
                patched[s, c] = x.astype(jnp.bfloat16)
                patch_copy(s, c).start()

    order = jnp.int32(0)
    for s in range(INST):
        length = lens[s, 1]
        rank = jnp.minimum(order, DUPS - 1)
        order = order + (length > 0).astype(jnp.int32)

        @pl.when(length > 0)
        def _():
            def read(p, c):
                if full:
                    return extra[s, pl.ds((p * 2 + c) * PAGE, PAGE)]
                row = pl.multiple_of(B_DUP + rank * 2 * PIECE + c * PIECE, PIECE)
                return jnp.concatenate(
                    [second[p * MIGPG + i, pl.ds(row, PIECE)] for i in range(MIGPG)], axis=0
                )

            def write(p, c, x):
                dups[s, c, pl.ds(p * PAGE, PAGE)] = x

            for p in range(MIGPG):
                masked_page(read, write, length, lambda: second[s, pl.ds(32 + ROWS, 16)], p)
            dup_copy(s).start()

    for s in range(INST):
        for slot in range(CAP):
            filled = lens[s, slot] > 0
            rows = second[s, pl.ds(slot * 32, ROWS)]
            out[s * CAP + slot] = jnp.where(filled, rows, jnp.zeros_like(rows))
    for s in range(INST):
        @pl.when(lens[s, 0] > 0)
        def _():
            for c in range(2):
                patch_copy(s, c).wait()

        @pl.when(lens[s, 1] > 0)
        def _():
            dup_copy(s).wait()


def settle_all(full, lens, window, second, extra, cache):
    def kernel(*refs):
        settle_kernel(full, *refs)

    return pl.pallas_call(
        kernel,
        out_shape=(
            jax.ShapeDtypeStruct(cache.shape, jnp.bfloat16),
            jax.ShapeDtypeStruct((INST * CAP, ROWS, HD), jnp.bfloat16),
        ),
        in_specs=[spec(SMEM)] + [spec(VMEM)] * 3 + [spec(pl.ANY)],
        out_specs=(spec(pl.ANY), spec(VMEM)),
        scratch_shapes=[
            pltpu.VMEM((INST, 2, 32, HD), jnp.bfloat16),
            pltpu.VMEM((INST, 2, MIGLEN, HD), jnp.bfloat16),
            pltpu.SemaphoreType.DMA((INST * 2,)),
            pltpu.SemaphoreType.DMA((INST,)),
        ],
        input_output_aliases={4: 0},
        compiler_params=pltpu.CompilerParams(vmem_limit_bytes=20 << 20),
        name="settle_full" if full else "settle_short",
    )(lens, window, second, extra, cache)


def on_device(
    queries,
    hidden_in,
    kv_weight,
    kv_pool,
    page_table,
    long_lengths,
    short_lengths,
    mig_order,
    destination,
):
    inst_index = lax.axis_index("inst")
    tp_index = lax.axis_index("tp")
    targets = destination.reshape(1, MIG)
    tables = (page_table, long_lengths, short_lengths, mig_order, targets)
    pages = kv_pool.reshape(PAGES, 2 * PAGE, HD)

    def from_x(value, k):
        return lax.ppermute(value, "tp", [(i, (i // 2 + k) % 4 * 2 + i % 2) for i in range(8)])

    def from_y(value):
        return lax.ppermute(value, "tp", [(i, i ^ 1) for i in range(8)])

    near = [hidden_in, from_x(hidden_in, 1), from_x(hidden_in, 2), from_x(hidden_in, 3)]
    far = [from_y(hidden_in)]
    far += [from_x(far[0], 1), from_y(near[2]), from_x(far[0], 3)]
    first = build(tables, pages)
    first, *blocks = lax.optimization_barrier((first, *near[1:], *far))
    blocks = jnp.stack([hidden_in, *blocks]).reshape(8, REQS * STEPS, -1)
    got_first = lax.all_to_all(first, "inst", split_axis=0, concat_axis=0, tiled=True)

    hidden_all = join(tp_index.reshape(1), blocks)
    fresh = jnp.einsum(
        "rd,dcn->rcn", hidden_all, kv_weight, preferred_element_type=jnp.float32
    ).astype(jnp.bfloat16)
    fresh = fresh.reshape(REQS, STEPS, 2, HD)
    values = jnp.pad(fresh[:, :, 1], ((0, 0), (0, 16 - STEPS), (0, 0)))
    keys_values = jnp.pad(
        fresh.transpose(0, 2, 1, 3).reshape(REQS, 2 * STEPS, HD),
        ((0, 0), (0, 16 - 2 * STEPS), (0, 0)),
    )
    stay, second = attend(
        tables, queries.reshape(REQS, ROWS, HD), keys_values, values, kv_pool
    )
    stay_out = stay.reshape(REQS, STEPS, KV_HEADS * HD)
    second = route(got_first, second)
    got_second = lax.all_to_all(second, "inst", split_axis=0, concat_axis=0, tiled=True)

    arriving, load = decode(
        inst_index.reshape(1), long_lengths, short_lengths, mig_order, got_first
    )
    load_share = load[0, :1]
    overflow = load[1, 0] > 0.5

    cache, window = place_first(arriving, got_first)

    def short_path(args):
        lens, window, second, cache = args
        return tuple(settle_all(False, lens, window, second, window, cache))

    def long_path(args):
        lens, window, second, cache = args
        send = build_second(page_table, mig_order, targets, pages)
        got = lax.all_to_all(send, "inst", split_axis=0, concat_axis=0, tiled=True)
        return tuple(settle_all(True, lens, window, second, got, cache))

    moved_cache, moved = lax.cond(
        overflow, long_path, short_path, (arriving, window, got_second, cache)
    )
    moved_out = moved.reshape(INST * CAP, STEPS, KV_HEADS * HD)
    return (stay_out, moved_out, moved_cache, load_share)


def solution(mesh):
    placed = (
        P("inst", None, "tp"),
        P("inst", None, "tp"),
        P(None, None, "tp"),
        P("inst", None, None, "tp"),
        P("inst", None),
        P("inst", None),
        P("inst", None),
        P("inst", None),
        P("inst", None),
    )
    return jax.shard_map(
        on_device,
        mesh=mesh,
        in_specs=placed,
        out_specs=(
            P("inst", None, "tp"),
            P("inst", None, "tp"),
            P("inst", None, None, "tp"),
            P("inst"),
        ),
        check_vma=False,
    )
```

```python
import math

import jax
import jax.numpy as jnp
from jax import lax
from jax.experimental import pallas as pl
from jax.experimental.pallas import tpu as pltpu
from jax.sharding import PartitionSpec as P

HEADS = 64
KV_HEADS = 8
HD = 128
PAGE = 128
MAXPG = 64
MIGPG = 4
LONG = 2
MIG = 16
CAP = 2
STEPS = 2
SHORT = 20
REQS = 22
MIGLEN = 512
INST = 16
PAGES = 208
ROWS = 16
DUPS = 4
PIECE = MIGLEN // INST

A_DUP = 2 * MIGLEN
A_META = A_DUP + 2 * PIECE
A_ROWS = A_META + 16
B_DUP = 64
B_ROWS = B_DUP + DUPS * 2 * PIECE

SMEM = pltpu.SMEM
VMEM = pltpu.VMEM


def spec(space):
    return pl.BlockSpec(memory_space=space)


def clear(count):
    for i in range(INST):
        count[i] = 0


def take_slot(count, to):
    slot = count[to]
    count[to] = slot + 1
    return slot


def build_kernel(
    table, longs, shorts, order, dest, pool, out, count, slots, held, extra, stage, sems, extra_sem, out_sems, stage_sem
):
    def load(page, k, p):
        return pltpu.make_async_copy(
            pool.at[page], held.at[k, pl.ds(p * 2 * PAGE, 2 * PAGE)], sems.at[k]
        )

    def send(k):
        return pltpu.make_async_copy(
            held.at[k], out.at[dest[0, k], pl.ds(0, 2 * MIGLEN)], out_sems.at[k]
        )

    clear(count)

    def begin(k, dup_at):
        slot = take_slot(count, dest[0, k])
        slots[k] = slot
        first = LONG * MAXPG + order[0, k] * MIGPG

        @pl.when(slot == 0)
        def _():
            for p in range(MIGPG):
                load(table[0, first + p], k, p).start()

        second = (slot == 1) & (dup_at < 0)

        @pl.when(second)
        def _():
            for p in range(MIGPG):
                pltpu.make_async_copy(pool.at[table[0, first + p]], extra.at[p], extra_sem).start()

        return jnp.where(second, k, dup_at)

    dup_at = lax.fori_loop(0, MIG, begin, jnp.int32(-1))
    lane = lax.broadcasted_iota(jnp.int32, (16, 128), 1)
    total = jnp.int32(STEPS * REQS)
    for i in range(LONG):
        total = total + longs[0, i]
    for i in range(SHORT):
        total = total + shorts[0, i]
    dup_to = jnp.where(dup_at >= 0, dest[0, jnp.maximum(dup_at, 0)] + 1, 0)
    row = jnp.zeros((16, 128), jnp.int32)
    for at, value in ((64, total & 127), (65, (total >> 7) & 127), (66, total >> 14), (67, dup_to)):
        row = jnp.where(lane == at, value, row)
    for k in range(MIG):
        at = dest[0, k] * CAP + slots[k]
        length = shorts[0, order[0, k]]
        row = jnp.where(lane == at, length & 255, row)
        row = jnp.where(lane == at + 32, length >> 8, row)
    tables = row.astype(jnp.float32).astype(jnp.bfloat16)
    for m in range(INST):
        stage[m, pl.ds(2 * PIECE, 16)] = tables

    def each(k, carry):
        @pl.when(slots[k] == 0)
        def _():
            pltpu.make_async_copy(held.at[k], held.at[k], sems.at[k]).wait()
            send(k).start()

        return carry

    lax.fori_loop(0, MIG, each, 0)

    @pl.when(dup_at >= 0)
    def _():
        pltpu.make_async_copy(extra, extra, extra_sem).wait()
        for m in range(INST):
            for c in range(2):
                stage[m, pl.ds(c * PIECE, PIECE)] = extra[
                    m // MIGPG, pl.ds(c * PAGE + m % MIGPG * PIECE, PIECE)
                ]

    last = pltpu.make_async_copy(stage, out.at[:, pl.ds(A_DUP, A_ROWS - A_DUP)], stage_sem)
    last.start()

    def finish(k, carry):
        @pl.when(slots[k] == 0)
        def _():
            send(k).wait()

        return carry

    lax.fori_loop(0, MIG, finish, 0)
    last.wait()


def build(tables, pool):
    return pl.pallas_call(
        build_kernel,
        out_shape=jax.ShapeDtypeStruct((INST, A_ROWS, HD), jnp.bfloat16),
        in_specs=[spec(SMEM)] * 5 + [spec(pl.ANY)],
        out_specs=spec(pltpu.HBM),
        scratch_shapes=[
            pltpu.SMEM((INST,), jnp.int32),
            pltpu.SMEM((MIG,), jnp.int32),
            pltpu.VMEM((MIG, 2 * MIGLEN, HD), jnp.bfloat16),
            pltpu.VMEM((MIGPG, 2 * PAGE, HD), jnp.bfloat16),
            pltpu.VMEM((INST, A_ROWS - A_DUP, HD), jnp.bfloat16),
            pltpu.SemaphoreType.DMA((MIG,)),
            pltpu.SemaphoreType.DMA(()),
            pltpu.SemaphoreType.DMA((MIG,)),
            pltpu.SemaphoreType.DMA(()),
        ],
        compiler_params=pltpu.CompilerParams(vmem_limit_bytes=60 << 20),
        cost_estimate=pl.CostEstimate(flops=0, bytes_accessed=9 << 20, transcendentals=0),
        name="build_first",
    )(*tables, pool)


def second_kernel(table, order, dest, pool, out, count, held, sems, out_sems):
    def load(k, p):
        page = table[0, LONG * MAXPG + order[0, k] * MIGPG + p]
        return pltpu.make_async_copy(
            pool.at[page], held.at[dest[0, k], pl.ds(p * 2 * PAGE, 2 * PAGE)], sems.at[k * MIGPG + p]
        )

    def send(k):
        to = dest[0, k]
        return pltpu.make_async_copy(held.at[to], out.at[to], out_sems.at[k])

    for stage in range(3):
        clear(count)

        def each(k, carry):
            slot = take_slot(count, dest[0, k])

            @pl.when(slot == 1)
            def _():
                if stage == 0:
                    for p in range(MIGPG):
                        load(k, p).start()
                elif stage == 1:
                    for p in range(MIGPG):
                        load(k, p).wait()
                    send(k).start()
                else:
                    send(k).wait()

            return carry

        lax.fori_loop(0, MIG, each, 0)


def build_second(table, order, dest, pool):
    return pl.pallas_call(
        second_kernel,
        out_shape=jax.ShapeDtypeStruct((INST, 2 * MIGLEN, HD), jnp.bfloat16),
        in_specs=[spec(SMEM)] * 3 + [spec(pl.ANY)],
        out_specs=spec(pl.ANY),
        scratch_shapes=[
            pltpu.SMEM((INST,), jnp.int32),
            pltpu.VMEM((INST, 2 * MIGLEN, HD), jnp.bfloat16),
            pltpu.SemaphoreType.DMA((MIG * MIGPG,)),
            pltpu.SemaphoreType.DMA((MIG,)),
        ],
        compiler_params=pltpu.CompilerParams(vmem_limit_bytes=12 << 20),
        name="build_second",
    )(table, order, dest, pool)


def dot_nt(a, b):
    return lax.dot_general(a, b, (((1,), (1,)), ((), ())), preferred_element_type=jnp.float32)


def dot_nn(a, b):
    return lax.dot_general(a, b, (((1,), (0,)), ((), ())), preferred_element_type=jnp.float32)


GROUP = 4
CHUNK = 1024
SCALE = 1.0 / math.sqrt(HD)


def attend_kernel(
    table, longs, shorts, order, dest, query, keys_values, values, pool, stay, out,
    count, place, cache, score, side, page_sems, long_sems, side_sem,
):
    def load(pg, sem):
        return pltpu.make_async_copy(pool.at[table[0, pg]], cache.at[:, pg], sem)

    def wait_pages(first, size, sem):
        pltpu.make_async_copy(
            cache.at[:, pl.ds(first, size)], cache.at[:, pl.ds(first, size)], sem
        ).wait()

    for r in range(SHORT // GROUP):
        def start_short(i, carry, r=r):
            load(LONG * MAXPG + r * GROUP * MIGPG + i, page_sems.at[r]).start()
            return carry

        lax.fori_loop(0, GROUP * MIGPG, start_short, 0)
    per = CHUNK // PAGE
    chunks = [(longs[0, j] + CHUNK - 1) // CHUNK for j in range(LONG)]
    for j in range(LONG):
        def start_long(i, carry, j=j):
            for p in range(per):
                load(j * MAXPG + i * per + p, long_sems.at[j, i]).start()
            return carry

        lax.fori_loop(0, chunks[j], start_long, 0)

    clear(count)
    for i in range(SHORT):
        place[i] = -1

    def settle(k, carry):
        to = dest[0, k]
        place[order[0, k]] = to * CAP + take_slot(count, to)
        return carry

    lax.fori_loop(0, MIG, settle, 0)

    def fresh_scores(q, r):
        s = dot_nt(q, keys_values[r]) * SCALE
        step = lax.broadcasted_iota(jnp.int32, s.shape, 0) // 8
        col = lax.broadcasted_iota(jnp.int32, s.shape, 1)
        return jnp.where((col <= step) & (col < STEPS), s, -1e30)

    def short_group(g, carry):
        first = pl.multiple_of(LONG * MAXPG + g * GROUP * MIGPG, GROUP * MIGPG)
        wait_pages(first, GROUP * MIGPG, page_sems.at[g])
        pos = lax.broadcasted_iota(jnp.int32, (ROWS, MIGLEN), 1)
        old, new = [], []
        for i in range(GROUP):
            r = g * GROUP + i
            q = query[LONG + r]
            k = cache[0, pl.ds(first + i * MIGPG, MIGPG)].reshape(MIGLEN, HD)
            s = dot_nt(q, k) * SCALE
            old.append(jnp.where(pos < shorts[0, r], s, -1e30))
            new.append(fresh_scores(q, LONG + r))
        old = jnp.concatenate(old, axis=0)
        new = jnp.concatenate(new, axis=0)
        peak = jnp.maximum(jnp.max(old, 1, keepdims=True), jnp.max(new, 1, keepdims=True))
        old = jnp.exp(old - peak)
        new = jnp.exp(new - peak)
        denominator = jnp.sum(old, 1, keepdims=True) + jnp.sum(new, 1, keepdims=True)
        old = (old / denominator).astype(jnp.bfloat16)
        new = (new / denominator).astype(jnp.bfloat16)
        for i in range(GROUP):
            r = g * GROUP + i
            v = cache[1, pl.ds(first + i * MIGPG, MIGPG)].reshape(MIGLEN, HD)
            o = dot_nn(old[i * ROWS:(i + 1) * ROWS], v)
            o = o + dot_nn(new[i * ROWS:(i + 1) * ROWS], values[LONG + r])
            o = o.astype(jnp.bfloat16)
            at = place[r]

            @pl.when(at < 0)
            def _():
                stay[LONG + r] = o

            @pl.when(at >= 0)
            def _():
                stay[LONG + r] = jnp.zeros_like(o)
                row = pl.multiple_of(at % CAP * 32, 32)
                side[at // CAP, pl.ds(row, ROWS)] = o
                side[at // CAP, pl.ds(pl.multiple_of(row + ROWS, 16), 16)] = keys_values[LONG + r]

        return carry

    lax.fori_loop(0, SHORT // GROUP, short_group, 0)

    side_copy = pltpu.make_async_copy(side, out.at[:, pl.ds(0, B_DUP)], side_sem)
    side_copy.start()

    for j in range(LONG):
        q = query[j]
        new = fresh_scores(q, j)
        length = longs[0, j]

        def scores(i, top, j=j, q=q, length=length):
            first = pl.multiple_of(j * MAXPG + i * per, per)
            wait_pages(first, per, long_sems.at[j, i])
            s = dot_nt(q, cache[0, pl.ds(first, per)].reshape(CHUNK, HD)) * SCALE
            pos = lax.broadcasted_iota(jnp.int32, s.shape, 1) + i * CHUNK
            s = jnp.where(pos < length, s, -1e30)
            score[j, i] = s
            return jnp.maximum(top, jnp.max(s, 1, keepdims=True))

        top = lax.fori_loop(0, chunks[j], scores, jnp.max(new, 1, keepdims=True))
        new = jnp.exp(new - top)

        def exponents(i, denominator, j=j, top=top):
            e = jnp.exp(score[j, i] - top)
            score[j, i] = e
            return denominator + jnp.sum(e, 1, keepdims=True)

        denominator = lax.fori_loop(0, chunks[j], exponents, jnp.sum(new, 1, keepdims=True))
        inverse = 1.0 / denominator

        def blend(i, o, j=j, inverse=inverse):
            first = pl.multiple_of(j * MAXPG + i * per, per)
            v = cache[1, pl.ds(first, per)].reshape(CHUNK, HD)
            return o + dot_nn((score[j, i] * inverse).astype(jnp.bfloat16), v)

        o = dot_nn((new * inverse).astype(jnp.bfloat16), values[j])
        stay[j] = lax.fori_loop(0, chunks[j], blend, o).astype(jnp.bfloat16)
    side_copy.wait()


def attend(tables, query, keys_values, values, pool):
    return pl.pallas_call(
        attend_kernel,
        out_shape=(
            jax.ShapeDtypeStruct((REQS, ROWS, HD), jnp.bfloat16),
            jax.ShapeDtypeStruct((INST, B_ROWS, HD), jnp.bfloat16),
        ),
        in_specs=[spec(SMEM)] * 5 + [spec(VMEM)] * 3 + [spec(pl.ANY)],
        out_specs=(spec(VMEM), spec(pltpu.HBM)),
        scratch_shapes=[
            pltpu.SMEM((INST,), jnp.int32),
            pltpu.SMEM((SHORT,), jnp.int32),
            pltpu.VMEM((2, PAGES, PAGE, HD), jnp.bfloat16),
            pltpu.VMEM((LONG, MAXPG * PAGE // CHUNK, ROWS, CHUNK), jnp.float32),
            pltpu.VMEM((INST, B_DUP, HD), jnp.bfloat16),
            pltpu.SemaphoreType.DMA((SHORT // GROUP,)),
            pltpu.SemaphoreType.DMA((LONG, MAXPG * PAGE // CHUNK)),
            pltpu.SemaphoreType.DMA(()),
        ],
        compiler_params=pltpu.CompilerParams(vmem_limit_bytes=24 << 20),
        cost_estimate=pl.CostEstimate(
            flops=4 * 26624 * 16 * 128, bytes_accessed=14 << 20, transcendentals=26624 * 16
        ),
        name="attend_all",
    )(*tables, query, keys_values, values, pool)


def join_kernel(here, blocks, out):
    me = here[0]
    width = blocks.shape[2]
    for k in range(8):
        x = (me // 2 + 4 - k // 2) % 4
        y = (me + k % 2) % 2
        at = pl.multiple_of((x * 2 + y) * width, width)
        out[:, pl.ds(at, width)] = blocks[k]


def join(here, blocks):
    _, rows, width = blocks.shape
    return pl.pallas_call(
        join_kernel,
        out_shape=jax.ShapeDtypeStruct((rows, width * 8), jnp.bfloat16),
        in_specs=[spec(SMEM), spec(VMEM)],
        out_specs=spec(VMEM),
        name="join_hidden",
    )(here, blocks)


def route_kernel(received, _, out, small, count, slots, sem, out_sems):
    copy = pltpu.make_async_copy(received.at[:, pl.ds(A_DUP, A_ROWS - A_DUP)], small, sem)
    copy.start()
    clear(count)
    copy.wait()
    lane = lax.broadcasted_iota(jnp.int32, (16, 128), 1)
    targets = []
    for s in range(INST):
        tables = small[s, pl.ds(2 * PIECE, 16)].astype(jnp.float32)
        targets.append(jnp.max(jnp.where(lane == 67, tables, 0.0)).astype(jnp.int32) - 1)

    def forward(s, to, slot):
        row = pl.multiple_of(B_DUP + slot * 2 * PIECE, 2 * PIECE)
        return pltpu.make_async_copy(
            small.at[s, pl.ds(0, 2 * PIECE)], out.at[to, pl.ds(row, 2 * PIECE)], out_sems.at[s]
        )

    for s, to in enumerate(targets):
        slots[s] = DUPS

        @pl.when(to >= 0)
        def _():
            slots[s] = take_slot(count, to)

        @pl.when((to >= 0) & (slots[s] < DUPS))
        def _():
            forward(s, to, slots[s]).start()

    for s, to in enumerate(targets):
        @pl.when((to >= 0) & (slots[s] < DUPS))
        def _():
            forward(s, to, slots[s]).wait()


def route(received, second):
    return pl.pallas_call(
        route_kernel,
        out_shape=jax.ShapeDtypeStruct((INST, B_ROWS, HD), jnp.bfloat16),
        in_specs=[spec(pl.ANY), spec(pltpu.HBM)],
        out_specs=spec(pltpu.HBM),
        scratch_shapes=[
            pltpu.VMEM((INST, A_ROWS - A_DUP, HD), jnp.bfloat16),
            pltpu.SMEM((INST,), jnp.int32),
            pltpu.SMEM((INST,), jnp.int32),
            pltpu.SemaphoreType.DMA(()),
            pltpu.SemaphoreType.DMA((INST,)),
        ],
        input_output_aliases={1: 0},
        cost_estimate=pl.CostEstimate(flops=0, bytes_accessed=1 << 20, transcendentals=0),
        name="route_pieces",
    )(received, second)


def decode_kernel(here, longs, shorts, order, received, lens, load, small, sem):
    copy = pltpu.make_async_copy(received.at[:, pl.ds(A_META, 16)], small, sem)
    copy.start()
    resident = jnp.int32(STEPS * (LONG + SHORT - MIG))
    for i in range(LONG):
        resident = resident + longs[0, i]
    for i in range(MIG, SHORT):
        resident = resident + shorts[0, order[0, i]]
    copy.wait()

    def total(x, axis=None):
        return jnp.sum(x, axis=axis, keepdims=True)

    x = jnp.max(small[...].astype(jnp.float32), axis=1)
    lane = lax.broadcasted_iota(jnp.int32, x.shape, 1)
    table = jnp.where(lane < INST * CAP, x + 256.0 * pltpu.roll(x, 96, 1), 0.0)
    own = resident.astype(jnp.float32)
    result = jnp.zeros_like(x)
    for slot in range(CAP):
        length = total(jnp.where(lane == here[0] * CAP + slot, table, 0.0), 1)
        result = jnp.where(lane == slot, length, result)
        own = own + total(jnp.where(length > 0.0, length + STEPS, 0.0))
    lens[...] = result.astype(jnp.int32)
    digits = jnp.where(lane == 64, 1.0, jnp.where(lane == 65, 128.0, jnp.where(lane == 66, 16384.0, 0.0)))
    share = own * INST / total(x * digits)
    double = jnp.where((table > 0.0) & (lane % 2 == 1), 1.0, 0.0)
    sends = jnp.max(total(double, 1), keepdims=True)
    takes = jnp.max(total(double, 0), keepdims=True)
    over = jnp.where((sends > 1.0) | (takes > DUPS), 1.0, 0.0)
    row = lax.broadcasted_iota(jnp.int32, (8, 128), 0)
    load[...] = jnp.where(row == 0, share, over)


def decode(here, longs, shorts, order, received):
    return pl.pallas_call(
        decode_kernel,
        out_shape=(
            jax.ShapeDtypeStruct((INST, 128), jnp.int32),
            jax.ShapeDtypeStruct((8, 128), jnp.float32),
        ),
        in_specs=[spec(SMEM)] * 4 + [spec(pl.ANY)],
        out_specs=(spec(VMEM), spec(VMEM)),
        scratch_shapes=[
            pltpu.VMEM((INST, 16, HD), jnp.bfloat16),
            pltpu.SemaphoreType.DMA(()),
        ],
        name="decode_tables",
    )(here, longs, shorts, order, received)


def window_base(length):
    return pl.multiple_of(jnp.minimum(length // 16 * 16, MIGLEN - 32), 16)


def masked_page(read, write, length, fresh, p):
    grown = length + STEPS if fresh is not None else length
    whole = length >= (p + 1) * PAGE
    empty = grown <= p * PAGE

    @pl.when(whole)
    def _():
        for c in range(2):
            write(p, c, read(p, c))

    @pl.when(empty)
    def _():
        for c in range(2):
            write(p, c, jnp.zeros((PAGE, HD), jnp.bfloat16))

    @pl.when(jnp.logical_not(whole | empty))
    def _():
        at = lax.broadcasted_iota(jnp.int32, (PAGE, HD), 0) + p * PAGE
        for c in range(2):
            x = jnp.where(at < length, read(p, c).astype(jnp.float32), 0.0)
            if fresh is not None:
                rows = fresh().astype(jnp.float32)
                for t in range(STEPS):
                    x = jnp.where(at == length + t, rows[c * 2 + t:c * 2 + t + 1], x)
            write(p, c, x.astype(jnp.bfloat16))


def place_kernel(lens, block, cache, window):
    s = pl.program_id(0)
    length = lens[s, 0]

    def read(p, c):
        return block[0, pl.ds((p * 2 + c) * PAGE, PAGE)]

    def write(p, c, x):
        cache[0, c, pl.ds(p * PAGE, PAGE)] = x

    for p in range(MIGPG):
        masked_page(read, write, length, None, p)
    cache[1] = jnp.zeros((2, MIGLEN, HD), jnp.bfloat16)
    base = window_base(length)
    for c in range(2):
        window[0, c] = cache[0, c, pl.ds(base, 32)]


def place_first(lens, received):
    return pl.pallas_call(
        place_kernel,
        out_shape=(
            jax.ShapeDtypeStruct((INST * CAP, 2, MIGLEN, HD), jnp.bfloat16),
            jax.ShapeDtypeStruct((INST, 2, 32, HD), jnp.bfloat16),
        ),
        grid_spec=pltpu.PrefetchScalarGridSpec(
            num_scalar_prefetch=1,
            grid=(INST,),
            in_specs=[pl.BlockSpec((1, 2 * MIGLEN, HD), lambda s, _: (s, 0, 0))],
            out_specs=[
                pl.BlockSpec((CAP, 2, MIGLEN, HD), lambda s, _: (s, 0, 0, 0)),
                pl.BlockSpec((1, 2, 32, HD), lambda s, _: (s, 0, 0, 0)),
            ],
        ),
        compiler_params=pltpu.CompilerParams(vmem_limit_bytes=8 << 20),
        cost_estimate=pl.CostEstimate(flops=0, bytes_accessed=13 << 20, transcendentals=0),
        name="place_first",
    )(lens, received)


def settle_kernel(full, lens, window, second, extra, _, cache, out, patched, dups, sems, dup_sems):
    at = lax.broadcasted_iota(jnp.int32, (32, HD), 0)

    def patch_copy(s, c):
        return pltpu.make_async_copy(
            patched.at[s, c],
            cache.at[s * CAP, c, pl.ds(window_base(lens[s, 0]), 32)],
            sems.at[s * 2 + c],
        )

    def dup_copy(s):
        return pltpu.make_async_copy(dups.at[s], cache.at[s * CAP + 1], dup_sems.at[s])

    for s in range(INST):
        length = lens[s, 0]

        @pl.when(length > 0)
        def _():
            fresh = second[s, pl.ds(ROWS, 16)].astype(jnp.float32)
            where = at + window_base(length)
            for c in range(2):
                x = window[s, c].astype(jnp.float32)
                for t in range(STEPS):
                    x = jnp.where(where == length + t, fresh[c * 2 + t:c * 2 + t + 1], x)
                patched[s, c] = x.astype(jnp.bfloat16)
                patch_copy(s, c).start()

    order = jnp.int32(0)
    for s in range(INST):
        length = lens[s, 1]
        rank = jnp.minimum(order, DUPS - 1)
        order = order + (length > 0).astype(jnp.int32)

        @pl.when(length > 0)
        def _():
            def read(p, c):
                if full:
                    return extra[s, pl.ds((p * 2 + c) * PAGE, PAGE)]
                row = pl.multiple_of(B_DUP + rank * 2 * PIECE + c * PIECE, PIECE)
                return jnp.concatenate(
                    [second[p * MIGPG + i, pl.ds(row, PIECE)] for i in range(MIGPG)], axis=0
                )

            def write(p, c, x):
                dups[s, c, pl.ds(p * PAGE, PAGE)] = x

            for p in range(MIGPG):
                masked_page(read, write, length, lambda: second[s, pl.ds(32 + ROWS, 16)], p)
            dup_copy(s).start()

    for s in range(INST):
        for slot in range(CAP):
            filled = lens[s, slot] > 0
            rows = second[s, pl.ds(slot * 32, ROWS)]
            out[s * CAP + slot] = jnp.where(filled, rows, jnp.zeros_like(rows))
    for s in range(INST):
        @pl.when(lens[s, 0] > 0)
        def _():
            for c in range(2):
                patch_copy(s, c).wait()

        @pl.when(lens[s, 1] > 0)
        def _():
            dup_copy(s).wait()


def settle_all(full, lens, window, second, extra, cache):
    def kernel(*refs):
        settle_kernel(full, *refs)

    return pl.pallas_call(
        kernel,
        out_shape=(
            jax.ShapeDtypeStruct(cache.shape, jnp.bfloat16),
            jax.ShapeDtypeStruct((INST * CAP, ROWS, HD), jnp.bfloat16),
        ),
        in_specs=[spec(SMEM)] + [spec(VMEM)] * 3 + [spec(pl.ANY)],
        out_specs=(spec(pl.ANY), spec(VMEM)),
        scratch_shapes=[
            pltpu.VMEM((INST, 2, 32, HD), jnp.bfloat16),
            pltpu.VMEM((INST, 2, MIGLEN, HD), jnp.bfloat16),
            pltpu.SemaphoreType.DMA((INST * 2,)),
            pltpu.SemaphoreType.DMA((INST,)),
        ],
        input_output_aliases={4: 0},
        compiler_params=pltpu.CompilerParams(vmem_limit_bytes=20 << 20),
        name="settle_full" if full else "settle_short",
    )(lens, window, second, extra, cache)


def on_device(
    queries,
    hidden_in,
    kv_weight,
    kv_pool,
    page_table,
    long_lengths,
    short_lengths,
    mig_order,
    destination,
):
    inst_index = lax.axis_index("inst")
    tp_index = lax.axis_index("tp")
    targets = destination.reshape(1, MIG)
    tables = (page_table, long_lengths, short_lengths, mig_order, targets)
    pages = kv_pool.reshape(PAGES, 2 * PAGE, HD)

    def from_x(value, k):
        return lax.ppermute(value, "tp", [(i, (i // 2 + k) % 4 * 2 + i % 2) for i in range(8)])

    def from_y(value):
        return lax.ppermute(value, "tp", [(i, i ^ 1) for i in range(8)])

    mate = from_y(hidden_in)
    first = build(tables, pages)
    first, mate = lax.optimization_barrier((first, mate))
    pair = jnp.stack([hidden_in, mate])
    blocks = jnp.stack([pair, *[from_x(pair, k) for k in range(1, 4)]])
    blocks = blocks.reshape(8, REQS * STEPS, -1)
    got_first = lax.all_to_all(first, "inst", split_axis=0, concat_axis=0, tiled=True)

    hidden_all = join(tp_index.reshape(1), blocks)
    fresh = jnp.einsum(
        "rd,dcn->rcn", hidden_all, kv_weight, preferred_element_type=jnp.float32
    ).astype(jnp.bfloat16)
    fresh = fresh.reshape(REQS, STEPS, 2, HD)
    values = jnp.pad(fresh[:, :, 1], ((0, 0), (0, 16 - STEPS), (0, 0)))
    keys_values = jnp.pad(
        fresh.transpose(0, 2, 1, 3).reshape(REQS, 2 * STEPS, HD),
        ((0, 0), (0, 16 - 2 * STEPS), (0, 0)),
    )
    stay, second = attend(
        tables, queries.reshape(REQS, ROWS, HD), keys_values, values, kv_pool
    )
    stay_out = stay.reshape(REQS, STEPS, KV_HEADS * HD)
    second = route(got_first, second)
    got_second = lax.all_to_all(second, "inst", split_axis=0, concat_axis=0, tiled=True)

    arriving, load = decode(
        inst_index.reshape(1), long_lengths, short_lengths, mig_order, got_first
    )
    load_share = load[0, :1]
    overflow = load[1, 0] > 0.5

    cache, window = place_first(arriving, got_first)

    def short_path(args):
        lens, window, second, cache = args
        return tuple(settle_all(False, lens, window, second, window, cache))

    def long_path(args):
        lens, window, second, cache = args
        send = build_second(page_table, mig_order, targets, pages)
        got = lax.all_to_all(send, "inst", split_axis=0, concat_axis=0, tiled=True)
        return tuple(settle_all(True, lens, window, second, got, cache))

    moved_cache, moved = lax.cond(
        overflow, long_path, short_path, (arriving, window, got_second, cache)
    )
    moved_out = moved.reshape(INST * CAP, STEPS, KV_HEADS * HD)
    return (stay_out, moved_out, moved_cache, load_share)


def solution(mesh):
    placed = (
        P("inst", None, "tp"),
        P("inst", None, "tp"),
        P(None, None, "tp"),
        P("inst", None, None, "tp"),
        P("inst", None),
        P("inst", None),
        P("inst", None),
        P("inst", None),
        P("inst", None),
    )
    return jax.shard_map(
        on_device,
        mesh=mesh,
        in_specs=placed,
        out_specs=(
            P("inst", None, "tp"),
            P("inst", None, "tp"),
            P("inst", None, None, "tp"),
            P("inst"),
        ),
        check_vma=False,
    )
```

```python
import math

import jax
import jax.numpy as jnp
from jax import lax
from jax.experimental import pallas as pl
from jax.experimental.pallas import tpu as pltpu
from jax.sharding import PartitionSpec as P

HEADS = 64
KV_HEADS = 8
HD = 128
PAGE = 128
MAXPG = 64
MIGPG = 4
LONG = 2
MIG = 16
CAP = 2
STEPS = 2
SHORT = 20
REQS = 22
MIGLEN = 512
INST = 16
PAGES = 208
ROWS = 16
DUPS = 4
PIECE = MIGLEN // INST

A_DUP = 2 * MIGLEN
A_META = A_DUP + 2 * PIECE
A_ROWS = A_META + 16
B_FRESH = CAP * 16
B_DUP = B_FRESH + 16
B_ROWS = B_DUP + DUPS * 2 * PIECE

SMEM = pltpu.SMEM
VMEM = pltpu.VMEM


def spec(space):
    return pl.BlockSpec(memory_space=space)


def clear(count):
    for i in range(INST):
        count[i] = 0


def take_slot(count, to):
    slot = count[to]
    count[to] = slot + 1
    return slot


def build_kernel(
    table, longs, shorts, order, dest, pool, out, count, slots, held, extra, stage, sems, extra_sem, out_sems, stage_sem
):
    def load(page, k, p):
        return pltpu.make_async_copy(
            pool.at[page], held.at[k, pl.ds(p * 2 * PAGE, 2 * PAGE)], sems.at[k]
        )

    def send(k):
        return pltpu.make_async_copy(
            held.at[k], out.at[dest[0, k], pl.ds(0, 2 * MIGLEN)], out_sems.at[k]
        )

    clear(count)

    def begin(k, dup_at):
        slot = take_slot(count, dest[0, k])
        slots[k] = slot
        first = LONG * MAXPG + order[0, k] * MIGPG

        @pl.when(slot == 0)
        def _():
            for p in range(MIGPG):
                load(table[0, first + p], k, p).start()

        second = (slot == 1) & (dup_at < 0)

        @pl.when(second)
        def _():
            for p in range(MIGPG):
                pltpu.make_async_copy(pool.at[table[0, first + p]], extra.at[p], extra_sem).start()

        return jnp.where(second, k, dup_at)

    dup_at = jnp.int32(-1)
    for k in range(MIG):
        dup_at = begin(k, dup_at)

    def each(k, carry):
        @pl.when(slots[k] == 0)
        def _():
            pltpu.make_async_copy(held.at[k], held.at[k], sems.at[k]).wait()
            send(k).start()

        return carry

    for k in range(MIG):
        each(k, 0)

    lane = lax.broadcasted_iota(jnp.int32, (16, 128), 1)
    total = jnp.int32(STEPS * REQS)
    for i in range(LONG):
        total = total + longs[0, i]
    for i in range(SHORT):
        total = total + shorts[0, i]
    dup_to = jnp.where(dup_at >= 0, dest[0, jnp.maximum(dup_at, 0)] + 1, 0)
    row = jnp.zeros((16, 128), jnp.int32)
    for at, value in ((64, total & 127), (65, (total >> 7) & 127), (66, total >> 14), (67, dup_to)):
        row = jnp.where(lane == at, value, row)
    for k in range(MIG):
        at = dest[0, k] * CAP + slots[k]
        length = shorts[0, order[0, k]]
        row = jnp.where(lane == at, length & 255, row)
        row = jnp.where(lane == at + 32, length >> 8, row)
    tables = row.astype(jnp.float32).astype(jnp.bfloat16)
    for m in range(INST):
        stage[m, pl.ds(2 * PIECE, 16)] = tables

    @pl.when(dup_at >= 0)
    def _():
        pltpu.make_async_copy(extra, extra, extra_sem).wait()
        for m in range(INST):
            for c in range(2):
                stage[m, pl.ds(c * PIECE, PIECE)] = extra[
                    m // MIGPG, pl.ds(c * PAGE + m % MIGPG * PIECE, PIECE)
                ]

    last = pltpu.make_async_copy(stage, out.at[:, pl.ds(A_DUP, A_ROWS - A_DUP)], stage_sem)
    last.start()

    def finish(k, carry):
        @pl.when(slots[k] == 0)
        def _():
            send(k).wait()

        return carry

    lax.fori_loop(0, MIG, finish, 0)
    last.wait()


def build(tables, pool):
    return pl.pallas_call(
        build_kernel,
        out_shape=jax.ShapeDtypeStruct((INST, A_ROWS, HD), jnp.bfloat16),
        in_specs=[spec(SMEM)] * 5 + [spec(pl.ANY)],
        out_specs=spec(pltpu.HBM),
        scratch_shapes=[
            pltpu.SMEM((INST,), jnp.int32),
            pltpu.SMEM((MIG,), jnp.int32),
            pltpu.VMEM((MIG, 2 * MIGLEN, HD), jnp.bfloat16),
            pltpu.VMEM((MIGPG, 2 * PAGE, HD), jnp.bfloat16),
            pltpu.VMEM((INST, A_ROWS - A_DUP, HD), jnp.bfloat16),
            pltpu.SemaphoreType.DMA((MIG,)),
            pltpu.SemaphoreType.DMA(()),
            pltpu.SemaphoreType.DMA((MIG,)),
            pltpu.SemaphoreType.DMA(()),
        ],
        compiler_params=pltpu.CompilerParams(vmem_limit_bytes=60 << 20),
        cost_estimate=pl.CostEstimate(flops=0, bytes_accessed=9 << 20, transcendentals=0),
        name="build_first",
    )(*tables, pool)


def second_kernel(table, order, dest, pool, out, count, held, sems, out_sems):
    def load(k, p):
        page = table[0, LONG * MAXPG + order[0, k] * MIGPG + p]
        return pltpu.make_async_copy(
            pool.at[page], held.at[dest[0, k], pl.ds(p * 2 * PAGE, 2 * PAGE)], sems.at[k * MIGPG + p]
        )

    def send(k):
        to = dest[0, k]
        return pltpu.make_async_copy(held.at[to], out.at[to], out_sems.at[k])

    for stage in range(3):
        clear(count)

        def each(k, carry):
            slot = take_slot(count, dest[0, k])

            @pl.when(slot == 1)
            def _():
                if stage == 0:
                    for p in range(MIGPG):
                        load(k, p).start()
                elif stage == 1:
                    for p in range(MIGPG):
                        load(k, p).wait()
                    send(k).start()
                else:
                    send(k).wait()

            return carry

        lax.fori_loop(0, MIG, each, 0)


def build_second(table, order, dest, pool):
    return pl.pallas_call(
        second_kernel,
        out_shape=jax.ShapeDtypeStruct((INST, 2 * MIGLEN, HD), jnp.bfloat16),
        in_specs=[spec(SMEM)] * 3 + [spec(pl.ANY)],
        out_specs=spec(pl.ANY),
        scratch_shapes=[
            pltpu.SMEM((INST,), jnp.int32),
            pltpu.VMEM((INST, 2 * MIGLEN, HD), jnp.bfloat16),
            pltpu.SemaphoreType.DMA((MIG * MIGPG,)),
            pltpu.SemaphoreType.DMA((MIG,)),
        ],
        compiler_params=pltpu.CompilerParams(vmem_limit_bytes=12 << 20),
        name="build_second",
    )(table, order, dest, pool)


def dot_nt(a, b):
    return lax.dot_general(a, b, (((1,), (1,)), ((), ())), preferred_element_type=jnp.float32)


def dot_nn(a, b):
    return lax.dot_general(a, b, (((1,), (0,)), ((), ())), preferred_element_type=jnp.float32)


GROUP = 4
CHUNK = 1024
SCALE = 1.0 / math.sqrt(HD)


def attend_kernel(
    table, longs, shorts, order, dest, query, keys_values, values, pool, stay, out,
    count, place, cache, score, side, rows, page_sems, long_sems, side_sem,
):
    def load(pg, sem):
        return pltpu.make_async_copy(pool.at[table[0, pg]], cache.at[:, pg], sem)

    def wait_pages(first, size, sem):
        pltpu.make_async_copy(
            cache.at[:, pl.ds(first, size)], cache.at[:, pl.ds(first, size)], sem
        ).wait()

    for r in range(SHORT // GROUP):
        def start_short(i, carry, r=r):
            load(LONG * MAXPG + r * GROUP * MIGPG + i, page_sems.at[r]).start()
            return carry

        lax.fori_loop(0, GROUP * MIGPG, start_short, 0)
    per = CHUNK // PAGE
    chunks = [(longs[0, j] + CHUNK - 1) // CHUNK for j in range(LONG)]
    for j in range(LONG):
        def start_long(i, carry, j=j):
            for p in range(per):
                load(j * MAXPG + i * per + p, long_sems.at[j, i]).start()
            return carry

        lax.fori_loop(0, chunks[j], start_long, 0)

    clear(count)
    for i in range(SHORT):
        place[i] = -1

    def settle(k, carry):
        to = dest[0, k]
        place[order[0, k]] = to * CAP + take_slot(count, to)
        return carry

    lax.fori_loop(0, MIG, settle, 0)

    def fresh_scores(q, r):
        s = dot_nt(q, keys_values[r]) * SCALE
        step = lax.broadcasted_iota(jnp.int32, s.shape, 0) // 8
        col = lax.broadcasted_iota(jnp.int32, s.shape, 1)
        return jnp.where((col <= step) & (col < STEPS), s, -1e30)

    def short_group(g, carry):
        first = pl.multiple_of(LONG * MAXPG + g * GROUP * MIGPG, GROUP * MIGPG)
        wait_pages(first, GROUP * MIGPG, page_sems.at[g])
        pos = lax.broadcasted_iota(jnp.int32, (ROWS, MIGLEN), 1)
        old, new = [], []
        for i in range(GROUP):
            r = g * GROUP + i
            q = query[LONG + r]
            k = cache[0, pl.ds(first + i * MIGPG, MIGPG)].reshape(MIGLEN, HD)
            s = dot_nt(q, k) * SCALE
            old.append(jnp.where(pos < shorts[0, r], s, -1e30))
            new.append(fresh_scores(q, LONG + r))
        old = jnp.concatenate(old, axis=0)
        new = jnp.concatenate(new, axis=0)
        peak = jnp.maximum(jnp.max(old, 1, keepdims=True), jnp.max(new, 1, keepdims=True))
        old = jnp.exp(old - peak)
        new = jnp.exp(new - peak)
        denominator = jnp.sum(old, 1, keepdims=True) + jnp.sum(new, 1, keepdims=True)
        old = (old / denominator).astype(jnp.bfloat16)
        new = (new / denominator).astype(jnp.bfloat16)
        for i in range(GROUP):
            r = g * GROUP + i
            v = cache[1, pl.ds(first + i * MIGPG, MIGPG)].reshape(MIGLEN, HD)
            o = dot_nn(old[i * ROWS:(i + 1) * ROWS], v)
            o = o + dot_nn(new[i * ROWS:(i + 1) * ROWS], values[LONG + r])
            o = o.astype(jnp.bfloat16)
            at = place[r]

            @pl.when(at < 0)
            def _():
                stay[LONG + r] = o

            @pl.when(at >= 0)
            def _():
                stay[LONG + r] = jnp.zeros_like(o)
                side[at // CAP, pl.ds(pl.multiple_of(at % CAP * ROWS, ROWS), ROWS)] = o
                rows[at // CAP, pl.ds(pl.multiple_of(at % CAP * 8, 8), 8)] = keys_values[
                    LONG + r
                ].astype(jnp.float32)[:8]

        return carry

    lax.fori_loop(0, SHORT // GROUP, short_group, 0)

    side[:, pl.ds(B_FRESH, 16)] = rows[...].astype(jnp.bfloat16)
    side_copy = pltpu.make_async_copy(side, out.at[:, pl.ds(0, B_DUP)], side_sem)
    side_copy.start()

    for j in range(LONG):
        q = query[j]
        new = fresh_scores(q, j)
        length = longs[0, j]

        def scores(i, top, j=j, q=q, length=length):
            first = pl.multiple_of(j * MAXPG + i * per, per)
            wait_pages(first, per, long_sems.at[j, i])
            s = dot_nt(q, cache[0, pl.ds(first, per)].reshape(CHUNK, HD)) * SCALE
            pos = lax.broadcasted_iota(jnp.int32, s.shape, 1) + i * CHUNK
            s = jnp.where(pos < length, s, -1e30)
            score[j, i] = s
            return jnp.maximum(top, jnp.max(s, 1, keepdims=True))

        top = lax.fori_loop(0, chunks[j], scores, jnp.max(new, 1, keepdims=True))
        new = jnp.exp(new - top)

        def exponents(i, denominator, j=j, top=top):
            e = jnp.exp(score[j, i] - top)
            score[j, i] = e
            return denominator + jnp.sum(e, 1, keepdims=True)

        denominator = lax.fori_loop(0, chunks[j], exponents, jnp.sum(new, 1, keepdims=True))
        inverse = 1.0 / denominator

        def blend(i, o, j=j, inverse=inverse):
            first = pl.multiple_of(j * MAXPG + i * per, per)
            v = cache[1, pl.ds(first, per)].reshape(CHUNK, HD)
            return o + dot_nn((score[j, i] * inverse).astype(jnp.bfloat16), v)

        o = dot_nn((new * inverse).astype(jnp.bfloat16), values[j])
        stay[j] = lax.fori_loop(0, chunks[j], blend, o).astype(jnp.bfloat16)
    side_copy.wait()


def attend(tables, query, keys_values, values, pool):
    return pl.pallas_call(
        attend_kernel,
        out_shape=(
            jax.ShapeDtypeStruct((REQS, ROWS, HD), jnp.bfloat16),
            jax.ShapeDtypeStruct((INST, B_ROWS, HD), jnp.bfloat16),
        ),
        in_specs=[spec(SMEM)] * 5 + [spec(VMEM)] * 3 + [spec(pl.ANY)],
        out_specs=(spec(VMEM), spec(pltpu.HBM)),
        scratch_shapes=[
            pltpu.SMEM((INST,), jnp.int32),
            pltpu.SMEM((SHORT,), jnp.int32),
            pltpu.VMEM((2, PAGES, PAGE, HD), jnp.bfloat16),
            pltpu.VMEM((LONG, MAXPG * PAGE // CHUNK, ROWS, CHUNK), jnp.float32),
            pltpu.VMEM((INST, B_DUP, HD), jnp.bfloat16),
            pltpu.VMEM((INST, 16, HD), jnp.float32),
            pltpu.SemaphoreType.DMA((SHORT // GROUP,)),
            pltpu.SemaphoreType.DMA((LONG, MAXPG * PAGE // CHUNK)),
            pltpu.SemaphoreType.DMA(()),
        ],
        compiler_params=pltpu.CompilerParams(vmem_limit_bytes=24 << 20),
        cost_estimate=pl.CostEstimate(
            flops=4 * 26624 * 16 * 128, bytes_accessed=14 << 20, transcendentals=26624 * 16
        ),
        name="attend_all",
    )(*tables, query, keys_values, values, pool)


def join_kernel(here, blocks, out):
    me = here[0]
    width = blocks.shape[2]
    for k in range(8):
        x = (me // 2 + 4 - k // 2) % 4
        y = (me + k % 2) % 2
        at = pl.multiple_of((x * 2 + y) * width, width)
        out[:, pl.ds(at, width)] = blocks[k]


def join(here, blocks):
    _, rows, width = blocks.shape
    return pl.pallas_call(
        join_kernel,
        out_shape=jax.ShapeDtypeStruct((rows, width * 8), jnp.bfloat16),
        in_specs=[spec(SMEM), spec(VMEM)],
        out_specs=spec(VMEM),
        name="join_hidden",
    )(here, blocks)


def route_kernel(received, _, out, small, count, slots, sem, out_sems):
    copy = pltpu.make_async_copy(received.at[:, pl.ds(A_DUP, A_ROWS - A_DUP)], small, sem)
    copy.start()
    clear(count)
    copy.wait()
    lane = lax.broadcasted_iota(jnp.int32, (16, 128), 1)
    targets = []
    for s in range(INST):
        tables = small[s, pl.ds(2 * PIECE, 16)].astype(jnp.float32)
        targets.append(jnp.max(jnp.where(lane == 67, tables, 0.0)).astype(jnp.int32) - 1)

    def forward(s, to, slot):
        row = pl.multiple_of(B_DUP + slot * 2 * PIECE, 16)
        return pltpu.make_async_copy(
            small.at[s, pl.ds(0, 2 * PIECE)], out.at[to, pl.ds(row, 2 * PIECE)], out_sems.at[s]
        )

    for s, to in enumerate(targets):
        slots[s] = DUPS

        @pl.when(to >= 0)
        def _():
            slots[s] = take_slot(count, to)

        @pl.when((to >= 0) & (slots[s] < DUPS))
        def _():
            forward(s, to, slots[s]).start()

    for s, to in enumerate(targets):
        @pl.when((to >= 0) & (slots[s] < DUPS))
        def _():
            forward(s, to, slots[s]).wait()


def route(received, second):
    return pl.pallas_call(
        route_kernel,
        out_shape=jax.ShapeDtypeStruct((INST, B_ROWS, HD), jnp.bfloat16),
        in_specs=[spec(pl.ANY), spec(pltpu.HBM)],
        out_specs=spec(pltpu.HBM),
        scratch_shapes=[
            pltpu.VMEM((INST, A_ROWS - A_DUP, HD), jnp.bfloat16),
            pltpu.SMEM((INST,), jnp.int32),
            pltpu.SMEM((INST,), jnp.int32),
            pltpu.SemaphoreType.DMA(()),
            pltpu.SemaphoreType.DMA((INST,)),
        ],
        input_output_aliases={1: 0},
        cost_estimate=pl.CostEstimate(flops=0, bytes_accessed=1 << 20, transcendentals=0),
        name="route_pieces",
    )(received, second)


def decode_kernel(here, longs, shorts, order, received, lens, load, small, sem):
    copy = pltpu.make_async_copy(received.at[:, pl.ds(A_META, 16)], small, sem)
    copy.start()
    resident = jnp.int32(STEPS * (LONG + SHORT - MIG))
    for i in range(LONG):
        resident = resident + longs[0, i]
    for i in range(MIG, SHORT):
        resident = resident + shorts[0, order[0, i]]
    copy.wait()

    def total(x, axis=None):
        return jnp.sum(x, axis=axis, keepdims=True)

    x = jnp.max(small[...].astype(jnp.float32), axis=1)
    lane = lax.broadcasted_iota(jnp.int32, x.shape, 1)
    table = jnp.where(lane < INST * CAP, x + 256.0 * pltpu.roll(x, 96, 1), 0.0)
    own = resident.astype(jnp.float32)
    result = jnp.zeros_like(x)
    for slot in range(CAP):
        length = total(jnp.where(lane == here[0] * CAP + slot, table, 0.0), 1)
        result = jnp.where(lane == slot, length, result)
        own = own + total(jnp.where(length > 0.0, length + STEPS, 0.0))
    lens[...] = result.astype(jnp.int32)
    digits = jnp.where(lane == 64, 1.0, jnp.where(lane == 65, 128.0, jnp.where(lane == 66, 16384.0, 0.0)))
    share = own * INST / total(x * digits)
    double = jnp.where((table > 0.0) & (lane % 2 == 1), 1.0, 0.0)
    sends = jnp.max(total(double, 1), keepdims=True)
    takes = jnp.max(total(double, 0), keepdims=True)
    over = jnp.where((sends > 1.0) | (takes > DUPS), 1.0, 0.0)
    row = lax.broadcasted_iota(jnp.int32, (8, 128), 0)
    load[...] = jnp.where(row == 0, share, over)


def decode(here, longs, shorts, order, received):
    return pl.pallas_call(
        decode_kernel,
        out_shape=(
            jax.ShapeDtypeStruct((INST, 128), jnp.int32),
            jax.ShapeDtypeStruct((8, 128), jnp.float32),
        ),
        in_specs=[spec(SMEM)] * 4 + [spec(pl.ANY)],
        out_specs=(spec(VMEM), spec(VMEM)),
        scratch_shapes=[
            pltpu.VMEM((INST, 16, HD), jnp.bfloat16),
            pltpu.SemaphoreType.DMA(()),
        ],
        name="decode_tables",
    )(here, longs, shorts, order, received)


def window_base(length):
    return pl.multiple_of(jnp.minimum(length // 16 * 16, MIGLEN - 32), 16)


def masked_page(read, write, length, fresh, p):
    grown = length + STEPS if fresh is not None else length
    whole = length >= (p + 1) * PAGE
    empty = grown <= p * PAGE

    @pl.when(whole)
    def _():
        for c in range(2):
            write(p, c, read(p, c))

    @pl.when(empty)
    def _():
        for c in range(2):
            write(p, c, jnp.zeros((PAGE, HD), jnp.bfloat16))

    @pl.when(jnp.logical_not(whole | empty))
    def _():
        at = lax.broadcasted_iota(jnp.int32, (PAGE, HD), 0) + p * PAGE
        for c in range(2):
            x = jnp.where(at < length, read(p, c).astype(jnp.float32), 0.0)
            if fresh is not None:
                rows = fresh()
                for t in range(STEPS):
                    x = jnp.where(at == length + t, rows[c * 2 + t:c * 2 + t + 1], x)
            write(p, c, x.astype(jnp.bfloat16))


def place_kernel(lens, block, cache, window):
    s = pl.program_id(0)
    length = lens[s, 0]

    def read(p, c):
        return block[0, pl.ds((p * 2 + c) * PAGE, PAGE)]

    def write(p, c, x):
        cache[0, c, pl.ds(p * PAGE, PAGE)] = x

    for p in range(MIGPG):
        masked_page(read, write, length, None, p)
    cache[1] = jnp.zeros((2, MIGLEN, HD), jnp.bfloat16)
    base = window_base(length)
    for c in range(2):
        window[0, c] = cache[0, c, pl.ds(base, 32)]


def place_first(lens, received):
    return pl.pallas_call(
        place_kernel,
        out_shape=(
            jax.ShapeDtypeStruct((INST * CAP, 2, MIGLEN, HD), jnp.bfloat16),
            jax.ShapeDtypeStruct((INST, 2, 32, HD), jnp.bfloat16),
        ),
        grid_spec=pltpu.PrefetchScalarGridSpec(
            num_scalar_prefetch=1,
            grid=(INST,),
            in_specs=[pl.BlockSpec((1, 2 * MIGLEN, HD), lambda s, _: (s, 0, 0))],
            out_specs=[
                pl.BlockSpec((CAP, 2, MIGLEN, HD), lambda s, _: (s, 0, 0, 0)),
                pl.BlockSpec((1, 2, 32, HD), lambda s, _: (s, 0, 0, 0)),
            ],
        ),
        compiler_params=pltpu.CompilerParams(vmem_limit_bytes=8 << 20),
        cost_estimate=pl.CostEstimate(flops=0, bytes_accessed=13 << 20, transcendentals=0),
        name="place_first",
    )(lens, received)


def settle_kernel(full, lens, window, second, extra, _, cache, out, patched, dups, sems, dup_sems):
    at = lax.broadcasted_iota(jnp.int32, (32, HD), 0)

    def patch_copy(s, c):
        return pltpu.make_async_copy(
            patched.at[s, c],
            cache.at[s * CAP, c, pl.ds(window_base(lens[s, 0]), 32)],
            sems.at[s * 2 + c],
        )

    def dup_copy(s):
        return pltpu.make_async_copy(dups.at[s], cache.at[s * CAP + 1], dup_sems.at[s])

    for s in range(INST):
        length = lens[s, 0]

        @pl.when(length > 0)
        def _():
            fresh = second[s, pl.ds(B_FRESH, 16)].astype(jnp.float32)[:8]
            where = at + window_base(length)
            for c in range(2):
                x = window[s, c].astype(jnp.float32)
                for t in range(STEPS):
                    x = jnp.where(where == length + t, fresh[c * 2 + t:c * 2 + t + 1], x)
                patched[s, c] = x.astype(jnp.bfloat16)
                patch_copy(s, c).start()

    order = jnp.int32(0)
    for s in range(INST):
        length = lens[s, 1]
        rank = jnp.minimum(order, DUPS - 1)
        order = order + (length > 0).astype(jnp.int32)

        @pl.when(length > 0)
        def _():
            def read(p, c):
                if full:
                    return extra[s, pl.ds((p * 2 + c) * PAGE, PAGE)]
                row = pl.multiple_of(B_DUP + rank * 2 * PIECE + c * PIECE, 16)
                return jnp.concatenate(
                    [second[p * MIGPG + i, pl.ds(row, PIECE)] for i in range(MIGPG)], axis=0
                )

            def write(p, c, x):
                dups[s, c, pl.ds(p * PAGE, PAGE)] = x

            for p in range(MIGPG):
                masked_page(read, write, length, lambda: second[s, pl.ds(B_FRESH, 16)].astype(jnp.float32)[8:], p)
            dup_copy(s).start()

    for s in range(INST):
        for slot in range(CAP):
            filled = lens[s, slot] > 0
            rows = second[s, pl.ds(slot * ROWS, ROWS)]
            out[s * CAP + slot] = jnp.where(filled, rows, jnp.zeros_like(rows))
    for s in range(INST):
        @pl.when(lens[s, 0] > 0)
        def _():
            for c in range(2):
                patch_copy(s, c).wait()

        @pl.when(lens[s, 1] > 0)
        def _():
            dup_copy(s).wait()


def settle_all(full, lens, window, second, extra, cache):
    def kernel(*refs):
        settle_kernel(full, *refs)

    return pl.pallas_call(
        kernel,
        out_shape=(
            jax.ShapeDtypeStruct(cache.shape, jnp.bfloat16),
            jax.ShapeDtypeStruct((INST * CAP, ROWS, HD), jnp.bfloat16),
        ),
        in_specs=[spec(SMEM)] + [spec(VMEM)] * 3 + [spec(pl.ANY)],
        out_specs=(spec(pl.ANY), spec(VMEM)),
        scratch_shapes=[
            pltpu.VMEM((INST, 2, 32, HD), jnp.bfloat16),
            pltpu.VMEM((INST, 2, MIGLEN, HD), jnp.bfloat16),
            pltpu.SemaphoreType.DMA((INST * 2,)),
            pltpu.SemaphoreType.DMA((INST,)),
        ],
        input_output_aliases={4: 0},
        compiler_params=pltpu.CompilerParams(vmem_limit_bytes=20 << 20),
        name="settle_full" if full else "settle_short",
    )(lens, window, second, extra, cache)


def on_device(
    queries,
    hidden_in,
    kv_weight,
    kv_pool,
    page_table,
    long_lengths,
    short_lengths,
    mig_order,
    destination,
):
    inst_index = lax.axis_index("inst")
    tp_index = lax.axis_index("tp")
    targets = destination.reshape(1, MIG)
    tables = (page_table, long_lengths, short_lengths, mig_order, targets)
    pages = kv_pool.reshape(PAGES, 2 * PAGE, HD)

    def from_x(value, k):
        return lax.ppermute(value, "tp", [(i, (i // 2 + k) % 4 * 2 + i % 2) for i in range(8)])

    def from_y(value):
        return lax.ppermute(value, "tp", [(i, i ^ 1) for i in range(8)])

    mate = from_y(hidden_in)
    first = build(tables, pages)
    first, mate = lax.optimization_barrier((first, mate))
    pair = jnp.stack([hidden_in, mate])
    blocks = jnp.stack([pair, *[from_x(pair, k) for k in range(1, 4)]])
    blocks = blocks.reshape(8, REQS * STEPS, -1)
    got_first = lax.all_to_all(first, "inst", split_axis=0, concat_axis=0, tiled=True)

    hidden_all = join(tp_index.reshape(1), blocks)
    fresh = jnp.einsum(
        "rd,dcn->rcn", hidden_all, kv_weight, preferred_element_type=jnp.float32
    ).astype(jnp.bfloat16)
    fresh = fresh.reshape(REQS, STEPS, 2, HD)
    values = jnp.pad(fresh[:, :, 1], ((0, 0), (0, 16 - STEPS), (0, 0)))
    keys_values = jnp.pad(
        fresh.transpose(0, 2, 1, 3).reshape(REQS, 2 * STEPS, HD),
        ((0, 0), (0, 16 - 2 * STEPS), (0, 0)),
    )
    stay, second = attend(
        tables, queries.reshape(REQS, ROWS, HD), keys_values, values, kv_pool
    )
    stay_out = stay.reshape(REQS, STEPS, KV_HEADS * HD)
    second = route(got_first, second)
    got_second = lax.all_to_all(second, "inst", split_axis=0, concat_axis=0, tiled=True)

    arriving, load = decode(
        inst_index.reshape(1), long_lengths, short_lengths, mig_order, got_first
    )
    load_share = load[0, :1]
    overflow = load[1, 0] > 0.5

    cache, window = place_first(arriving, got_first)

    def short_path(args):
        lens, window, second, cache = args
        return tuple(settle_all(False, lens, window, second, window, cache))

    def long_path(args):
        lens, window, second, cache = args
        send = build_second(page_table, mig_order, targets, pages)
        got = lax.all_to_all(send, "inst", split_axis=0, concat_axis=0, tiled=True)
        return tuple(settle_all(True, lens, window, second, got, cache))

    moved_cache, moved = lax.cond(
        overflow, long_path, short_path, (arriving, window, got_second, cache)
    )
    moved_out = moved.reshape(INST * CAP, STEPS, KV_HEADS * HD)
    return (stay_out, moved_out, moved_cache, load_share)


def solution(mesh):
    placed = (
        P("inst", None, "tp"),
        P("inst", None, "tp"),
        P(None, None, "tp"),
        P("inst", None, None, "tp"),
        P("inst", None),
        P("inst", None),
        P("inst", None),
        P("inst", None),
        P("inst", None),
    )
    return jax.shard_map(
        on_device,
        mesh=mesh,
        in_specs=placed,
        out_specs=(
            P("inst", None, "tp"),
            P("inst", None, "tp"),
            P("inst", None, None, "tp"),
            P("inst"),
        ),
        check_vma=False,
    )
```

```python
import math

import jax
import jax.numpy as jnp
from jax import lax
from jax.experimental import pallas as pl
from jax.experimental.pallas import tpu as pltpu
from jax.sharding import PartitionSpec as P

HEADS = 64
KV_HEADS = 8
HD = 128
PAGE = 128
MAXPG = 64
MIGPG = 4
LONG = 2
MIG = 16
CAP = 2
STEPS = 2
SHORT = 20
REQS = 22
MIGLEN = 512
INST = 16
PAGES = 208
ROWS = 16
DUPS = 4
PIECE = MIGLEN // INST

A_DUP = 2 * MIGLEN
A_META = A_DUP + 2 * PIECE
A_ROWS = A_META + 16
B_FRESH = CAP * 16
B_DUP = B_FRESH + 16
B_ROWS = B_DUP + DUPS * 2 * PIECE

SMEM = pltpu.SMEM
VMEM = pltpu.VMEM


def spec(space):
    return pl.BlockSpec(memory_space=space)


def clear(count):
    for i in range(INST):
        count[i] = 0


def take_slot(count, to):
    slot = count[to]
    count[to] = slot + 1
    return slot


def build_kernel(
    table, longs, shorts, order, dest, pool, out, count, slots, held, extra, stage, sems, extra_sem, out_sems, stage_sem
):
    def load(page, k, p):
        return pltpu.make_async_copy(
            pool.at[page], held.at[k, pl.ds(p * 2 * PAGE, 2 * PAGE)], sems.at[k]
        )

    def send(k):
        return pltpu.make_async_copy(
            held.at[k], out.at[dest[0, k], pl.ds(0, 2 * MIGLEN)], out_sems.at[k]
        )

    clear(count)

    def begin(k, dup_at):
        slot = take_slot(count, dest[0, k])
        slots[k] = slot
        first = LONG * MAXPG + order[0, k] * MIGPG

        @pl.when(slot == 0)
        def _():
            for p in range(MIGPG):
                load(table[0, first + p], k, p).start()

        second = (slot == 1) & (dup_at < 0)

        @pl.when(second)
        def _():
            for p in range(MIGPG):
                pltpu.make_async_copy(pool.at[table[0, first + p]], extra.at[p], extra_sem).start()

        return jnp.where(second, k, dup_at)

    dup_at = jnp.int32(-1)
    for k in range(MIG):
        dup_at = begin(k, dup_at)

    def each(k, carry):
        @pl.when(slots[k] == 0)
        def _():
            pltpu.make_async_copy(held.at[k], held.at[k], sems.at[k]).wait()
            send(k).start()

        return carry

    for k in range(MIG):
        each(k, 0)

    lane = lax.broadcasted_iota(jnp.int32, (16, 128), 1)
    total = jnp.int32(STEPS * REQS)
    for i in range(LONG):
        total = total + longs[0, i]
    for i in range(SHORT):
        total = total + shorts[0, i]
    dup_to = jnp.where(dup_at >= 0, dest[0, jnp.maximum(dup_at, 0)] + 1, 0)
    row = jnp.zeros((16, 128), jnp.int32)
    for at, value in ((64, total & 127), (65, (total >> 7) & 127), (66, total >> 14), (67, dup_to)):
        row = jnp.where(lane == at, value, row)
    for k in range(MIG):
        at = dest[0, k] * CAP + slots[k]
        length = shorts[0, order[0, k]]
        row = jnp.where(lane == at, length & 255, row)
        row = jnp.where(lane == at + 32, length >> 8, row)
    tables = row.astype(jnp.float32).astype(jnp.bfloat16)
    for m in range(INST):
        stage[m, pl.ds(2 * PIECE, 16)] = tables

    @pl.when(dup_at >= 0)
    def _():
        pltpu.make_async_copy(extra, extra, extra_sem).wait()
        for m in range(INST):
            for c in range(2):
                stage[m, pl.ds(c * PIECE, PIECE)] = extra[
                    m // MIGPG, pl.ds(c * PAGE + m % MIGPG * PIECE, PIECE)
                ]

    last = pltpu.make_async_copy(stage, out.at[:, pl.ds(A_DUP, A_ROWS - A_DUP)], stage_sem)
    last.start()

    def finish(k, carry):
        @pl.when(slots[k] == 0)
        def _():
            send(k).wait()

        return carry

    lax.fori_loop(0, MIG, finish, 0)
    last.wait()


def build(tables, pool):
    return pl.pallas_call(
        build_kernel,
        out_shape=jax.ShapeDtypeStruct((INST, A_ROWS, HD), jnp.bfloat16),
        in_specs=[spec(SMEM)] * 5 + [spec(pl.ANY)],
        out_specs=spec(pltpu.HBM),
        scratch_shapes=[
            pltpu.SMEM((INST,), jnp.int32),
            pltpu.SMEM((MIG,), jnp.int32),
            pltpu.VMEM((MIG, 2 * MIGLEN, HD), jnp.bfloat16),
            pltpu.VMEM((MIGPG, 2 * PAGE, HD), jnp.bfloat16),
            pltpu.VMEM((INST, A_ROWS - A_DUP, HD), jnp.bfloat16),
            pltpu.SemaphoreType.DMA((MIG,)),
            pltpu.SemaphoreType.DMA(()),
            pltpu.SemaphoreType.DMA((MIG,)),
            pltpu.SemaphoreType.DMA(()),
        ],
        compiler_params=pltpu.CompilerParams(vmem_limit_bytes=60 << 20),
        cost_estimate=pl.CostEstimate(flops=0, bytes_accessed=9 << 20, transcendentals=0),
        name="build_first",
    )(*tables, pool)


def second_kernel(table, order, dest, pool, out, count, held, sems, out_sems):
    def load(k, p):
        page = table[0, LONG * MAXPG + order[0, k] * MIGPG + p]
        return pltpu.make_async_copy(
            pool.at[page], held.at[dest[0, k], pl.ds(p * 2 * PAGE, 2 * PAGE)], sems.at[k * MIGPG + p]
        )

    def send(k):
        to = dest[0, k]
        return pltpu.make_async_copy(held.at[to], out.at[to], out_sems.at[k])

    for stage in range(3):
        clear(count)

        def each(k, carry):
            slot = take_slot(count, dest[0, k])

            @pl.when(slot == 1)
            def _():
                if stage == 0:
                    for p in range(MIGPG):
                        load(k, p).start()
                elif stage == 1:
                    for p in range(MIGPG):
                        load(k, p).wait()
                    send(k).start()
                else:
                    send(k).wait()

            return carry

        lax.fori_loop(0, MIG, each, 0)


def build_second(table, order, dest, pool):
    return pl.pallas_call(
        second_kernel,
        out_shape=jax.ShapeDtypeStruct((INST, 2 * MIGLEN, HD), jnp.bfloat16),
        in_specs=[spec(SMEM)] * 3 + [spec(pl.ANY)],
        out_specs=spec(pl.ANY),
        scratch_shapes=[
            pltpu.SMEM((INST,), jnp.int32),
            pltpu.VMEM((INST, 2 * MIGLEN, HD), jnp.bfloat16),
            pltpu.SemaphoreType.DMA((MIG * MIGPG,)),
            pltpu.SemaphoreType.DMA((MIG,)),
        ],
        compiler_params=pltpu.CompilerParams(vmem_limit_bytes=12 << 20),
        name="build_second",
    )(table, order, dest, pool)


def dot_nt(a, b):
    return lax.dot_general(a, b, (((1,), (1,)), ((), ())), preferred_element_type=jnp.float32)


def dot_nn(a, b):
    return lax.dot_general(a, b, (((1,), (0,)), ((), ())), preferred_element_type=jnp.float32)


GROUP = 4
CHUNK = 1024
SCALE = 1.0 / math.sqrt(HD)


def attend_kernel(
    table, longs, shorts, order, dest, query, keys_values, values, pool, stay, out,
    count, place, cache, score, side, rows, page_sems, long_sems, side_sem,
):
    def load(pg, sem):
        return pltpu.make_async_copy(pool.at[table[0, pg]], cache.at[:, pg], sem)

    def wait_pages(first, size, sem):
        pltpu.make_async_copy(
            cache.at[:, pl.ds(first, size)], cache.at[:, pl.ds(first, size)], sem
        ).wait()

    for r in range(SHORT // GROUP):
        def start_short(i, carry, r=r):
            load(LONG * MAXPG + r * GROUP * MIGPG + i, page_sems.at[r]).start()
            return carry

        lax.fori_loop(0, GROUP * MIGPG, start_short, 0)
    per = CHUNK // PAGE
    chunks = [(longs[0, j] + CHUNK - 1) // CHUNK for j in range(LONG)]
    for j in range(LONG):
        def start_long(i, carry, j=j):
            for p in range(per):
                load(j * MAXPG + i * per + p, long_sems.at[j, i]).start()
            return carry

        lax.fori_loop(0, chunks[j], start_long, 0)

    clear(count)
    for i in range(SHORT):
        place[i] = -1

    def settle(k, carry):
        to = dest[0, k]
        place[order[0, k]] = to * CAP + take_slot(count, to)
        return carry

    lax.fori_loop(0, MIG, settle, 0)

    def fresh_scores(q, r):
        s = dot_nt(q, keys_values[r]) * SCALE
        step = lax.broadcasted_iota(jnp.int32, s.shape, 0) // 8
        col = lax.broadcasted_iota(jnp.int32, s.shape, 1)
        return jnp.where((col <= step) & (col < STEPS), s, -1e30)

    def short_group(g, carry):
        first = pl.multiple_of(LONG * MAXPG + g * GROUP * MIGPG, GROUP * MIGPG)
        wait_pages(first, GROUP * MIGPG, page_sems.at[g])
        pos = lax.broadcasted_iota(jnp.int32, (ROWS, MIGLEN), 1)
        old, new = [], []
        for i in range(GROUP):
            r = g * GROUP + i
            q = query[LONG + r]
            k = cache[0, pl.ds(first + i * MIGPG, MIGPG)].reshape(MIGLEN, HD)
            s = dot_nt(q, k) * SCALE
            old.append(jnp.where(pos < shorts[0, r], s, -1e30))
            new.append(fresh_scores(q, LONG + r))
        old = jnp.concatenate(old, axis=0)
        new = jnp.concatenate(new, axis=0)
        peak = jnp.maximum(jnp.max(old, 1, keepdims=True), jnp.max(new, 1, keepdims=True))
        old = jnp.exp(old - peak)
        new = jnp.exp(new - peak)
        denominator = jnp.sum(old, 1, keepdims=True) + jnp.sum(new, 1, keepdims=True)
        old = (old / denominator).astype(jnp.bfloat16)
        new = (new / denominator).astype(jnp.bfloat16)
        for i in range(GROUP):
            r = g * GROUP + i
            v = cache[1, pl.ds(first + i * MIGPG, MIGPG)].reshape(MIGLEN, HD)
            o = dot_nn(old[i * ROWS:(i + 1) * ROWS], v)
            o = o + dot_nn(new[i * ROWS:(i + 1) * ROWS], values[LONG + r])
            o = o.astype(jnp.bfloat16)
            at = place[r]

            @pl.when(at < 0)
            def _():
                stay[LONG + r] = o

            @pl.when(at >= 0)
            def _():
                stay[LONG + r] = jnp.zeros_like(o)
                side[at // CAP, pl.ds(pl.multiple_of(at % CAP * ROWS, ROWS), ROWS)] = o
                rows[at // CAP, pl.ds(pl.multiple_of(at % CAP * 8, 8), 8)] = keys_values[
                    LONG + r
                ].astype(jnp.float32)[:8]

        return carry

    lax.fori_loop(0, SHORT // GROUP, short_group, 0)

    side[:, pl.ds(B_FRESH, 16)] = rows[...].astype(jnp.bfloat16)
    side_copy = pltpu.make_async_copy(side, out.at[:, pl.ds(0, B_DUP)], side_sem)
    side_copy.start()

    for j in range(LONG):
        q = query[j]
        new = fresh_scores(q, j)
        length = longs[0, j]

        def scores(i, top, j=j, q=q, length=length):
            first = pl.multiple_of(j * MAXPG + i * per, per)
            wait_pages(first, per, long_sems.at[j, i])
            s = dot_nt(q, cache[0, pl.ds(first, per)].reshape(CHUNK, HD)) * SCALE
            pos = lax.broadcasted_iota(jnp.int32, s.shape, 1) + i * CHUNK
            s = jnp.where(pos < length, s, -1e30)
            score[j, i] = s
            return jnp.maximum(top, jnp.max(s, 1, keepdims=True))

        top = lax.fori_loop(0, chunks[j], scores, jnp.max(new, 1, keepdims=True))
        new = jnp.exp(new - top)

        def exponents(i, denominator, j=j, top=top):
            e = jnp.exp(score[j, i] - top)
            score[j, i] = e
            return denominator + jnp.sum(e, 1, keepdims=True)

        denominator = lax.fori_loop(0, chunks[j], exponents, jnp.sum(new, 1, keepdims=True))
        inverse = 1.0 / denominator

        def blend(i, o, j=j, inverse=inverse):
            first = pl.multiple_of(j * MAXPG + i * per, per)
            v = cache[1, pl.ds(first, per)].reshape(CHUNK, HD)
            return o + dot_nn((score[j, i] * inverse).astype(jnp.bfloat16), v)

        o = dot_nn((new * inverse).astype(jnp.bfloat16), values[j])
        stay[j] = lax.fori_loop(0, chunks[j], blend, o).astype(jnp.bfloat16)
    side_copy.wait()


def attend(tables, query, keys_values, values, pool):
    return pl.pallas_call(
        attend_kernel,
        out_shape=(
            jax.ShapeDtypeStruct((REQS, ROWS, HD), jnp.bfloat16),
            jax.ShapeDtypeStruct((INST, B_ROWS, HD), jnp.bfloat16),
        ),
        in_specs=[spec(SMEM)] * 5 + [spec(VMEM)] * 3 + [spec(pl.ANY)],
        out_specs=(spec(VMEM), spec(pltpu.HBM)),
        scratch_shapes=[
            pltpu.SMEM((INST,), jnp.int32),
            pltpu.SMEM((SHORT,), jnp.int32),
            pltpu.VMEM((2, PAGES, PAGE, HD), jnp.bfloat16),
            pltpu.VMEM((LONG, MAXPG * PAGE // CHUNK, ROWS, CHUNK), jnp.float32),
            pltpu.VMEM((INST, B_DUP, HD), jnp.bfloat16),
            pltpu.VMEM((INST, 16, HD), jnp.float32),
            pltpu.SemaphoreType.DMA((SHORT // GROUP,)),
            pltpu.SemaphoreType.DMA((LONG, MAXPG * PAGE // CHUNK)),
            pltpu.SemaphoreType.DMA(()),
        ],
        compiler_params=pltpu.CompilerParams(vmem_limit_bytes=24 << 20),
        cost_estimate=pl.CostEstimate(
            flops=4 * 26624 * 16 * 128, bytes_accessed=14 << 20, transcendentals=26624 * 16
        ),
        name="attend_all",
    )(*tables, query, keys_values, values, pool)


def join_kernel(here, blocks, out):
    me = here[0]
    width = blocks.shape[2]
    for k in range(8):
        x = (me // 2 + 4 - k // 2) % 4
        y = (me + k % 2) % 2
        at = pl.multiple_of((x * 2 + y) * width, width)
        out[:, pl.ds(at, width)] = blocks[k]


def join(here, blocks):
    _, rows, width = blocks.shape
    return pl.pallas_call(
        join_kernel,
        out_shape=jax.ShapeDtypeStruct((rows, width * 8), jnp.bfloat16),
        in_specs=[spec(SMEM), spec(VMEM)],
        out_specs=spec(VMEM),
        name="join_hidden",
    )(here, blocks)


def route_kernel(received, _, out, tables, small, count, slots, sem, small_sem, out_sems):
    first = pltpu.make_async_copy(received.at[:, pl.ds(A_META, 16)], tables, sem)
    rest = pltpu.make_async_copy(received.at[:, pl.ds(A_DUP, 2 * PIECE)], small, small_sem)
    first.start()
    rest.start()
    clear(count)
    first.wait()
    lane = lax.broadcasted_iota(jnp.int32, (16, 128), 1)
    targets = []
    for s in range(INST):
        found = jnp.where(lane == 67, tables[s].astype(jnp.float32), 0.0)
        targets.append(jnp.max(found).astype(jnp.int32) - 1)
    rest.wait()

    def forward(s, to, slot):
        row = pl.multiple_of(B_DUP + slot * 2 * PIECE, 16)
        return pltpu.make_async_copy(
            small.at[s], out.at[to, pl.ds(row, 2 * PIECE)], out_sems.at[s]
        )

    for s, to in enumerate(targets):
        slots[s] = DUPS

        @pl.when(to >= 0)
        def _():
            slots[s] = take_slot(count, to)

        @pl.when((to >= 0) & (slots[s] < DUPS))
        def _():
            forward(s, to, slots[s]).start()

    for s, to in enumerate(targets):
        @pl.when((to >= 0) & (slots[s] < DUPS))
        def _():
            forward(s, to, slots[s]).wait()


def route(received, second):
    return pl.pallas_call(
        route_kernel,
        out_shape=jax.ShapeDtypeStruct((INST, B_ROWS, HD), jnp.bfloat16),
        in_specs=[spec(pl.ANY), spec(pltpu.HBM)],
        out_specs=spec(pltpu.HBM),
        scratch_shapes=[
            pltpu.VMEM((INST, 16, HD), jnp.bfloat16),
            pltpu.VMEM((INST, 2 * PIECE, HD), jnp.bfloat16),
            pltpu.SMEM((INST,), jnp.int32),
            pltpu.SMEM((INST,), jnp.int32),
            pltpu.SemaphoreType.DMA(()),
            pltpu.SemaphoreType.DMA(()),
            pltpu.SemaphoreType.DMA((INST,)),
        ],
        input_output_aliases={1: 0},
        cost_estimate=pl.CostEstimate(flops=0, bytes_accessed=1 << 20, transcendentals=0),
        name="route_pieces",
    )(received, second)


def decode_kernel(here, longs, shorts, order, received, lens, load, small, sem):
    copy = pltpu.make_async_copy(received.at[:, pl.ds(A_META, 16)], small, sem)
    copy.start()
    resident = jnp.int32(STEPS * (LONG + SHORT - MIG))
    for i in range(LONG):
        resident = resident + longs[0, i]
    for i in range(MIG, SHORT):
        resident = resident + shorts[0, order[0, i]]
    copy.wait()

    def total(x, axis=None):
        return jnp.sum(x, axis=axis, keepdims=True)

    x = jnp.max(small[...].astype(jnp.float32), axis=1)
    lane = lax.broadcasted_iota(jnp.int32, x.shape, 1)
    table = jnp.where(lane < INST * CAP, x + 256.0 * pltpu.roll(x, 96, 1), 0.0)
    own = resident.astype(jnp.float32)
    result = jnp.zeros_like(x)
    for slot in range(CAP):
        length = total(jnp.where(lane == here[0] * CAP + slot, table, 0.0), 1)
        result = jnp.where(lane == slot, length, result)
        own = own + total(jnp.where(length > 0.0, length + STEPS, 0.0))
    lens[...] = result.astype(jnp.int32)
    digits = jnp.where(lane == 64, 1.0, jnp.where(lane == 65, 128.0, jnp.where(lane == 66, 16384.0, 0.0)))
    share = own * INST / total(x * digits)
    double = jnp.where((table > 0.0) & (lane % 2 == 1), 1.0, 0.0)
    sends = jnp.max(total(double, 1), keepdims=True)
    takes = jnp.max(total(double, 0), keepdims=True)
    over = jnp.where((sends > 1.0) | (takes > DUPS), 1.0, 0.0)
    row = lax.broadcasted_iota(jnp.int32, (8, 128), 0)
    load[...] = jnp.where(row == 0, share, over)


def decode(here, longs, shorts, order, received):
    return pl.pallas_call(
        decode_kernel,
        out_shape=(
            jax.ShapeDtypeStruct((INST, 128), jnp.int32),
            jax.ShapeDtypeStruct((8, 128), jnp.float32),
        ),
        in_specs=[spec(SMEM)] * 4 + [spec(pl.ANY)],
        out_specs=(spec(VMEM), spec(VMEM)),
        scratch_shapes=[
            pltpu.VMEM((INST, 16, HD), jnp.bfloat16),
            pltpu.SemaphoreType.DMA(()),
        ],
        name="decode_tables",
    )(here, longs, shorts, order, received)


def window_base(length):
    return pl.multiple_of(jnp.minimum(length // 16 * 16, MIGLEN - 32), 16)


def masked_page(read, write, length, fresh, p):
    grown = length + STEPS if fresh is not None else length
    whole = length >= (p + 1) * PAGE
    empty = grown <= p * PAGE

    @pl.when(whole)
    def _():
        for c in range(2):
            write(p, c, read(p, c))

    @pl.when(empty)
    def _():
        for c in range(2):
            write(p, c, jnp.zeros((PAGE, HD), jnp.bfloat16))

    @pl.when(jnp.logical_not(whole | empty))
    def _():
        at = lax.broadcasted_iota(jnp.int32, (PAGE, HD), 0) + p * PAGE
        for c in range(2):
            x = jnp.where(at < length, read(p, c).astype(jnp.float32), 0.0)
            if fresh is not None:
                rows = fresh()
                for t in range(STEPS):
                    x = jnp.where(at == length + t, rows[c * 2 + t:c * 2 + t + 1], x)
            write(p, c, x.astype(jnp.bfloat16))


def place_kernel(lens, block, cache, window):
    s = pl.program_id(0)
    length = lens[s, 0]

    def read(p, c):
        return block[0, pl.ds((p * 2 + c) * PAGE, PAGE)]

    def write(p, c, x):
        cache[0, c, pl.ds(p * PAGE, PAGE)] = x

    for p in range(MIGPG):
        masked_page(read, write, length, None, p)
    cache[1] = jnp.zeros((2, MIGLEN, HD), jnp.bfloat16)
    base = window_base(length)
    for c in range(2):
        window[0, c] = cache[0, c, pl.ds(base, 32)]


def place_first(lens, received):
    return pl.pallas_call(
        place_kernel,
        out_shape=(
            jax.ShapeDtypeStruct((INST * CAP, 2, MIGLEN, HD), jnp.bfloat16),
            jax.ShapeDtypeStruct((INST, 2, 32, HD), jnp.bfloat16),
        ),
        grid_spec=pltpu.PrefetchScalarGridSpec(
            num_scalar_prefetch=1,
            grid=(INST,),
            in_specs=[pl.BlockSpec((1, 2 * MIGLEN, HD), lambda s, _: (s, 0, 0))],
            out_specs=[
                pl.BlockSpec((CAP, 2, MIGLEN, HD), lambda s, _: (s, 0, 0, 0)),
                pl.BlockSpec((1, 2, 32, HD), lambda s, _: (s, 0, 0, 0)),
            ],
        ),
        compiler_params=pltpu.CompilerParams(vmem_limit_bytes=8 << 20),
        cost_estimate=pl.CostEstimate(flops=0, bytes_accessed=13 << 20, transcendentals=0),
        name="place_first",
    )(lens, received)


def settle_kernel(full, lens, window, second, extra, _, cache, out, patched, dups, sems, dup_sems):
    at = lax.broadcasted_iota(jnp.int32, (32, HD), 0)

    def patch_copy(s, c):
        return pltpu.make_async_copy(
            patched.at[s, c],
            cache.at[s * CAP, c, pl.ds(window_base(lens[s, 0]), 32)],
            sems.at[s * 2 + c],
        )

    def dup_copy(s):
        return pltpu.make_async_copy(dups.at[s], cache.at[s * CAP + 1], dup_sems.at[s])

    for s in range(INST):
        length = lens[s, 0]

        @pl.when(length > 0)
        def _():
            fresh = second[s, pl.ds(B_FRESH, 16)].astype(jnp.float32)[:8]
            where = at + window_base(length)
            for c in range(2):
                x = window[s, c].astype(jnp.float32)
                for t in range(STEPS):
                    x = jnp.where(where == length + t, fresh[c * 2 + t:c * 2 + t + 1], x)
                patched[s, c] = x.astype(jnp.bfloat16)
                patch_copy(s, c).start()

    order = jnp.int32(0)
    for s in range(INST):
        length = lens[s, 1]
        rank = jnp.minimum(order, DUPS - 1)
        order = order + (length > 0).astype(jnp.int32)

        @pl.when(length > 0)
        def _():
            def read(p, c):
                if full:
                    return extra[s, pl.ds((p * 2 + c) * PAGE, PAGE)]
                row = pl.multiple_of(B_DUP + rank * 2 * PIECE + c * PIECE, 16)
                return jnp.concatenate(
                    [second[p * MIGPG + i, pl.ds(row, PIECE)] for i in range(MIGPG)], axis=0
                )

            def write(p, c, x):
                dups[s, c, pl.ds(p * PAGE, PAGE)] = x

            for p in range(MIGPG):
                masked_page(read, write, length, lambda: second[s, pl.ds(B_FRESH, 16)].astype(jnp.float32)[8:], p)
            dup_copy(s).start()

    for s in range(INST):
        for slot in range(CAP):
            filled = lens[s, slot] > 0
            rows = second[s, pl.ds(slot * ROWS, ROWS)]
            out[s * CAP + slot] = jnp.where(filled, rows, jnp.zeros_like(rows))
    for s in range(INST):
        @pl.when(lens[s, 0] > 0)
        def _():
            for c in range(2):
                patch_copy(s, c).wait()

        @pl.when(lens[s, 1] > 0)
        def _():
            dup_copy(s).wait()


def settle_all(full, lens, window, second, extra, cache):
    def kernel(*refs):
        settle_kernel(full, *refs)

    return pl.pallas_call(
        kernel,
        out_shape=(
            jax.ShapeDtypeStruct(cache.shape, jnp.bfloat16),
            jax.ShapeDtypeStruct((INST * CAP, ROWS, HD), jnp.bfloat16),
        ),
        in_specs=[spec(SMEM)] + [spec(VMEM)] * 3 + [spec(pl.ANY)],
        out_specs=(spec(pl.ANY), spec(VMEM)),
        scratch_shapes=[
            pltpu.VMEM((INST, 2, 32, HD), jnp.bfloat16),
            pltpu.VMEM((INST, 2, MIGLEN, HD), jnp.bfloat16),
            pltpu.SemaphoreType.DMA((INST * 2,)),
            pltpu.SemaphoreType.DMA((INST,)),
        ],
        input_output_aliases={4: 0},
        compiler_params=pltpu.CompilerParams(vmem_limit_bytes=20 << 20),
        name="settle_full" if full else "settle_short",
    )(lens, window, second, extra, cache)


def on_device(
    queries,
    hidden_in,
    kv_weight,
    kv_pool,
    page_table,
    long_lengths,
    short_lengths,
    mig_order,
    destination,
):
    inst_index = lax.axis_index("inst")
    tp_index = lax.axis_index("tp")
    targets = destination.reshape(1, MIG)
    tables = (page_table, long_lengths, short_lengths, mig_order, targets)
    pages = kv_pool.reshape(PAGES, 2 * PAGE, HD)

    def from_x(value, k):
        return lax.ppermute(value, "tp", [(i, (i // 2 + k) % 4 * 2 + i % 2) for i in range(8)])

    def from_y(value):
        return lax.ppermute(value, "tp", [(i, i ^ 1) for i in range(8)])

    mate = from_y(hidden_in)
    first = build(tables, pages)
    first, mate = lax.optimization_barrier((first, mate))
    pair = jnp.stack([hidden_in, mate])
    blocks = jnp.stack([pair, *[from_x(pair, k) for k in range(1, 4)]])
    blocks = blocks.reshape(8, REQS * STEPS, -1)
    got_first = lax.all_to_all(first, "inst", split_axis=0, concat_axis=0, tiled=True)

    hidden_all = join(tp_index.reshape(1), blocks)
    fresh = jnp.einsum(
        "rd,dcn->rcn", hidden_all, kv_weight, preferred_element_type=jnp.float32
    ).astype(jnp.bfloat16)
    fresh = fresh.reshape(REQS, STEPS, 2, HD)
    values = jnp.pad(fresh[:, :, 1], ((0, 0), (0, 16 - STEPS), (0, 0)))
    keys_values = jnp.pad(
        fresh.transpose(0, 2, 1, 3).reshape(REQS, 2 * STEPS, HD),
        ((0, 0), (0, 16 - 2 * STEPS), (0, 0)),
    )
    stay, second = attend(
        tables, queries.reshape(REQS, ROWS, HD), keys_values, values, kv_pool
    )
    stay_out = stay.reshape(REQS, STEPS, KV_HEADS * HD)
    second = route(got_first, second)
    got_second = lax.all_to_all(second, "inst", split_axis=0, concat_axis=0, tiled=True)

    arriving, load = decode(
        inst_index.reshape(1), long_lengths, short_lengths, mig_order, got_first
    )
    load_share = load[0, :1]
    overflow = load[1, 0] > 0.5

    cache, window = place_first(arriving, got_first)

    def short_path(args):
        lens, window, second, cache = args
        return tuple(settle_all(False, lens, window, second, window, cache))

    def long_path(args):
        lens, window, second, cache = args
        send = build_second(page_table, mig_order, targets, pages)
        got = lax.all_to_all(send, "inst", split_axis=0, concat_axis=0, tiled=True)
        return tuple(settle_all(True, lens, window, second, got, cache))

    moved_cache, moved = lax.cond(
        overflow, long_path, short_path, (arriving, window, got_second, cache)
    )
    moved = lax.optimization_barrier(moved)
    moved_out = moved.reshape(INST * CAP, STEPS, KV_HEADS * HD)
    return (stay_out, moved_out, moved_cache, load_share)


def solution(mesh):
    placed = (
        P("inst", None, "tp"),
        P("inst", None, "tp"),
        P(None, None, "tp"),
        P("inst", None, None, "tp"),
        P("inst", None),
        P("inst", None),
        P("inst", None),
        P("inst", None),
        P("inst", None),
    )
    return jax.shard_map(
        on_device,
        mesh=mesh,
        in_specs=placed,
        out_specs=(
            P("inst", None, "tp"),
            P("inst", None, "tp"),
            P("inst", None, None, "tp"),
            P("inst"),
        ),
        check_vma=False,
    )
```

```python
import math

import jax
import jax.numpy as jnp
from jax import lax
from jax.experimental import pallas as pl
from jax.experimental.pallas import tpu as pltpu
from jax.sharding import PartitionSpec as P

HEADS = 64
KV_HEADS = 8
HD = 128
PAGE = 128
MAXPG = 64
MIGPG = 4
LONG = 2
MIG = 16
CAP = 2
STEPS = 2
SHORT = 20
REQS = 22
MIGLEN = 512
INST = 16
PAGES = 208
ROWS = 16
DUPS = 4
PIECE = MIGLEN // INST

A_DUP = 2 * MIGLEN
A_META = A_DUP + 2 * PIECE
A_ROWS = A_META + 16
B_FRESH = CAP * 16
B_DUP = B_FRESH + 16
B_ROWS = B_DUP + DUPS * 2 * PIECE

SMEM = pltpu.SMEM
VMEM = pltpu.VMEM


def spec(space):
    return pl.BlockSpec(memory_space=space)


def clear(count):
    for i in range(INST):
        count[i] = 0


def take_slot(count, to):
    slot = count[to]
    count[to] = slot + 1
    return slot


def build_kernel(
    table, longs, shorts, order, dest, pool, out, count, slots, held, extra, stage, sems, extra_sem, out_sems, stage_sem
):
    def load(page, k, p):
        return pltpu.make_async_copy(
            pool.at[page], held.at[k, pl.ds(p * 2 * PAGE, 2 * PAGE)], sems.at[k]
        )

    def send(k):
        return pltpu.make_async_copy(
            held.at[k], out.at[dest[0, k], pl.ds(0, 2 * MIGLEN)], out_sems.at[k]
        )

    clear(count)

    def begin(k, dup_at):
        slot = take_slot(count, dest[0, k])
        slots[k] = slot
        first = LONG * MAXPG + order[0, k] * MIGPG

        @pl.when(slot == 0)
        def _():
            for p in range(MIGPG):
                load(table[0, first + p], k, p).start()

        second = (slot == 1) & (dup_at < 0)

        @pl.when(second)
        def _():
            for p in range(MIGPG):
                pltpu.make_async_copy(pool.at[table[0, first + p]], extra.at[p], extra_sem).start()

        return jnp.where(second, k, dup_at)

    dup_at = jnp.int32(-1)
    for k in range(MIG):
        dup_at = begin(k, dup_at)

    def each(k, carry):
        @pl.when(slots[k] == 0)
        def _():
            pltpu.make_async_copy(held.at[k], held.at[k], sems.at[k]).wait()
            send(k).start()

        return carry

    for k in range(MIG):
        each(k, 0)

    lane = lax.broadcasted_iota(jnp.int32, (16, 128), 1)
    total = jnp.int32(STEPS * REQS)
    for i in range(LONG):
        total = total + longs[0, i]
    for i in range(SHORT):
        total = total + shorts[0, i]
    dup_to = jnp.where(dup_at >= 0, dest[0, jnp.maximum(dup_at, 0)] + 1, 0)
    row = jnp.zeros((16, 128), jnp.int32)
    for at, value in ((64, total & 127), (65, (total >> 7) & 127), (66, total >> 14), (67, dup_to)):
        row = jnp.where(lane == at, value, row)
    for k in range(MIG):
        at = dest[0, k] * CAP + slots[k]
        length = shorts[0, order[0, k]]
        row = jnp.where(lane == at, length & 255, row)
        row = jnp.where(lane == at + 32, length >> 8, row)
    tables = row.astype(jnp.float32).astype(jnp.bfloat16)
    for m in range(INST):
        stage[m, pl.ds(2 * PIECE, 16)] = tables

    @pl.when(dup_at >= 0)
    def _():
        pltpu.make_async_copy(extra, extra, extra_sem).wait()
        for m in range(INST):
            for c in range(2):
                stage[m, pl.ds(c * PIECE, PIECE)] = extra[
                    m // MIGPG, pl.ds(c * PAGE + m % MIGPG * PIECE, PIECE)
                ]

    last = pltpu.make_async_copy(stage, out.at[:, pl.ds(A_DUP, A_ROWS - A_DUP)], stage_sem)
    last.start()

    def finish(k, carry):
        @pl.when(slots[k] == 0)
        def _():
            send(k).wait()

        return carry

    lax.fori_loop(0, MIG, finish, 0)
    last.wait()


def build(tables, pool):
    return pl.pallas_call(
        build_kernel,
        out_shape=jax.ShapeDtypeStruct((INST, A_ROWS, HD), jnp.bfloat16),
        in_specs=[spec(SMEM)] * 5 + [spec(pl.ANY)],
        out_specs=spec(pltpu.HBM),
        scratch_shapes=[
            pltpu.SMEM((INST,), jnp.int32),
            pltpu.SMEM((MIG,), jnp.int32),
            pltpu.VMEM((MIG, 2 * MIGLEN, HD), jnp.bfloat16),
            pltpu.VMEM((MIGPG, 2 * PAGE, HD), jnp.bfloat16),
            pltpu.VMEM((INST, A_ROWS - A_DUP, HD), jnp.bfloat16),
            pltpu.SemaphoreType.DMA((MIG,)),
            pltpu.SemaphoreType.DMA(()),
            pltpu.SemaphoreType.DMA((MIG,)),
            pltpu.SemaphoreType.DMA(()),
        ],
        compiler_params=pltpu.CompilerParams(vmem_limit_bytes=60 << 20),
        cost_estimate=pl.CostEstimate(flops=0, bytes_accessed=9 << 20, transcendentals=0),
        name="build_first",
    )(*tables, pool)


def second_kernel(table, order, dest, pool, out, count, held, sems, out_sems):
    def load(k, p):
        page = table[0, LONG * MAXPG + order[0, k] * MIGPG + p]
        return pltpu.make_async_copy(
            pool.at[page], held.at[dest[0, k], pl.ds(p * 2 * PAGE, 2 * PAGE)], sems.at[k * MIGPG + p]
        )

    def send(k):
        to = dest[0, k]
        return pltpu.make_async_copy(held.at[to], out.at[to], out_sems.at[k])

    for stage in range(3):
        clear(count)

        def each(k, carry):
            slot = take_slot(count, dest[0, k])

            @pl.when(slot == 1)
            def _():
                if stage == 0:
                    for p in range(MIGPG):
                        load(k, p).start()
                elif stage == 1:
                    for p in range(MIGPG):
                        load(k, p).wait()
                    send(k).start()
                else:
                    send(k).wait()

            return carry

        lax.fori_loop(0, MIG, each, 0)


def build_second(table, order, dest, pool):
    return pl.pallas_call(
        second_kernel,
        out_shape=jax.ShapeDtypeStruct((INST, 2 * MIGLEN, HD), jnp.bfloat16),
        in_specs=[spec(SMEM)] * 3 + [spec(pl.ANY)],
        out_specs=spec(pl.ANY),
        scratch_shapes=[
            pltpu.SMEM((INST,), jnp.int32),
            pltpu.VMEM((INST, 2 * MIGLEN, HD), jnp.bfloat16),
            pltpu.SemaphoreType.DMA((MIG * MIGPG,)),
            pltpu.SemaphoreType.DMA((MIG,)),
        ],
        compiler_params=pltpu.CompilerParams(vmem_limit_bytes=12 << 20),
        name="build_second",
    )(table, order, dest, pool)


def dot_nt(a, b):
    return lax.dot_general(a, b, (((1,), (1,)), ((), ())), preferred_element_type=jnp.float32)


def dot_nn(a, b):
    return lax.dot_general(a, b, (((1,), (0,)), ((), ())), preferred_element_type=jnp.float32)


GROUP = 4
CHUNK = 1024
SCALE = 1.0 / math.sqrt(HD)


def attend_kernel(
    table, longs, shorts, order, dest, query, keys_values, values, pool, stay, out,
    count, place, cache, score, side, rows, page_sems, long_sems, side_sem,
):
    def load(pg, sem):
        return pltpu.make_async_copy(pool.at[table[0, pg]], cache.at[:, pg], sem)

    def wait_pages(first, size, sem):
        pltpu.make_async_copy(
            cache.at[:, pl.ds(first, size)], cache.at[:, pl.ds(first, size)], sem
        ).wait()

    for r in range(SHORT // GROUP):
        def start_short(i, carry, r=r):
            load(LONG * MAXPG + r * GROUP * MIGPG + i, page_sems.at[r]).start()
            return carry

        lax.fori_loop(0, GROUP * MIGPG, start_short, 0)
    per = CHUNK // PAGE
    chunks = [(longs[0, j] + CHUNK - 1) // CHUNK for j in range(LONG)]
    for j in range(LONG):
        def start_long(i, carry, j=j):
            for p in range(per):
                load(j * MAXPG + i * per + p, long_sems.at[j, i]).start()
            return carry

        lax.fori_loop(0, chunks[j], start_long, 0)

    clear(count)
    for i in range(SHORT):
        place[i] = -1

    def settle(k, carry):
        to = dest[0, k]
        place[order[0, k]] = to * CAP + take_slot(count, to)
        return carry

    lax.fori_loop(0, MIG, settle, 0)

    def fresh_scores(q, r):
        s = dot_nt(q, keys_values[r]) * SCALE
        step = lax.broadcasted_iota(jnp.int32, s.shape, 0) // 8
        col = lax.broadcasted_iota(jnp.int32, s.shape, 1)
        return jnp.where((col <= step) & (col < STEPS), s, -1e30)

    def short_group(g, carry):
        first = pl.multiple_of(LONG * MAXPG + g * GROUP * MIGPG, GROUP * MIGPG)
        wait_pages(first, GROUP * MIGPG, page_sems.at[g])
        pos = lax.broadcasted_iota(jnp.int32, (ROWS, MIGLEN), 1)
        old, new = [], []
        for i in range(GROUP):
            r = g * GROUP + i
            q = query[LONG + r]
            k = cache[0, pl.ds(first + i * MIGPG, MIGPG)].reshape(MIGLEN, HD)
            s = dot_nt(q, k) * SCALE
            old.append(jnp.where(pos < shorts[0, r], s, -1e30))
            new.append(fresh_scores(q, LONG + r))
        old = jnp.concatenate(old, axis=0)
        new = jnp.concatenate(new, axis=0)
        peak = jnp.maximum(jnp.max(old, 1, keepdims=True), jnp.max(new, 1, keepdims=True))
        old = jnp.exp(old - peak)
        new = jnp.exp(new - peak)
        denominator = jnp.sum(old, 1, keepdims=True) + jnp.sum(new, 1, keepdims=True)
        old = (old / denominator).astype(jnp.bfloat16)
        new = (new / denominator).astype(jnp.bfloat16)
        for i in range(GROUP):
            r = g * GROUP + i
            v = cache[1, pl.ds(first + i * MIGPG, MIGPG)].reshape(MIGLEN, HD)
            o = dot_nn(old[i * ROWS:(i + 1) * ROWS], v)
            o = o + dot_nn(new[i * ROWS:(i + 1) * ROWS], values[LONG + r])
            o = o.astype(jnp.bfloat16)
            at = place[r]

            @pl.when(at < 0)
            def _():
                stay[LONG + r] = o

            @pl.when(at >= 0)
            def _():
                stay[LONG + r] = jnp.zeros_like(o)
                side[at // CAP, pl.ds(pl.multiple_of(at % CAP * ROWS, ROWS), ROWS)] = o
                rows[at // CAP, pl.ds(pl.multiple_of(at % CAP * 8, 8), 8)] = keys_values[
                    LONG + r
                ].astype(jnp.float32)[:8]

        return carry

    lax.fori_loop(0, SHORT // GROUP, short_group, 0)

    side[:, pl.ds(B_FRESH, 16)] = rows[...].astype(jnp.bfloat16)
    side_copy = pltpu.make_async_copy(side, out.at[:, pl.ds(0, B_DUP)], side_sem)
    side_copy.start()

    for j in range(LONG):
        q = query[j]
        new = fresh_scores(q, j)
        length = longs[0, j]

        def scores(i, top, j=j, q=q, length=length):
            first = pl.multiple_of(j * MAXPG + i * per, per)
            wait_pages(first, per, long_sems.at[j, i])
            s = dot_nt(q, cache[0, pl.ds(first, per)].reshape(CHUNK, HD)) * SCALE
            pos = lax.broadcasted_iota(jnp.int32, s.shape, 1) + i * CHUNK
            s = jnp.where(pos < length, s, -1e30)
            score[j, i] = s
            return jnp.maximum(top, jnp.max(s, 1, keepdims=True))

        top = lax.fori_loop(0, chunks[j], scores, jnp.max(new, 1, keepdims=True))
        new = jnp.exp(new - top)

        def exponents(i, denominator, j=j, top=top):
            e = jnp.exp(score[j, i] - top)
            score[j, i] = e
            return denominator + jnp.sum(e, 1, keepdims=True)

        denominator = lax.fori_loop(0, chunks[j], exponents, jnp.sum(new, 1, keepdims=True))
        inverse = 1.0 / denominator

        def blend(i, o, j=j, inverse=inverse):
            first = pl.multiple_of(j * MAXPG + i * per, per)
            v = cache[1, pl.ds(first, per)].reshape(CHUNK, HD)
            return o + dot_nn((score[j, i] * inverse).astype(jnp.bfloat16), v)

        o = dot_nn((new * inverse).astype(jnp.bfloat16), values[j])
        stay[j] = lax.fori_loop(0, chunks[j], blend, o).astype(jnp.bfloat16)
    side_copy.wait()


def attend(tables, query, keys_values, values, pool):
    return pl.pallas_call(
        attend_kernel,
        out_shape=(
            jax.ShapeDtypeStruct((REQS, ROWS, HD), jnp.bfloat16),
            jax.ShapeDtypeStruct((INST, B_ROWS, HD), jnp.bfloat16),
        ),
        in_specs=[spec(SMEM)] * 5 + [spec(VMEM)] * 3 + [spec(pl.ANY)],
        out_specs=(spec(VMEM), spec(pltpu.HBM)),
        scratch_shapes=[
            pltpu.SMEM((INST,), jnp.int32),
            pltpu.SMEM((SHORT,), jnp.int32),
            pltpu.VMEM((2, PAGES, PAGE, HD), jnp.bfloat16),
            pltpu.VMEM((LONG, MAXPG * PAGE // CHUNK, ROWS, CHUNK), jnp.float32),
            pltpu.VMEM((INST, B_DUP, HD), jnp.bfloat16),
            pltpu.VMEM((INST, 16, HD), jnp.float32),
            pltpu.SemaphoreType.DMA((SHORT // GROUP,)),
            pltpu.SemaphoreType.DMA((LONG, MAXPG * PAGE // CHUNK)),
            pltpu.SemaphoreType.DMA(()),
        ],
        compiler_params=pltpu.CompilerParams(vmem_limit_bytes=24 << 20),
        cost_estimate=pl.CostEstimate(
            flops=4 * 26624 * 16 * 128, bytes_accessed=14 << 20, transcendentals=26624 * 16
        ),
        name="attend_all",
    )(*tables, query, keys_values, values, pool)


def join_kernel(here, blocks, out):
    me = here[0]
    width = blocks.shape[2]
    for k in range(8):
        x = (me // 2 + 4 - k // 2) % 4
        y = (me + k % 2) % 2
        at = pl.multiple_of((x * 2 + y) * width, width)
        out[:, pl.ds(at, width)] = blocks[k]


def join(here, blocks):
    _, rows, width = blocks.shape
    return pl.pallas_call(
        join_kernel,
        out_shape=jax.ShapeDtypeStruct((rows, width * 8), jnp.bfloat16),
        in_specs=[spec(SMEM), spec(VMEM)],
        out_specs=spec(VMEM),
        name="join_hidden",
    )(here, blocks)


def route_kernel(received, _, out, tables, small, count, slots, sem, small_sem, out_sems):
    first = pltpu.make_async_copy(received.at[:, pl.ds(A_META, 16)], tables, sem)
    rest = pltpu.make_async_copy(received.at[:, pl.ds(A_DUP, 2 * PIECE)], small, small_sem)
    first.start()
    rest.start()
    clear(count)
    first.wait()
    lane = lax.broadcasted_iota(jnp.int32, (16, 128), 1)
    targets = []
    for s in range(INST):
        found = jnp.where(lane == 67, tables[s].astype(jnp.float32), 0.0)
        targets.append(jnp.max(found).astype(jnp.int32) - 1)
    rest.wait()

    def forward(s, to, slot):
        row = pl.multiple_of(B_DUP + slot * 2 * PIECE, 16)
        return pltpu.make_async_copy(
            small.at[s], out.at[to, pl.ds(row, 2 * PIECE)], out_sems.at[s]
        )

    for s, to in enumerate(targets):
        slots[s] = DUPS

        @pl.when(to >= 0)
        def _():
            slots[s] = take_slot(count, to)

        @pl.when((to >= 0) & (slots[s] < DUPS))
        def _():
            forward(s, to, slots[s]).start()

    for s, to in enumerate(targets):
        @pl.when((to >= 0) & (slots[s] < DUPS))
        def _():
            forward(s, to, slots[s]).wait()


def route(received, second):
    return pl.pallas_call(
        route_kernel,
        out_shape=jax.ShapeDtypeStruct((INST, B_ROWS, HD), jnp.bfloat16),
        in_specs=[spec(pl.ANY), spec(pltpu.HBM)],
        out_specs=spec(pltpu.HBM),
        scratch_shapes=[
            pltpu.VMEM((INST, 16, HD), jnp.bfloat16),
            pltpu.VMEM((INST, 2 * PIECE, HD), jnp.bfloat16),
            pltpu.SMEM((INST,), jnp.int32),
            pltpu.SMEM((INST,), jnp.int32),
            pltpu.SemaphoreType.DMA(()),
            pltpu.SemaphoreType.DMA(()),
            pltpu.SemaphoreType.DMA((INST,)),
        ],
        input_output_aliases={1: 0},
        cost_estimate=pl.CostEstimate(flops=0, bytes_accessed=1 << 20, transcendentals=0),
        name="route_pieces",
    )(received, second)


def decode_kernel(here, longs, shorts, order, received, lens, load, small, sem):
    copy = pltpu.make_async_copy(received.at[:, pl.ds(A_META, 16)], small, sem)
    copy.start()
    resident = jnp.int32(STEPS * (LONG + SHORT - MIG))
    for i in range(LONG):
        resident = resident + longs[0, i]
    for i in range(MIG, SHORT):
        resident = resident + shorts[0, order[0, i]]
    copy.wait()

    def total(x, axis=None):
        return jnp.sum(x, axis=axis, keepdims=True)

    x = jnp.max(small[...].astype(jnp.float32), axis=1)
    lane = lax.broadcasted_iota(jnp.int32, x.shape, 1)
    table = jnp.where(lane < INST * CAP, x + 256.0 * pltpu.roll(x, 96, 1), 0.0)
    own = resident.astype(jnp.float32)
    result = jnp.zeros_like(x)
    for slot in range(CAP):
        length = total(jnp.where(lane == here[0] * CAP + slot, table, 0.0), 1)
        result = jnp.where(lane == slot, length, result)
        own = own + total(jnp.where(length > 0.0, length + STEPS, 0.0))
    lens[...] = result.astype(jnp.int32)
    digits = jnp.where(lane == 64, 1.0, jnp.where(lane == 65, 128.0, jnp.where(lane == 66, 16384.0, 0.0)))
    share = own * INST / total(x * digits)
    double = jnp.where((table > 0.0) & (lane % 2 == 1), 1.0, 0.0)
    sends = jnp.max(total(double, 1), keepdims=True)
    takes = jnp.max(total(double, 0), keepdims=True)
    over = jnp.where((sends > 1.0) | (takes > DUPS), 1.0, 0.0)
    row = lax.broadcasted_iota(jnp.int32, (8, 128), 0)
    load[...] = jnp.where(row == 0, share, over)


def decode(here, longs, shorts, order, received):
    return pl.pallas_call(
        decode_kernel,
        out_shape=(
            jax.ShapeDtypeStruct((INST, 128), jnp.int32),
            jax.ShapeDtypeStruct((8, 128), jnp.float32),
        ),
        in_specs=[spec(SMEM)] * 4 + [spec(pl.ANY)],
        out_specs=(spec(VMEM), spec(VMEM)),
        scratch_shapes=[
            pltpu.VMEM((INST, 16, HD), jnp.bfloat16),
            pltpu.SemaphoreType.DMA(()),
        ],
        name="decode_tables",
    )(here, longs, shorts, order, received)


def window_base(length):
    return pl.multiple_of(jnp.minimum(length // 16 * 16, MIGLEN - 32), 16)


def masked_page(read, write, length, fresh, p):
    grown = length + STEPS if fresh is not None else length
    whole = length >= (p + 1) * PAGE
    empty = grown <= p * PAGE

    @pl.when(whole)
    def _():
        for c in range(2):
            write(p, c, read(p, c))

    @pl.when(empty)
    def _():
        for c in range(2):
            write(p, c, jnp.zeros((PAGE, HD), jnp.bfloat16))

    @pl.when(jnp.logical_not(whole | empty))
    def _():
        at = lax.broadcasted_iota(jnp.int32, (PAGE, HD), 0) + p * PAGE
        for c in range(2):
            x = jnp.where(at < length, read(p, c).astype(jnp.float32), 0.0)
            if fresh is not None:
                rows = fresh()
                for t in range(STEPS):
                    x = jnp.where(at == length + t, rows[c * 2 + t:c * 2 + t + 1], x)
            write(p, c, x.astype(jnp.bfloat16))


def place_kernel(lens, block, cache, window):
    s = pl.program_id(0)
    length = lens[s, 0]

    def read(p, c):
        return block[0, pl.ds((p * 2 + c) * PAGE, PAGE)]

    def write(p, c, x):
        cache[0, c, pl.ds(p * PAGE, PAGE)] = x

    for p in range(MIGPG):
        masked_page(read, write, length, None, p)
    cache[1] = jnp.zeros((2, MIGLEN, HD), jnp.bfloat16)
    base = window_base(length)
    for c in range(2):
        window[0, c] = cache[0, c, pl.ds(base, 32)]


def place_first(lens, received):
    return pl.pallas_call(
        place_kernel,
        out_shape=(
            jax.ShapeDtypeStruct((INST * CAP, 2, MIGLEN, HD), jnp.bfloat16),
            jax.ShapeDtypeStruct((INST, 2, 32, HD), jnp.bfloat16),
        ),
        grid_spec=pltpu.PrefetchScalarGridSpec(
            num_scalar_prefetch=1,
            grid=(INST,),
            in_specs=[pl.BlockSpec((1, 2 * MIGLEN, HD), lambda s, _: (s, 0, 0))],
            out_specs=[
                pl.BlockSpec((CAP, 2, MIGLEN, HD), lambda s, _: (s, 0, 0, 0)),
                pl.BlockSpec((1, 2, 32, HD), lambda s, _: (s, 0, 0, 0)),
            ],
        ),
        compiler_params=pltpu.CompilerParams(vmem_limit_bytes=8 << 20),
        cost_estimate=pl.CostEstimate(flops=0, bytes_accessed=13 << 20, transcendentals=0),
        name="place_first",
    )(lens, received)


def settle_kernel(full, lens, window, second, extra, _, cache, out, patched, dups, sems, dup_sems):
    at = lax.broadcasted_iota(jnp.int32, (32, HD), 0)

    def patch_copy(s, c):
        return pltpu.make_async_copy(
            patched.at[s, c],
            cache.at[s * CAP, c, pl.ds(window_base(lens[s, 0]), 32)],
            sems.at[s * 2 + c],
        )

    def dup_copy(s):
        return pltpu.make_async_copy(dups.at[s], cache.at[s * CAP + 1], dup_sems.at[s])

    for s in range(INST):
        length = lens[s, 0]
        fresh = second[s, pl.ds(B_FRESH, 16)].astype(jnp.float32)[:8]
        where = at + window_base(length) - jnp.where(length > 0, length, -MIGLEN)
        for c in range(2):
            x = window[s, c].astype(jnp.float32)
            for t in range(STEPS):
                x = jnp.where(where == t, fresh[c * 2 + t:c * 2 + t + 1], x)
            patched[s, c] = x.astype(jnp.bfloat16)
            patch_copy(s, c).start()

    order = jnp.int32(0)
    for s in range(INST):
        length = lens[s, 1]
        rank = jnp.minimum(order, DUPS - 1)
        order = order + (length > 0).astype(jnp.int32)

        @pl.when(length > 0)
        def _():
            def read(p, c):
                if full:
                    return extra[s, pl.ds((p * 2 + c) * PAGE, PAGE)]
                row = pl.multiple_of(B_DUP + rank * 2 * PIECE + c * PIECE, 16)
                return jnp.concatenate(
                    [second[p * MIGPG + i, pl.ds(row, PIECE)] for i in range(MIGPG)], axis=0
                )

            def write(p, c, x):
                dups[s, c, pl.ds(p * PAGE, PAGE)] = x

            for p in range(MIGPG):
                masked_page(read, write, length, lambda: second[s, pl.ds(B_FRESH, 16)].astype(jnp.float32)[8:], p)
            dup_copy(s).start()

    for s in range(INST):
        for slot in range(CAP):
            filled = lens[s, slot] > 0
            rows = second[s, pl.ds(slot * ROWS, ROWS)]
            out[s * CAP + slot] = jnp.where(filled, rows, jnp.zeros_like(rows))
    for s in range(INST):
        for c in range(2):
            patch_copy(s, c).wait()

        @pl.when(lens[s, 1] > 0)
        def _():
            dup_copy(s).wait()


def settle_all(full, lens, window, second, extra, cache):
    def kernel(*refs):
        settle_kernel(full, *refs)

    return pl.pallas_call(
        kernel,
        out_shape=(
            jax.ShapeDtypeStruct(cache.shape, jnp.bfloat16),
            jax.ShapeDtypeStruct((INST * CAP, ROWS, HD), jnp.bfloat16),
        ),
        in_specs=[spec(SMEM)] + [spec(VMEM)] * 3 + [spec(pl.ANY)],
        out_specs=(spec(pl.ANY), spec(VMEM)),
        scratch_shapes=[
            pltpu.VMEM((INST, 2, 32, HD), jnp.bfloat16),
            pltpu.VMEM((INST, 2, MIGLEN, HD), jnp.bfloat16),
            pltpu.SemaphoreType.DMA((INST * 2,)),
            pltpu.SemaphoreType.DMA((INST,)),
        ],
        input_output_aliases={4: 0},
        compiler_params=pltpu.CompilerParams(vmem_limit_bytes=20 << 20),
        name="settle_full" if full else "settle_short",
    )(lens, window, second, extra, cache)


def on_device(
    queries,
    hidden_in,
    kv_weight,
    kv_pool,
    page_table,
    long_lengths,
    short_lengths,
    mig_order,
    destination,
):
    inst_index = lax.axis_index("inst")
    tp_index = lax.axis_index("tp")
    targets = destination.reshape(1, MIG)
    tables = (page_table, long_lengths, short_lengths, mig_order, targets)
    pages = kv_pool.reshape(PAGES, 2 * PAGE, HD)

    def from_x(value, k):
        return lax.ppermute(value, "tp", [(i, (i // 2 + k) % 4 * 2 + i % 2) for i in range(8)])

    def from_y(value):
        return lax.ppermute(value, "tp", [(i, i ^ 1) for i in range(8)])

    mate = from_y(hidden_in)
    first = build(tables, pages)
    first, mate = lax.optimization_barrier((first, mate))
    pair = jnp.stack([hidden_in, mate])
    blocks = jnp.stack([pair, *[from_x(pair, k) for k in range(1, 4)]])
    blocks = blocks.reshape(8, REQS * STEPS, -1)
    got_first = lax.all_to_all(first, "inst", split_axis=0, concat_axis=0, tiled=True)

    hidden_all = join(tp_index.reshape(1), blocks)
    fresh = jnp.einsum(
        "rd,dcn->rcn", hidden_all, kv_weight, preferred_element_type=jnp.float32
    ).astype(jnp.bfloat16)
    fresh = fresh.reshape(REQS, STEPS, 2, HD)
    values = jnp.pad(fresh[:, :, 1], ((0, 0), (0, 16 - STEPS), (0, 0)))
    keys_values = jnp.pad(
        fresh.transpose(0, 2, 1, 3).reshape(REQS, 2 * STEPS, HD),
        ((0, 0), (0, 16 - 2 * STEPS), (0, 0)),
    )
    stay, second = attend(
        tables, queries.reshape(REQS, ROWS, HD), keys_values, values, kv_pool
    )
    stay_out = stay.reshape(REQS, STEPS, KV_HEADS * HD)
    second = route(got_first, second)
    got_second = lax.all_to_all(second, "inst", split_axis=0, concat_axis=0, tiled=True)

    arriving, load = decode(
        inst_index.reshape(1), long_lengths, short_lengths, mig_order, got_first
    )
    load_share = load[0, :1]
    overflow = load[1, 0] > 0.5

    cache, window = place_first(arriving, got_first)

    def short_path(args):
        lens, window, second, cache = args
        return tuple(settle_all(False, lens, window, second, window, cache))

    def long_path(args):
        lens, window, second, cache = args
        send = build_second(page_table, mig_order, targets, pages)
        got = lax.all_to_all(send, "inst", split_axis=0, concat_axis=0, tiled=True)
        return tuple(settle_all(True, lens, window, second, got, cache))

    moved_cache, moved = lax.cond(
        overflow, long_path, short_path, (arriving, window, got_second, cache)
    )
    moved = lax.optimization_barrier(moved)
    moved_out = moved.reshape(INST * CAP, STEPS, KV_HEADS * HD)
    return (stay_out, moved_out, moved_cache, load_share)


def solution(mesh):
    placed = (
        P("inst", None, "tp"),
        P("inst", None, "tp"),
        P(None, None, "tp"),
        P("inst", None, None, "tp"),
        P("inst", None),
        P("inst", None),
        P("inst", None),
        P("inst", None),
        P("inst", None),
    )
    return jax.shard_map(
        on_device,
        mesh=mesh,
        in_specs=placed,
        out_specs=(
            P("inst", None, "tp"),
            P("inst", None, "tp"),
            P("inst", None, None, "tp"),
            P("inst"),
        ),
        check_vma=False,
    )
```
